32 devices in a mesh: edge: 8 (over z, x), feat: 4 (over y, core).
Axes of the slice: x: 2, y: 2, z: 4, core: 2. Of those that a mesh axis runs over, the one named last changes fastest.
Arguments:
- features: bfloat16 [4096, 2048], P('edge', 'feat'), may hold values from -6 to 6
- tiles: bfloat16 [384, 128, 128], P('edge'), may hold values from -0.109375 to 0.109375
- tile_slot: int32 [768], P('edge'), may hold values from 0 to 31, as said below
- tile_col: int32 [768], P('edge'), may hold values from 0 to 3, as said below
- tile_id: int32 [768], P('edge'), may hold values from 0 to 47
- touched: int32 [8, 8, 4], replicated, may hold values from 0 to 3, as said below
- weight: bfloat16 [2048, 2048], P(None, 'feat'), may hold values from -0.125 to 0.125
- readers: int32 [128], P('edge'), may hold values from 0 to 31, as said below
Outputs:
- hidden: bfloat16 [4096, 2048], P('edge', 'feat')
- ghosts: bfloat16 [16384, 2048], P('edge', 'feat')
The draws below stay inside these ranges and needn't reach their ends.
Inputs may be any that keep to these rules, and one draw needn't show every extreme that they name: For each sender and owner, the 4 entries of touched are distinct block numbers below 4. Within one device's 96 listed products, the pairs (tile_slot, tile_col) are all distinct. Within one device's 96 listed products, the pairs (tile_slot, tile_col) are all distinct. `readers`: one device's 16 entries are distinct, and at most 2 of them lie in the row blocks of any one index of edge; every device's list has some index of edge with exactly 2.
All inputs are finite; a program needn't handle non-finite values.
Results may differ from the reference program's by a relative error of at most 0.0049.
Values may be sent and summed in bfloat16 or wider, within the bound.
No kernel may reach another device: no remote copies, remote signals or barrier semaphores. Data moves between devices by JAX's collectives and lax.ppermute only.
A program may use at most 128 MiB of HBM per device.

```python
import math
import jax
import jax.numpy as jnp
from jax import lax

F = 2048
BLOCK = 128
TABLE = 48
CAP = 4
READ = 16
RCAP = 2
BLK_DEV = 4
TILES = 96
VERTS = 4096
NBLOCKS = 32
N_EDGE = 8


def draw_touched(key, part):
    scores = jax.random.randint(key, (N_EDGE, N_EDGE, BLK_DEV), 0, 1 << 20) * BLK_DEV
    scores = scores + jnp.arange(BLK_DEV, dtype=jnp.int32)
    order = jnp.argsort(scores, axis=-1)
    return order[:, :, :CAP].astype(jnp.int32)


def listed_pairs(key):
    base = jax.random.fold_in(key, 11)
    slot_total = N_EDGE * CAP
    offsets = jax.random.randint(jax.random.fold_in(base, 1), (N_EDGE,), 0, BLK_DEV)
    slot_list = jnp.repeat(jnp.arange(slot_total, dtype=jnp.int32), BLK_DEV - 1)
    stepping = jnp.tile(jnp.arange(BLK_DEV - 1, dtype=jnp.int32), slot_total)
    columns = (slot_list[None, :] + offsets[:, None] + 1 + stepping[None, :]) % BLK_DEV
    slot_rows = jnp.broadcast_to(slot_list[None, :], (N_EDGE, TILES))
    device_keys = jax.random.split(jax.random.fold_in(base, 2), N_EDGE)
    order = jax.vmap(lambda k: jax.random.permutation(k, TILES))(device_keys)
    slot_out = jnp.take_along_axis(slot_rows, order, axis=1)
    column_out = jnp.take_along_axis(columns, order, axis=1)
    return (slot_out.reshape(-1).astype(jnp.int32), column_out.reshape(-1).astype(jnp.int32))


def draw_tile_slot(key, part):
    return listed_pairs(key)[0]


def draw_tile_col(key, part):
    return listed_pairs(key)[1]


def draw_readers(key, part):
    base = jax.random.fold_in(key, 23)
    slot_total = N_EDGE * RCAP

    def one_list(device_key):
        first_key, owner_key, block_key, shuffle_key = jax.random.split(device_key, 4)
        scores = jax.random.randint(first_key, (slot_total,), 0, 1 << 20) * slot_total + jnp.arange(slot_total, dtype=jnp.int32)
        first_owner = jax.random.randint(owner_key, (), 0, N_EDGE)
        owner_of = jnp.arange(slot_total, dtype=jnp.int32) // RCAP
        scores = jnp.where(owner_of == first_owner, jnp.arange(slot_total, dtype=jnp.int32) - slot_total, scores)
        picked = jnp.argsort(scores)[:READ].astype(jnp.int32)
        owners = picked // RCAP
        within = picked % RCAP
        block_scores = jax.random.randint(block_key, (N_EDGE, BLK_DEV), 0, 1 << 20) * BLK_DEV + jnp.arange(BLK_DEV, dtype=jnp.int32)
        block_order = jnp.argsort(block_scores, axis=-1).astype(jnp.int32)
        chosen = owners * BLK_DEV + block_order[owners, within]
        return chosen[jax.random.permutation(shuffle_key, READ)]
    device_keys = jax.random.split(base, N_EDGE)
    return jax.vmap(one_list)(device_keys).reshape(-1).astype(jnp.int32)


def with_ends(result, rng, low, top_value):
    spot = [jax.random.randint(jax.random.fold_in(rng, axis), (), 0, length) for axis, length in enumerate(result.shape)]
    widest = result.shape.index(max(result.shape))
    neighbour = spot[:widest] + [(spot[widest] + 1) % result.shape[widest]] + spot[widest + 1:]
    return result.at[tuple(spot)].set(low).at[tuple(neighbour)].set(top_value)


def shard_levels(stream_key, dims, cuts, low, top_value):
    level, own = 1.0, jax.random.fold_in(stream_key, 6)
    for axis_at, parts in cuts:
        steps = jnp.exp(jax.random.uniform(jax.random.fold_in(own, axis_at), (parts,), jnp.float32, low / len(cuts), top_value / len(cuts)))
        level = level * jnp.repeat(steps, dims[axis_at] // parts).reshape([-1 if axis == axis_at else 1 for axis in range(len(dims))])
    return level


def scatter_about(rng, shape, width, reach, pieces=(), kind=jnp.bfloat16):
    entries = width * jax.random.normal(rng, shape, jnp.float32)
    if pieces:
        entries = entries * shard_levels(rng, shape, pieces, -0.22, 0.18)
    return jnp.clip(entries, -reach, reach).astype(kind)


def setup_inputs(seed: int = 0) -> dict:
    key_list = jax.random.split(jax.random.key(seed), 9)
    return {
        "features": scatter_about(key_list[0], (VERTS, F), 1.0, 6.0, ((0, 8), (1, 4))),
        "tiles": scatter_about(key_list[1], (N_EDGE * TABLE, BLOCK, BLOCK), (BLOCK * TILES // BLK_DEV) ** -0.5, 0.109375, ((0, 8),)),
        "tile_slot": draw_tile_slot(jax.random.fold_in(key_list[8], 71), 0),
        "tile_col": draw_tile_col(jax.random.fold_in(key_list[8], 71), 0),
        "tile_id": with_ends(jax.random.randint(key_list[4], (N_EDGE * TILES,), 0, TABLE), jax.random.fold_in(key_list[4], 1), 0, TABLE - 1).astype(jnp.int32),
        "touched": draw_touched(jax.random.fold_in(key_list[8], 71), 0),
        "weight": scatter_about(key_list[6], (F, F), F ** -0.5, 0.125, ((1, 4),)),
        "readers": draw_readers(jax.random.fold_in(key_list[8], 71), 0),
    }


def reference(features, tiles, tile_slot, tile_col, tile_id, touched, weight, readers):
    per_step = math.gcd(TILES, 64)
    everyone = N_EDGE * TILES
    blocked = features.reshape(NBLOCKS, BLOCK, F)

    def add_group(turn, running):
        first_pos = (turn * per_step).astype(jnp.int32)
        positions = first_pos + jnp.arange(per_step, dtype=jnp.int32)
        device = positions // TILES
        slots = lax.dynamic_slice_in_dim(tile_slot, first_pos, per_step)
        columns = lax.dynamic_slice_in_dim(tile_col, first_pos, per_step)
        chosen = lax.dynamic_slice_in_dim(tile_id, first_pos, per_step)
        owner = slots // CAP
        local_block = touched[device, owner, slots % CAP]
        target = owner * BLK_DEV + local_block
        source = device * BLK_DEV + columns
        adjacency = tiles[device * TABLE + chosen].astype(jnp.float32)
        inputs = blocked[source].astype(jnp.float32)
        product = jnp.einsum("gij,gjc->gic", adjacency, inputs, precision=lax.Precision.HIGHEST)
        return running.at[target].add(product)

    summed = lax.fori_loop(0, everyone // per_step, add_group, jnp.zeros((NBLOCKS, BLOCK, F), jnp.float32))
    aggregated = summed.reshape(VERTS, F).astype(jnp.bfloat16)
    hidden = jnp.maximum(jnp.dot(aggregated, weight, preferred_element_type=jnp.float32), 0.0).astype(jnp.bfloat16)
    ghosts = hidden.reshape(NBLOCKS, BLOCK, F)[readers].reshape(N_EDGE * READ * BLOCK, F)
    return hidden, ghosts
```

```python
import functools

import jax
import jax.numpy as jnp
from jax import lax
from jax.experimental import pallas as pl
from jax.experimental.pallas import tpu as pltpu
from jax.sharding import PartitionSpec as P

PARTS = 2
READ_CAP = 2
VMEM_BYTES = 40 * 1024 * 1024


def partial_sums(table, tiles, inputs, peers, parts):
    block = tiles.shape[1]
    blocks = inputs.shape[0] // block
    width = inputs.shape[1]
    rows = block // parts

    def body(table_ref, tiles_ref, x_ref, *refs):
        outs, lhs = refs[:parts], refs[parts]
        first, step = peers.start, peers.step

        def one_peer(i, carry):
            base = (first + i * step) * blocks * blocks
            for b in range(blocks):
                for col in range(blocks):
                    entry = table_ref[base + b * blocks + col]
                    tile = tiles_ref[jnp.maximum(entry - 1, 0)]
                    tile = jnp.where(entry > 0, tile, jnp.zeros_like(tile))
                    for c in range(parts):
                        lhs[
                            pl.ds((c * blocks + b) * rows, rows), pl.ds(col * block, block)
                        ] = tile[c * rows : (c + 1) * rows]
            total = jnp.dot(lhs[...], x_ref[...], preferred_element_type=jnp.float32)
            total = total.astype(jnp.bfloat16).reshape(parts, blocks, rows, width)
            for c in range(parts):
                outs[c][i] = total[c]
            return carry

        lax.fori_loop(0, len(peers), one_peer, 0)

    part = jax.ShapeDtypeStruct((len(peers), blocks, rows, width), jnp.bfloat16)
    vmem = pl.BlockSpec(memory_space=pltpu.VMEM)
    return pl.pallas_call(
        body,
        out_shape=[part] * parts,
        in_specs=[pl.BlockSpec(memory_space=pltpu.SMEM), vmem, vmem],
        out_specs=[vmem] * parts,
        scratch_shapes=[pltpu.VMEM((blocks * block, blocks * block), jnp.bfloat16)],
        compiler_params=pltpu.CompilerParams(vmem_limit_bytes=VMEM_BYTES),
        cost_estimate=pl.CostEstimate(
            flops=2 * len(peers) * (blocks * block) ** 2 * width,
            bytes_accessed=2 * (tiles.size + inputs.size + len(peers) * blocks * block * width),
            transcendentals=0,
        ),
    )(table, tiles, inputs)


def mix(gathered, weight):
    pieces, blocks, rows, depth = gathered.shape
    width = weight.shape[1]

    def body(g_ref, w_ref, out_ref):
        total = jnp.zeros((blocks * rows, width), jnp.float32)
        for f in range(pieces):
            total += jnp.dot(
                g_ref[f].reshape(blocks * rows, depth),
                w_ref[f * depth : (f + 1) * depth],
                preferred_element_type=jnp.float32,
            )
        out_ref[...] = jnp.maximum(total, 0.0).astype(jnp.bfloat16).reshape(out_ref.shape)

    vmem = pl.BlockSpec(memory_space=pltpu.VMEM)
    return pl.pallas_call(
        body,
        out_shape=jax.ShapeDtypeStruct((blocks, rows, width), jnp.bfloat16),
        in_specs=[vmem, vmem],
        out_specs=vmem,
        compiler_params=pltpu.CompilerParams(vmem_limit_bytes=VMEM_BYTES),
        cost_estimate=pl.CostEstimate(
            flops=2 * gathered.size * width,
            bytes_accessed=2 * (gathered.size + weight.size + blocks * rows * width),
            transcendentals=0,
        ),
    )(gathered, weight)


def pick(choice, source):
    count = choice.shape[0]

    def body(choice_ref, src_ref, out_ref, sems):
        copies = [
            pltpu.make_async_copy(src_ref.at[choice_ref[i]], out_ref.at[i], sems.at[i]) for i in range(count)
        ]
        for copy in copies:
            copy.start()
        for copy in copies:
            copy.wait()

    return pl.pallas_call(
        body,
        out_shape=jax.ShapeDtypeStruct((count, *source.shape[1:]), source.dtype),
        in_specs=[pl.BlockSpec(memory_space=pltpu.SMEM), pl.BlockSpec(memory_space=pl.ANY)],
        out_specs=pl.BlockSpec(memory_space=pl.ANY),
        scratch_shapes=[pltpu.SemaphoreType.DMA((count,))],
        cost_estimate=pl.CostEstimate(
            flops=0, bytes_accessed=4 * count * source[0].size, transcendentals=0
        ),
    )(choice, source)


def lay_out(place, near, far, block):
    count, parts = place.shape[0], len(near)
    near_count = near[0].shape[0]
    rows, width = near[0].shape[1:]

    def body(place_ref, *refs):
        near_refs, far_refs = refs[:parts], refs[parts : 2 * parts]
        out_ref, sems = refs[2 * parts :]
        for c in range(parts):
            for r in range(count):
                target = out_ref.at[r, pl.ds(c * rows, rows)]
                spot = place_ref[r]

                @pl.when(spot < near_count)
                def _():
                    pltpu.make_async_copy(near_refs[c].at[spot], target, sems.at[c, r]).start()

                @pl.when(spot >= near_count)
                def _():
                    pltpu.make_async_copy(far_refs[c].at[spot - near_count], target, sems.at[c, r]).start()

        for c in range(parts):
            for r in range(count):
                target = out_ref.at[r, pl.ds(c * rows, rows)]
                pltpu.make_async_copy(near_refs[c].at[0], target, sems.at[c, r]).wait()

    hbm = pl.BlockSpec(memory_space=pl.ANY)
    return pl.pallas_call(
        body,
        out_shape=jax.ShapeDtypeStruct((count, block, width), jnp.bfloat16),
        in_specs=[pl.BlockSpec(memory_space=pltpu.SMEM)] + [hbm] * (2 * parts),
        out_specs=hbm,
        scratch_shapes=[pltpu.SemaphoreType.DMA((parts, count))],
        cost_estimate=pl.CostEstimate(
            flops=0, bytes_accessed=4 * count * block * width, transcendentals=0
        ),
    )(place, *near, *far)


def local(features, tiles, tile_slot, tile_col, tile_id, touched, weight, readers):
    edges = lax.axis_size("edge")
    half = edges // 2
    me = lax.axis_index("edge")
    block = tiles.shape[1]
    blocks = features.shape[0] // block
    width = features.shape[1]
    cap = touched.shape[2]
    parts = PARTS

    mine = lax.dynamic_index_in_dim(touched, me, 0, keepdims=False).reshape(-1)
    slots = jnp.arange(edges * cap, dtype=jnp.int32)
    target = jnp.sum(jnp.where(tile_slot[:, None] == slots[None, :], mine[None, :], 0), axis=1)
    peer = lax.bitwise_xor(tile_slot // cap, me)
    spot = (peer * blocks + target) * blocks + tile_col
    spots = jnp.arange(edges * blocks * blocks, dtype=jnp.int32)
    table = jnp.sum(jnp.where(spot[:, None] == spots[None, :], tile_id[:, None] + 1, 0), axis=0)

    def flip(value, bits):
        return lax.ppermute(value, "edge", [(e, e ^ bits) for e in range(edges)])

    side = me % 2
    other = flip(readers, 1)
    order = jnp.arange(readers.shape[0], dtype=jnp.int32)

    def ranks(listed):
        same = (listed[:, None] // blocks) == (listed[None, :] // blocks)
        return jnp.sum((same & (order[None, :] < order[:, None])).astype(jnp.int32), axis=1)

    owner_at = jnp.arange(half * READ_CAP, dtype=jnp.int32) // READ_CAP
    rank_at = jnp.arange(half * READ_CAP, dtype=jnp.int32) % READ_CAP
    hit = ((other // blocks)[None, :] == (2 * owner_at + side)[:, None]) & (ranks(other)[None, :] == rank_at[:, None])
    choice = owner_at * blocks + jnp.sum(jnp.where(hit, (other % blocks)[None, :], 0), axis=1)
    owner = readers // blocks
    place = jnp.where(
        owner % 2 == side,
        (owner // 2) * blocks + readers % blocks,
        half * blocks + (owner // 2) * READ_CAP + ranks(readers),
    )

    away = partial_sums(table, tiles, features, range(1, edges, 2), parts)
    kept = partial_sums(table, tiles, features, range(0, edges, 2), parts)
    sides = [[e for e in range(edges) if e % 2 == s] for s in range(2)]
    hidden, near, far = [], [], []
    for c in range(parts):
        got = flip(away[c], 1)
        total = kept[c][0].astype(jnp.float32) + got[0].astype(jnp.float32)
        for i in range(1, half):
            pair = (kept[c][i].astype(jnp.float32) + got[i].astype(jnp.float32)).astype(jnp.bfloat16)
            total = total + flip(pair, 2 * i).astype(jnp.float32)
        gathered = lax.all_gather(total.astype(jnp.bfloat16), "feat", axis=0)
        mixed = mix(gathered, weight)
        hidden.append(mixed)
        column = lax.all_gather(mixed, "edge", axis=0, axis_index_groups=sides)
        column = column.reshape(half * blocks, block // parts, width)
        near.append(column)
        far.append(flip(pick(choice, column), 1))
    ghosts = lay_out(place, near, far, block)
    return (
        jnp.concatenate(hidden, axis=1).reshape(blocks * block, width),
        ghosts.reshape(-1, width),
    )


def solution(mesh):
    in_specs = (
        P("edge", "feat"),
        P("edge", None, None),
        P("edge"),
        P("edge"),
        P("edge"),
        P(),
        P(None, "feat"),
        P("edge"),
    )
    out_specs = (P("edge", "feat"), P("edge", "feat"))
    return jax.shard_map(local, mesh=mesh, in_specs=in_specs, out_specs=out_specs, check_vma=False)
```

```python
import jax
import jax.numpy as jnp
from jax import lax
from jax.experimental import pallas as pl
from jax.experimental.pallas import tpu as pltpu
from jax.sharding import PartitionSpec as P

PARTS = 4
READ_CAP = 2
VMEM_BYTES = 40 * 1024 * 1024

SMEM = pl.BlockSpec(memory_space=pltpu.SMEM)
VMEM = pl.BlockSpec(memory_space=pltpu.VMEM)
ANY = pl.BlockSpec(memory_space=pl.ANY)


def reversed_bits(value, bits):
    result = value & 1
    for i in range(1, bits):
        result = (result << 1) | ((value >> i) & 1)
    return result


def partial_sums(me, slot, col, tile_id, touched, tiles, features, first, count, parts):
    block = tiles.shape[1]
    blocks = features.shape[0] // block
    width = features.shape[1]
    rows = block // parts
    products = slot.shape[0]
    edges, cap = touched.shape[1], touched.shape[2]
    bits = edges.bit_length() - 1
    square = blocks * blocks

    def body(me_ref, slot_ref, col_ref, id_ref, touched_ref, tiles_hbm, x_hbm, *refs):
        outs = refs[:parts]
        table, tiles_ref, x_ref, lhs, sems = refs[parts:]
        load_tiles = pltpu.make_async_copy(tiles_hbm, tiles_ref, sems.at[0])
        load_x = pltpu.make_async_copy(x_hbm, x_ref, sems.at[1])
        load_tiles.start()
        load_x.start()

        def clear(i, carry):
            table[i] = 0
            return carry

        lax.fori_loop(0, edges * square, clear, 0, unroll=8)

        def enter(k, carry):
            owner, entry = slot_ref[k] // cap, slot_ref[k] % cap
            target = touched_ref[owner * cap + entry]
            place = reversed_bits(owner ^ me_ref[0], bits)
            table[(place * blocks + target) * blocks + col_ref[k]] = id_ref[k] + 1
            return carry

        lax.fori_loop(0, products, enter, 0, unroll=4)
        load_tiles.wait()
        load_x.wait()

        def one_owner(i, carry):
            base = (first + i) * square
            for b in range(blocks):
                for c in range(blocks):
                    entry = table[base + b * blocks + c]
                    tile = tiles_ref[jnp.maximum(entry - 1, 0)]
                    tile = jnp.where(entry > 0, tile, jnp.zeros_like(tile))
                    for part in range(parts):
                        lhs[pl.ds((part * blocks + b) * rows, rows), pl.ds(c * block, block)] = tile[
                            part * rows : (part + 1) * rows
                        ]
            total = jnp.dot(lhs[...], x_ref[...], preferred_element_type=jnp.float32)
            total = total.astype(jnp.bfloat16).reshape(parts, blocks, rows, width)
            for part in range(parts):
                outs[part][i] = total[part]
            return carry

        lax.fori_loop(0, count, one_owner, 0)

    return pl.pallas_call(
        body,
        out_shape=[jax.ShapeDtypeStruct((count, blocks, rows, width), jnp.bfloat16)] * parts,
        in_specs=[SMEM] * 5 + [ANY] * 2,
        out_specs=[VMEM] * parts,
        scratch_shapes=[
            pltpu.SMEM((edges * square,), jnp.int32),
            pltpu.VMEM(tiles.shape, jnp.bfloat16),
            pltpu.VMEM(features.shape, jnp.bfloat16),
            pltpu.VMEM((blocks * block, blocks * block), jnp.bfloat16),
            pltpu.SemaphoreType.DMA((2,)),
        ],
        compiler_params=pltpu.CompilerParams(vmem_limit_bytes=VMEM_BYTES),
        cost_estimate=pl.CostEstimate(
            flops=2 * count * (blocks * block) ** 2 * width,
            bytes_accessed=2 * (tiles.size + features.size + count * blocks * block * width),
            transcendentals=0,
        ),
    )(me, slot, col, tile_id, touched[me[0]].reshape(-1), tiles, features)


def mix(mine, pieces, weight):
    blocks, rows, depth = pieces[0].shape
    width = weight.shape[1]

    def body(mine_ref, w_ref, *refs):
        out_ref = refs[-1]
        total = jnp.zeros((blocks * rows, width), jnp.float32)
        for j, piece in enumerate(refs[:-1]):
            at = pl.multiple_of((mine_ref[0] ^ j) * depth, depth)
            total += jnp.dot(
                piece[...].reshape(blocks * rows, depth),
                w_ref[pl.ds(at, depth)],
                preferred_element_type=jnp.float32,
            )
        out_ref[...] = jnp.maximum(total, 0.0).astype(jnp.bfloat16).reshape(out_ref.shape)

    return pl.pallas_call(
        body,
        out_shape=jax.ShapeDtypeStruct((blocks, rows, width), jnp.bfloat16),
        in_specs=[SMEM] + [VMEM] * (1 + len(pieces)),
        out_specs=VMEM,
        compiler_params=pltpu.CompilerParams(vmem_limit_bytes=VMEM_BYTES),
        cost_estimate=pl.CostEstimate(
            flops=2 * len(pieces) * pieces[0].size * width,
            bytes_accessed=2 * (len(pieces) * pieces[0].size + weight.size + blocks * rows * width),
            transcendentals=0,
        ),
    )(mine, weight, *pieces)


def pick(choice, near):
    count = choice.shape[0]

    def body(choice_ref, *refs):
        for i in range(count):
            refs[-1][i] = refs[i // READ_CAP][choice_ref[i]]

    return pl.pallas_call(
        body,
        out_shape=jax.ShapeDtypeStruct((count, *near[0].shape[1:]), near[0].dtype),
        in_specs=[SMEM] + [VMEM] * len(near),
        out_specs=VMEM,
        compiler_params=pltpu.CompilerParams(vmem_limit_bytes=VMEM_BYTES),
        cost_estimate=pl.CostEstimate(flops=0, bytes_accessed=4 * count * near[0][0].size, transcendentals=0),
    )(choice, *near)


def lay_out(place, near, far, ghosts, part, block):
    count = place.shape[0]
    blocks, rows, width = near[0].shape
    near_count = len(near) * blocks

    def body(place_ref, *refs):
        sources, far_ref = refs[: len(near)], refs[len(near)]
        out_ref, sems = refs[-2:]

        def target(r):
            return out_ref.at[r, pl.ds(part * rows, rows)]

        for r in range(count):
            spot = place_ref[r]
            for i, source in enumerate(sources):

                @pl.when(spot // blocks == i)
                def _():
                    pltpu.make_async_copy(source.at[spot % blocks], target(r), sems.at[r]).start()

            @pl.when(spot >= near_count)
            def _():
                pltpu.make_async_copy(far_ref.at[spot - near_count], target(r), sems.at[r]).start()

        for r in range(count):
            pltpu.make_async_copy(far_ref.at[0], target(r), sems.at[r]).wait()

    earlier = [] if ghosts is None else [ghosts]
    return pl.pallas_call(
        body,
        out_shape=jax.ShapeDtypeStruct((count, block, width), jnp.bfloat16),
        in_specs=[SMEM] + [VMEM] * (len(near) + 1) + [ANY] * len(earlier),
        out_specs=ANY,
        scratch_shapes=[pltpu.SemaphoreType.DMA((count,))],
        input_output_aliases={len(near) + 2: 0} if earlier else {},
        compiler_params=pltpu.CompilerParams(vmem_limit_bytes=VMEM_BYTES),
        cost_estimate=pl.CostEstimate(flops=0, bytes_accessed=4 * count * rows * width, transcendentals=0),
    )(place, *near, far, *earlier)


def local(features, tiles, tile_slot, tile_col, tile_id, touched, weight, readers):
    edges, feats = lax.axis_size("edge"), lax.axis_size("feat")
    half = edges // 2
    me, mine = lax.axis_index("edge"), lax.axis_index("feat")
    block = tiles.shape[1]
    blocks = features.shape[0] // block
    width = features.shape[1]
    parts = PARTS

    def flip(value, bit, axis="edge"):
        return lax.ppermute(value, axis, [(d, d ^ bit) for d in range(lax.axis_size(axis))])

    def spread(value, size, lowest, axis):
        held = {0: value}
        bit = size // 2
        while bit >= lowest:
            held.update({j | bit: flip(held[j], bit, axis) for j in list(held)})
            bit //= 2
        return [held[j] for j in sorted(held)]

    order = jnp.arange(readers.shape[0], dtype=jnp.int32)

    def ranks(listed):
        same = (listed[:, None] // blocks) == (listed[None, :] // blocks)
        return jnp.sum((same & (order[None, :] < order[:, None])).astype(jnp.int32), axis=1)

    other = flip(readers, 1)
    entries = jnp.arange(half * READ_CAP, dtype=jnp.int32)
    wanted = lax.bitwise_xor(2 * (entries // READ_CAP), me)
    hit = ((other // blocks)[None, :] == wanted[:, None]) & (ranks(other)[None, :] == (entries % READ_CAP)[:, None])
    choice = jnp.sum(jnp.where(hit, (other % blocks)[None, :], 0), axis=1)
    peer = lax.bitwise_xor(readers // blocks, me)
    place = jnp.where(
        peer % 2 == 0,
        (peer // 2) * blocks + readers % blocks,
        half * blocks + (peer // 2) * READ_CAP + ranks(readers),
    )

    products = (me.reshape(1), tile_slot, tile_col, tile_id, touched, tiles, features)
    away = partial_sums(*products, half, half, parts)
    kept = partial_sums(*products, 0, half, parts)
    hidden, ghosts = [], None
    for part in range(parts):
        total = kept[part].astype(jnp.float32) + flip(away[part], 1).astype(jnp.float32)
        bit = 2
        while bit < edges:
            left = total.shape[0] // 2
            total = total[:left] + flip(total[left:].astype(jnp.bfloat16), bit).astype(jnp.float32)
            bit *= 2
        pieces = spread(total[0].astype(jnp.bfloat16), feats, 1, "feat")
        mixed = mix(mine.reshape(1), pieces, weight)
        hidden.append(mixed)
        near = spread(mixed, edges, 2, "edge")
        far = flip(pick(choice, near), 1)
        ghosts = lay_out(place, near, far, ghosts, part, block)
    return (
        jnp.concatenate(hidden, axis=1).reshape(blocks * block, width),
        ghosts.reshape(-1, width),
    )


def solution(mesh):
    in_specs = (
        P("edge", "feat"),
        P("edge", None, None),
        P("edge"),
        P("edge"),
        P("edge"),
        P(),
        P(None, "feat"),
        P("edge"),
    )
    out_specs = (P("edge", "feat"), P("edge", "feat"))
    return jax.shard_map(local, mesh=mesh, in_specs=in_specs, out_specs=out_specs, check_vma=False)
```

```python
import jax
import jax.numpy as jnp
from jax import lax
from jax.experimental import pallas as pl
from jax.experimental.pallas import tpu as pltpu
from jax.sharding import PartitionSpec as P

SHARES = (1, 2, 2, 2, 1)
READ_CAP = 2
VMEM_BYTES = 40 * 1024 * 1024
UNIT_TIME, STEP_TIME, LATENCY = 10.5, 0.7, 1.5

SMEM = pl.BlockSpec(memory_space=pltpu.SMEM)
VMEM = pl.BlockSpec(memory_space=pltpu.VMEM)
ANY = pl.BlockSpec(memory_space=pl.ANY)
TOKEN = jax.ShapeDtypeStruct((8, 128), jnp.float32)


def call(body, out_shape, in_specs, out_specs, operands, scratch=(), aliases=None, flops=0):
    moved = sum(a.size * a.dtype.itemsize for a in [*operands, *out_shape])
    return pl.pallas_call(
        body,
        out_shape=out_shape,
        in_specs=in_specs,
        out_specs=out_specs,
        scratch_shapes=list(scratch),
        input_output_aliases=aliases or {},
        compiler_params=pltpu.CompilerParams(vmem_limit_bytes=VMEM_BYTES),
        cost_estimate=pl.CostEstimate(flops=flops, bytes_accessed=moved, transcendentals=0),
    )(*operands)


def split(value, size):
    if size & (size - 1) == 0:
        return value >> (size.bit_length() - 1), value & (size - 1)
    return lax.div(value, size), lax.rem(value, size)


def reversed_bits(value, bits):
    result = value & 1
    for i in range(1, bits):
        result = (result << 1) | ((value >> i) & 1)
    return result


def multiply_owner(table, base, tiles, inputs, lhs, outs, index, spans, row_base, blocks, block):
    for b in range(blocks):
        for c in range(blocks):
            entry = table[base + b * blocks + c]
            tile = tiles[jnp.maximum(entry - 1, 0)]
            tile = jnp.where(entry > 0, tile, jnp.zeros_like(tile))
            at = 0
            for first, rows in spans:
                lhs[pl.ds(at + b * rows, rows), pl.ds(c * block, block)] = tile[first - row_base : first - row_base + rows]
                at += blocks * rows
    total = jnp.dot(lhs[...], inputs[...], preferred_element_type=jnp.float32).astype(jnp.bfloat16)
    at = 0
    for out, (first, rows) in zip(outs, spans):
        out[index] = total[at : at + blocks * rows].reshape(blocks, rows, total.shape[1])
        at += blocks * rows


def first_part(me, slot, col, tile_id, touched, tiles, features, first, count, span):
    block = tiles.shape[1]
    blocks = features.shape[0] // block
    width = features.shape[1]
    edges, cap = touched.shape[1], touched.shape[2]
    bits = edges.bit_length() - 1
    products = slot.shape[0]
    start, rows = span
    square = blocks * blocks

    def body(me_ref, slot_ref, col_ref, id_ref, touched_ref, tiles_hbm, x_hbm, table, out, x_out, tiles_ref, lhs, bases, sems):
        load_tiles = pltpu.make_async_copy(tiles_hbm.at[:, pl.ds(start, rows)], tiles_ref, sems.at[0])
        load_x = pltpu.make_async_copy(x_hbm, x_out, sems.at[1])
        load_tiles.start()
        load_x.start()

        def clear(i, carry):
            table[i] = 0
            return carry

        lax.fori_loop(0, edges * square, clear, 0, unroll=16)

        def place_slot(k, carry):
            owner, entry = split(k, cap)
            place = reversed_bits(owner ^ me_ref[0], bits)
            bases[k] = (place * blocks + touched_ref[k]) * blocks
            return carry

        lax.fori_loop(0, edges * cap, place_slot, 0, unroll=8)

        def enter(k, carry):
            table[bases[slot_ref[k]] + col_ref[k]] = id_ref[k] + 1
            return carry

        lax.fori_loop(0, products, enter, 0, unroll=8)
        load_tiles.wait()
        load_x.wait()

        def one_owner(i, carry):
            multiply_owner(
                table, (first + i) * square, tiles_ref, x_out, lhs, [out], i, [span], start, blocks, block
            )
            return carry

        lax.fori_loop(0, count, one_owner, 0)

    return call(
        body,
        [
            jax.ShapeDtypeStruct((edges * square,), jnp.int32),
            jax.ShapeDtypeStruct((count, blocks, rows, width), jnp.bfloat16),
            jax.ShapeDtypeStruct(features.shape, jnp.bfloat16),
        ],
        [SMEM] * 5 + [ANY] * 2,
        [SMEM, VMEM, VMEM],
        (me, slot, col, tile_id, touched[me[0]].reshape(-1), tiles, features),
        [
            pltpu.VMEM((tiles.shape[0], rows, block), jnp.bfloat16),
            pltpu.VMEM((blocks * rows, blocks * block), jnp.bfloat16),
            pltpu.SMEM((edges * cap,), jnp.int32),
            pltpu.SemaphoreType.DMA((2,)),
        ],
        flops=2 * count * blocks * rows * blocks * block * width,
    )


def other_parts(table, tiles, inputs, first, count, spans):
    block = tiles.shape[1]
    blocks = inputs.shape[0] // block
    width = inputs.shape[1]
    total_rows = sum(rows for _, rows in spans)

    def body(table_ref, tiles_hbm, x_ref, *refs):
        outs = refs[: len(spans)]
        tiles_ref, lhs, sem = refs[len(spans) :]
        load = pltpu.make_async_copy(tiles_hbm, tiles_ref, sem.at[0])
        load.start()
        load.wait()

        def one_owner(i, carry):
            base = (first + i) * blocks * blocks
            multiply_owner(table_ref, base, tiles_ref, x_ref, lhs, outs, i, spans, 0, blocks, block)
            return carry

        lax.fori_loop(0, count, one_owner, 0)

    return call(
        body,
        [jax.ShapeDtypeStruct((count, blocks, rows, width), jnp.bfloat16) for _, rows in spans],
        [SMEM, ANY, VMEM],
        [VMEM] * len(spans),
        (table, tiles, inputs),
        [
            pltpu.VMEM(tiles.shape, jnp.bfloat16),
            pltpu.VMEM((blocks * total_rows, blocks * block), jnp.bfloat16),
            pltpu.SemaphoreType.DMA((1,)),
        ],
        flops=2 * count * blocks * total_rows * blocks * block * width,
    )


def combine(token, total, got):
    count = total.shape[0]
    left = count // 2

    def body(token_ref, total_ref, got_ref, *outs):
        value = total_ref[...].astype(jnp.float32) + got_ref[...].astype(jnp.float32)
        if left:
            outs[0][...] = value[:left]
            outs[1][...] = value[left:].astype(jnp.bfloat16)
        else:
            outs[0][...] = value[0].astype(jnp.bfloat16)
        outs[-1][...] = token_ref[...]

    shape = total.shape[1:]
    if left:
        out_shape = [
            jax.ShapeDtypeStruct((left, *shape), jnp.float32),
            jax.ShapeDtypeStruct((count - left, *shape), jnp.bfloat16),
        ]
    else:
        out_shape = [jax.ShapeDtypeStruct(shape, jnp.bfloat16)]
    out_shape.append(TOKEN)
    return call(body, out_shape, [VMEM] * 3, [VMEM] * len(out_shape), (token, total, got))


def relay(token, values):
    def body(token_ref, *refs):
        for source, target in zip(refs[: len(values)], refs[len(values) :]):
            target[...] = source[...]
        refs[-1][...] = token_ref[...]

    out_shape = [jax.ShapeDtypeStruct(v.shape, v.dtype) for v in values] + [TOKEN]
    *copies, token = call(body, out_shape, [VMEM] * (1 + len(values)), [VMEM] * len(out_shape), (token, *values))
    return copies, token


def mix(token, mine, pieces, weight):
    blocks, rows, depth = pieces[0].shape
    width = weight.shape[1]

    def body(token_ref, mine_ref, w_ref, *refs):
        out_ref, token_out = refs[-2:]
        total = jnp.zeros((blocks * rows, width), jnp.float32)
        for j, piece in enumerate(refs[:-2]):
            at = pl.multiple_of((mine_ref[0] ^ j) * depth, depth)
            total += jnp.dot(
                piece[...].reshape(blocks * rows, depth),
                w_ref[pl.ds(at, depth)],
                preferred_element_type=jnp.float32,
            )
        out_ref[...] = jnp.maximum(total, 0.0).astype(jnp.bfloat16).reshape(out_ref.shape)
        token_out[...] = token_ref[...]

    return call(
        body,
        [jax.ShapeDtypeStruct((blocks, rows, width), jnp.bfloat16), TOKEN],
        [VMEM, SMEM] + [VMEM] * (1 + len(pieces)),
        [VMEM] * 2,
        (token, mine, weight, *pieces),
        flops=2 * len(pieces) * pieces[0].size * width,
    )


def pick(token, choice, near):
    count = choice.shape[0]

    def body(token_ref, choice_ref, *refs):
        for i in range(count):
            refs[-2][i] = refs[i // READ_CAP][choice_ref[i]]
        refs[-1][...] = token_ref[...]

    return call(
        body,
        [jax.ShapeDtypeStruct((count, *near[0].shape[1:]), near[0].dtype), TOKEN],
        [VMEM, SMEM] + [VMEM] * len(near),
        [VMEM] * 2,
        (token, choice, *near),
    )


def lay_out(token, place, near, far, outputs, span, block):
    count = place.shape[0]
    blocks, _, width = near[0].shape
    start, rows = span
    near_count = len(near) * blocks

    def body(token_ref, place_ref, *refs):
        sources, far_ref = refs[: len(near)], refs[len(near)]
        hidden_ref, ghost_ref, token_out, sems = refs[-4:]

        def target(r):
            return ghost_ref.at[r, pl.ds(start, rows)]

        own = pltpu.make_async_copy(sources[0], hidden_ref.at[:, pl.ds(start, rows)], sems.at[count])
        own.start()
        for r in range(count):
            spot = place_ref[r]
            which, within = split(spot, blocks)
            for i, source in enumerate(sources):

                @pl.when(which == i)
                def _():
                    pltpu.make_async_copy(source.at[within], target(r), sems.at[r]).start()

            @pl.when(spot >= near_count)
            def _():
                pltpu.make_async_copy(far_ref.at[spot - near_count], target(r), sems.at[r]).start()

        token_out[...] = token_ref[...]
        own.wait()
        for r in range(count):
            pltpu.make_async_copy(far_ref.at[0], target(r), sems.at[r]).wait()

    operands = (token, place, *near, far, *outputs)
    return call(
        body,
        [
            jax.ShapeDtypeStruct((blocks, block, width), jnp.bfloat16),
            jax.ShapeDtypeStruct((count, block, width), jnp.bfloat16),
            TOKEN,
        ],
        [VMEM, SMEM] + [VMEM] * (len(near) + 1) + [ANY] * len(outputs),
        [ANY, ANY, VMEM],
        operands,
        [pltpu.SemaphoreType.DMA((count + 1,))],
        aliases={len(operands) - 2: 0, len(operands) - 1: 1} if outputs else None,
    )


def local(features, tiles, tile_slot, tile_col, tile_id, touched, weight, readers):
    edges, feats = lax.axis_size("edge"), lax.axis_size("feat")
    half = edges // 2
    me, mine = lax.axis_index("edge"), lax.axis_index("feat")
    block = tiles.shape[1]
    blocks = features.shape[0] // block
    width = features.shape[1]

    def flip(value, bit, axis="edge"):
        return lax.ppermute(value, axis, [(d, d ^ bit) for d in range(lax.axis_size(axis))])

    order = jnp.arange(readers.shape[0], dtype=jnp.int32)

    def ranks(listed):
        same = (listed[:, None] // blocks) == (listed[None, :] // blocks)
        return jnp.sum((same & (order[None, :] < order[:, None])).astype(jnp.int32), axis=1)

    other = flip(readers, 1)
    entries = jnp.arange(half * READ_CAP, dtype=jnp.int32)
    wanted = lax.bitwise_xor(2 * (entries // READ_CAP), me)
    hit = ((other // blocks)[None, :] == wanted[:, None]) & (ranks(other)[None, :] == (entries % READ_CAP)[:, None])
    choice = jnp.sum(jnp.where(hit, (other % blocks)[None, :], 0), axis=1)
    peer = lax.bitwise_xor(readers // blocks, me)
    place = jnp.where(
        peer % 2 == 0,
        (peer // 2) * blocks + readers % blocks,
        half * blocks + (peer // 2) * READ_CAP + ranks(readers),
    )

    unit = block // sum(SHARES)
    spans = [(sum(SHARES[:i]) * unit, share * unit) for i, share in enumerate(SHARES)]
    table, early, inputs = first_part(
        me.reshape(1), tile_slot, tile_col, tile_id, touched, tiles, features, half, half, spans[0]
    )
    away = [early, *other_parts(table, tiles, inputs, half, half, spans[1:])]
    kept = other_parts(table, tiles, inputs, 0, half, spans)

    state = {"token": jnp.zeros(TOKEN.shape, TOKEN.dtype), "outputs": ()}

    def chained(function, *operands):
        *results, state["token"] = function(state["token"], *operands)
        return results

    def spread(value, size, lowest, axis, link, share):
        bits = [1 << i for i in reversed(range(size.bit_length() - 1)) if 1 << i >= lowest]
        held, sources = {0: value}, {0: value}
        while sources:
            fresh = {}
            for j, source in sources.items():
                for bit in bits:
                    if j == 0 or bit < (j & -j):
                        fresh[j | bit] = flip(source, bit, axis)
            held.update(fresh)
            yield link, share * len(fresh)
            onward = [j for j in fresh if any(bit < (j & -j) for bit in bits)]
            if not onward:
                break
            copies, state["token"] = relay(state["token"], [fresh[j] for j in onward])
            sources = dict(zip(onward, copies))
        return [held[j] for j in sorted(held)]

    def one_part(part):
        share = spans[part][1] / block
        got = flip(away[part], 1)
        yield "low", share * half
        total, sent = chained(combine, kept[part], got)
        bit = 2
        while bit < edges:
            got = flip(sent, bit)
            yield "high", share * 2
            total, *sent = chained(combine, total, got)
            sent = sent[0] if sent else None
            bit *= 2
        pieces = yield from spread(total, feats, 1, "feat", "feat", share / 2)
        (mixed,) = chained(mix, mine.reshape(1), pieces, weight)
        near = yield from spread(mixed, edges, 2, "edge", "high", share)
        (picked,) = chained(pick, choice, near)
        far = flip(picked, 1)
        yield "low", share * 2
        state["outputs"] = chained(lay_out, place, near, far, state["outputs"], spans[part], block)

    now, free, waiting = 0.0, {"low": 0.0, "high": 0.0, "feat": 0.0}, []

    def advance(part, steps):
        nonlocal now
        link, units = next(steps, (None, 0))
        if link is not None:
            now += STEP_TIME
            free[link] = max(free[link], now) + units * UNIT_TIME
            waiting.append((free[link] + LATENCY, part, steps))

    for part in range(len(spans)):
        advance(part, one_part(part))
    while waiting:
        ready, part, steps = min(waiting, key=lambda item: item[:2])
        waiting = [item for item in waiting if item[1] != part]
        now = max(now, ready)
        advance(part, steps)
    hidden, ghosts = state["outputs"]
    return hidden.reshape(blocks * block, width), ghosts.reshape(-1, width)


def solution(mesh):
    in_specs = (
        P("edge", "feat"),
        P("edge", None, None),
        P("edge"),
        P("edge"),
        P("edge"),
        P(),
        P(None, "feat"),
        P("edge"),
    )
    out_specs = (P("edge", "feat"), P("edge", "feat"))
    return jax.shard_map(local, mesh=mesh, in_specs=in_specs, out_specs=out_specs, check_vma=False)
```

```python
import jax
import jax.numpy as jnp
from jax import lax
from jax.experimental import pallas as pl
from jax.experimental.pallas import tpu as pltpu
from jax.sharding import PartitionSpec as P

SHARES = (2, 2, 2, 1, 1)
READ_CAP = 2
VMEM_BYTES = 12 * 1024 * 1024

SMEM = pl.BlockSpec(memory_space=pltpu.SMEM)
VMEM = pl.BlockSpec(memory_space=pltpu.VMEM)
HBM = pl.BlockSpec(memory_space=pltpu.HBM)


def call(body, out_shape, in_specs, out_specs, operands, scratch=(), aliases=None, limit=VMEM_BYTES):
    return pl.pallas_call(
        body,
        out_shape=out_shape,
        in_specs=in_specs,
        out_specs=out_specs,
        scratch_shapes=list(scratch),
        input_output_aliases=aliases or {},
        compiler_params=pltpu.CompilerParams(vmem_limit_bytes=limit),
        cost_estimate=pl.CostEstimate(flops=0, bytes_accessed=1, transcendentals=0),
    )(*operands)


class Task:
    def __init__(self, body, operands, out_shape, specs=None):
        self.body, self.operands, self.out_shape = body, operands, out_shape
        self.specs = specs or [VMEM] * len(operands)


def joint(tasks):
    def body(*refs):
        ins = refs[: sum(len(t.operands) for t in tasks)]
        outs = refs[len(ins) :]
        for t in tasks:
            t.body(ins[: len(t.operands)], outs[: len(t.out_shape)])
            ins, outs = ins[len(t.operands) :], outs[len(t.out_shape) :]

    out_shape = [s for t in tasks for s in t.out_shape]
    results = call(
        body,
        out_shape,
        [s for t in tasks for s in t.specs],
        [VMEM] * len(out_shape),
        [a for t in tasks for a in t.operands],
    )
    grouped = []
    for t in tasks:
        grouped.append(results[: len(t.out_shape)])
        results = results[len(t.out_shape) :]
    return grouped


def split(value, size):
    if size & (size - 1) == 0:
        return value >> (size.bit_length() - 1), value & (size - 1)
    return lax.div(value, size), lax.rem(value, size)


def reversed_bits(value, bits):
    result = value & 1
    for i in range(1, bits):
        result = (result << 1) | ((value >> i) & 1)
    return result


def lay_tiles(table, base, tiles, lhs, spans, row_base, blocks, block, at=0):
    for b in range(blocks):
        for c in range(blocks):
            entry = table[base + b * blocks + c]
            tile = tiles[jnp.maximum(entry - 1, 0)]
            tile = jnp.where(entry > 0, tile, jnp.zeros_like(tile))
            top = at
            for first, rows in spans:
                lhs[pl.ds(top + b * rows, rows), pl.ds(c * block, block)] = tile[first - row_base : first - row_base + rows]
                top = top + blocks * rows


def first_part(me, slot, col, tile_id, touched, tiles, features, after, first, count, span):
    block = tiles.shape[1]
    blocks = features.shape[0] // block
    width = features.shape[1]
    edges, cap = touched.shape[1], touched.shape[2]
    bits = edges.bit_length() - 1
    products = slot.shape[0]
    start, rows = span
    square = blocks * blocks

    def body(me_ref, slot_hbm, col_hbm, id_hbm, touched_ref, tiles_hbm, x_hbm, after_ref, *refs):
        table, low, high, x_out, *scratch = refs
        slot_ref, col_ref, id_ref, tiles_ref, lhs, bases, sems = scratch
        loads = [
            pltpu.make_async_copy(slot_hbm, slot_ref, sems.at[0]),
            pltpu.make_async_copy(col_hbm, col_ref, sems.at[1]),
            pltpu.make_async_copy(id_hbm, id_ref, sems.at[2]),
            pltpu.make_async_copy(x_hbm, x_out, sems.at[3]),
            pltpu.make_async_copy(tiles_hbm.at[:, pl.ds(start, rows)], tiles_ref, sems.at[4]),
        ]
        for load in loads:
            load.start()

        def clear(i, carry):
            table[i] = 0
            return carry

        lax.fori_loop(0, edges * square, clear, 0, unroll=16)

        def place_slot(k, carry):
            owner, _ = split(k, cap)
            place = reversed_bits(owner ^ me_ref[0], bits)
            bases[k] = (place * blocks + touched_ref[k]) * blocks
            return carry

        lax.fori_loop(0, edges * cap, place_slot, 0, unroll=8)
        for load in loads[:3]:
            load.wait()

        def enter(k, carry):
            table[bases[slot_ref[k]] + col_ref[k]] = id_ref[k] + 1
            return carry

        lax.fori_loop(0, products, enter, 0, unroll=8)
        for load in loads[3:]:
            load.wait()

        def one_owner(i, carry):
            at = pl.multiple_of(i * blocks * rows, blocks * rows)
            lay_tiles(table, (first + i) * square, tiles_ref, lhs, [span], start, blocks, block, at)
            return carry

        lax.fori_loop(0, count, one_owner, 0)
        half = count // 2 * blocks * rows
        for out, at in ((high, half), (low, 0)):
            total = jnp.dot(lhs[pl.ds(at, half)], x_out[...], preferred_element_type=jnp.float32)
            out[...] = total.astype(jnp.bfloat16).reshape(out.shape)

    part = jax.ShapeDtypeStruct((count // 2, blocks, rows, width), jnp.bfloat16)
    return call(
        body,
        [
            jax.ShapeDtypeStruct((edges * square,), jnp.int32),
            part,
            part,
            jax.ShapeDtypeStruct(features.shape, jnp.bfloat16),
        ],
        [SMEM, HBM, HBM, HBM, SMEM, HBM, HBM, SMEM],
        [SMEM, VMEM, VMEM, VMEM],
        (me, slot, col, tile_id, touched[me[0]].reshape(-1), tiles, features, after),
        [
            pltpu.SMEM((products,), jnp.int32),
            pltpu.SMEM((products,), jnp.int32),
            pltpu.SMEM((products,), jnp.int32),
            pltpu.VMEM((tiles.shape[0], rows, block), jnp.bfloat16),
            pltpu.VMEM((count * blocks * rows, blocks * block), jnp.bfloat16),
            pltpu.SMEM((edges * cap,), jnp.int32),
            pltpu.SemaphoreType.DMA((5,)),
        ],
        limit=62 * 1024 * 1024,
    )


def other_parts(table, tiles, inputs, first, count, spans):
    block = tiles.shape[1]
    blocks = inputs.shape[0] // block
    width = inputs.shape[1]
    total_rows = sum(rows for _, rows in spans)
    half = count // 2

    def body(table_ref, tiles_hbm, x_ref, *refs):
        outs = refs[: 2 * len(spans)]
        tiles_ref, lhs, sem = refs[2 * len(spans) :]
        load = pltpu.make_async_copy(tiles_hbm, tiles_ref, sem.at[0])
        load.start()
        load.wait()

        def one_owner(side):
            def step(i, carry):
                base = (first + side * half + i) * blocks * blocks
                lay_tiles(table_ref, base, tiles_ref, lhs, spans, 0, blocks, block)
                total = jnp.dot(lhs[...], x_ref[...], preferred_element_type=jnp.float32).astype(jnp.bfloat16)
                at = 0
                for n, (_, rows) in enumerate(spans):
                    outs[2 * n + side][i] = total[at : at + blocks * rows].reshape(blocks, rows, width)
                    at += blocks * rows
                return carry

            return step

        for side in (1, 0):
            lax.fori_loop(0, half, one_owner(side), 0)

    results = call(
        body,
        [
            jax.ShapeDtypeStruct((half, blocks, rows, width), jnp.bfloat16)
            for _, rows in spans
            for side in range(2)
        ],
        [SMEM, HBM, VMEM],
        [VMEM] * (2 * len(spans)),
        (table, tiles, inputs),
        [
            pltpu.VMEM(tiles.shape, jnp.bfloat16),
            pltpu.VMEM((blocks * total_rows, blocks * block), jnp.bfloat16),
            pltpu.SemaphoreType.DMA((1,)),
        ],
    )
    return [(results[2 * n], results[2 * n + 1]) for n in range(len(spans))]


def add_and_send(total, got):
    def body(ins, outs):
        outs[0][...] = (ins[0][...].astype(jnp.float32) + ins[1][...].astype(jnp.float32)).astype(jnp.bfloat16)

    return Task(body, [total, got], [jax.ShapeDtypeStruct(got.shape, jnp.bfloat16)])


def add_and_halve(terms):
    count, *shape = terms[0].shape
    left = count // 2

    def body(ins, outs):
        value = ins[0][...].astype(jnp.float32)
        for term in ins[1:]:
            value = value + term[...].astype(jnp.float32)
        if left:
            outs[0][...] = value[:left]
            outs[1][...] = value[left:].astype(jnp.bfloat16)
        else:
            outs[0][...] = value[0].astype(jnp.bfloat16)

    if left:
        out_shape = [
            jax.ShapeDtypeStruct((left, *shape), jnp.float32),
            jax.ShapeDtypeStruct((count - left, *shape), jnp.bfloat16),
        ]
    else:
        out_shape = [jax.ShapeDtypeStruct(tuple(shape), jnp.bfloat16)]
    return Task(body, terms, out_shape)


def mix_and_pick(me, mine, choice, weight, pieces, edges):
    blocks, rows, depth = pieces[0].shape
    width = weight.shape[1]

    def body(ins, outs):
        me_ref, mine_ref, choice_ref, w_ref, *piece_refs = ins
        out_ref, picked_ref = outs
        total = jnp.zeros((blocks * rows, width), jnp.float32)
        for j, piece in enumerate(piece_refs):
            at = pl.multiple_of((mine_ref[0] ^ j) * depth, depth)
            total += jnp.dot(
                piece[...].reshape(blocks * rows, depth),
                w_ref[pl.ds(at, depth)],
                preferred_element_type=jnp.float32,
            )
        out_ref[...] = jnp.maximum(total, 0.0).astype(jnp.bfloat16).reshape(out_ref.shape)
        for p in range(edges):
            for j in range(READ_CAP):
                picked_ref[me_ref[0] ^ p, j] = out_ref[choice_ref[p * READ_CAP + j]]

    return Task(
        body,
        [me, mine, choice, weight, *pieces],
        [
            jax.ShapeDtypeStruct((blocks, rows, width), jnp.bfloat16),
            jax.ShapeDtypeStruct((edges, READ_CAP, rows, width), jnp.bfloat16),
        ],
        [SMEM] * 3 + [VMEM] * (1 + len(pieces)),
    )


def wait_for(token):
    return Task(lambda ins, outs: None, [token], [])


def lay_out(entry, mixed, got, outputs, count, span, block):
    blocks, _, width = mixed.shape
    edges = got.shape[0]
    start, rows = span
    slots = edges * READ_CAP

    def body(entry_ref, mixed_ref, got_ref, *refs):
        hidden_ref, ghost_ref, token, sems = refs[-4:]
        token[...] = jnp.zeros_like(token)
        own = pltpu.make_async_copy(mixed_ref, hidden_ref.at[:, pl.ds(start, rows)], sems.at[slots])
        own.start()

        def each(act):
            for o in range(edges):
                for j in range(READ_CAP):
                    r = entry_ref[o * READ_CAP + j]

                    @pl.when(r >= 0)
                    def _():
                        target = ghost_ref.at[r, pl.ds(start, rows)]
                        act(pltpu.make_async_copy(got_ref.at[o, j], target, sems.at[o * READ_CAP + j]))

        each(lambda copy: copy.start())
        own.wait()
        each(lambda copy: copy.wait())

    operands = (entry, mixed, got, *outputs)
    return call(
        body,
        [
            jax.ShapeDtypeStruct((blocks, block, width), jnp.bfloat16),
            jax.ShapeDtypeStruct((count, block, width), jnp.bfloat16),
            jax.ShapeDtypeStruct((8, 128), jnp.float32),
        ],
        [SMEM] + [VMEM] * 2 + [HBM] * len(outputs),
        [HBM, HBM, VMEM],
        operands,
        [pltpu.SemaphoreType.DMA((slots + 1,))],
        aliases={3: 0, 4: 1} if outputs else None,
    )


def local(features, tiles, tile_slot, tile_col, tile_id, touched, weight, readers):
    edges, feats = lax.axis_size("edge"), lax.axis_size("feat")
    half = edges // 2
    me, mine = lax.axis_index("edge"), lax.axis_index("feat")
    block = tiles.shape[1]
    blocks = features.shape[0] // block
    width = features.shape[1]
    unit = block // sum(SHARES)
    spans = [(sum(SHARES[:i]) * unit, share * unit) for i, share in enumerate(SHARES)]

    def flip(value, bit, axis="edge"):
        return lax.ppermute(value, axis, [(d, d ^ bit) for d in range(lax.axis_size(axis))])

    neighbour = flip(readers, 1)
    lists, bit = jnp.stack([readers, neighbour]), 2
    while bit < edges:
        lists = jnp.concatenate([lists, flip(lists, bit)])
        bit *= 2
    count = readers.shape[0]
    order = jnp.arange(count, dtype=jnp.int32)
    position = jnp.arange(READ_CAP, dtype=jnp.int32)
    earlier = order[None, :] < order[:, None]
    asked = lists // blocks == me
    rank = jnp.sum((asked[:, None, :] & earlier[None]).astype(jnp.int32), axis=2)
    chosen = asked[:, None, :] & (rank[:, None, :] == position[None, :, None])
    choice = jnp.sum(jnp.where(chosen, (lists % blocks)[:, None, :], 0), axis=2).reshape(-1)
    owner = readers // blocks
    rank = jnp.sum(((owner[:, None] == owner[None, :]) & earlier).astype(jnp.int32), axis=1)
    place = jnp.arange(edges * READ_CAP, dtype=jnp.int32)
    found = (owner * READ_CAP + rank)[None, :] == place[:, None]
    entry = jnp.sum(jnp.where(found, order[None, :] + 1, 0), axis=1) - 1
    me, mine = me.reshape(1), mine.reshape(1)

    table, low, high, inputs = first_part(
        me, tile_slot, tile_col, tile_id, touched, tiles, features, neighbour, half, half, spans[0]
    )
    away = [(low, high)] + other_parts(table, tiles, inputs, half, half, spans[1:])
    kept = other_parts(table, tiles, inputs, 0, half, spans)
    outputs = ()

    def one_part(part):
        nonlocal outputs
        first = flip(away[part][1], 1)
        (sent,) = yield add_and_send(kept[part][1], first)
        second, got = flip(away[part][0], 1), flip(sent, 2)
        terms, bit = [kept[part][0], second, got], 2
        while True:
            total, *sent = yield add_and_halve(terms)
            if not sent:
                break
            bit *= 2
            terms = [total, flip(sent[0], bit)]
        pieces = [total] + [flip(total, j, "feat") for j in range(1, feats)]
        mixed, picked = yield mix_and_pick(me, mine, choice, weight, pieces, edges)
        got = lax.all_to_all(picked, "edge", split_axis=0, concat_axis=0)
        *outputs, token = lay_out(entry, mixed, got, outputs, count, spans[part], block)
        tokens[step + 2] = token

    tokens = {}
    ways, tasks, part = {}, {}, 0
    step = 0
    while part < len(spans) or tasks:
        if step % 2 == 0 and part < len(spans):
            ways[part] = one_part(part)
            tasks[part] = next(ways[part])
            part += 1
        ready = sorted(tasks)
        waits = [wait_for(tokens[step])] if step in tokens else []
        results = joint([tasks[n] for n in ready] + waits)
        tasks = {}
        for n, result in zip(ready, results):
            try:
                tasks[n] = ways[n].send(result)
            except StopIteration:
                pass
        step += 1
    hidden, ghosts = outputs
    return hidden.reshape(blocks * block, width), ghosts.reshape(-1, width)


def solution(mesh):
    in_specs = (
        P("edge", "feat"),
        P("edge", None, None),
        P("edge"),
        P("edge"),
        P("edge"),
        P(),
        P(None, "feat"),
        P("edge"),
    )
    out_specs = (P("edge", "feat"), P("edge", "feat"))
    return jax.shard_map(local, mesh=mesh, in_specs=in_specs, out_specs=out_specs, check_vma=False)
```

```python
import jax
import jax.numpy as jnp
from jax import lax
from jax.experimental import pallas as pl
from jax.experimental.pallas import tpu as pltpu
from jax.sharding import PartitionSpec as P

SHARES = (3, 3, 2)
READ_CAP = 2
VMEM_BYTES = 12 * 1024 * 1024
UNIT_TIME, STEP_TIME, LATENCY = 10.5, 1.2, 2.0

SMEM = pl.BlockSpec(memory_space=pltpu.SMEM)
VMEM = pl.BlockSpec(memory_space=pltpu.VMEM)
HBM = pl.BlockSpec(memory_space=pltpu.HBM)
TOKEN = jax.ShapeDtypeStruct((8, 128), jnp.float32)


def call(body, out_shape, in_specs, out_specs, operands, scratch=(), aliases=None, limit=VMEM_BYTES):
    return pl.pallas_call(
        body,
        out_shape=out_shape,
        in_specs=in_specs,
        out_specs=out_specs,
        scratch_shapes=list(scratch),
        input_output_aliases=aliases or {},
        compiler_params=pltpu.CompilerParams(vmem_limit_bytes=limit),
        cost_estimate=pl.CostEstimate(flops=0, bytes_accessed=1, transcendentals=0),
    )(*operands)


def split(value, size):
    if size & (size - 1) == 0:
        return value >> (size.bit_length() - 1), value & (size - 1)
    return lax.div(value, size), lax.rem(value, size)


def reversed_bits(value, bits):
    result = value & 1
    for i in range(1, bits):
        result = (result << 1) | ((value >> i) & 1)
    return result


def offsets_of(size, lowest):
    offsets, bit = [0], size // 2
    while bit >= lowest:
        offsets += [offset | bit for offset in offsets]
        bit //= 2
    return offsets


def lay_tiles(table, base, tiles, lhs, spans, row_base, blocks, block, at=0):
    for b in range(blocks):
        for c in range(blocks):
            entry = table[base + b * blocks + c]
            tile = tiles[jnp.maximum(entry - 1, 0)]
            tile = jnp.where(entry > 0, tile, jnp.zeros_like(tile))
            top = at
            for first, rows in spans:
                lhs[pl.ds(top + b * rows, rows), pl.ds(c * block, block)] = tile[first - row_base : first - row_base + rows]
                top = top + blocks * rows


def first_part(me, slot, col, tile_id, touched, tiles, features, after, first, count, span):
    block = tiles.shape[1]
    blocks = features.shape[0] // block
    width = features.shape[1]
    edges, cap = touched.shape[1], touched.shape[2]
    bits = edges.bit_length() - 1
    products = slot.shape[0]
    start, rows = span
    square = blocks * blocks

    def body(me_ref, slot_hbm, col_hbm, id_hbm, touched_ref, tiles_hbm, x_hbm, after_ref, *refs):
        table, out, x_out, *scratch = refs
        slot_ref, col_ref, id_ref, tiles_ref, lhs, bases, sems = scratch
        loads = [
            pltpu.make_async_copy(slot_hbm, slot_ref, sems.at[0]),
            pltpu.make_async_copy(col_hbm, col_ref, sems.at[1]),
            pltpu.make_async_copy(id_hbm, id_ref, sems.at[2]),
            pltpu.make_async_copy(x_hbm, x_out, sems.at[3]),
            pltpu.make_async_copy(tiles_hbm.at[:, pl.ds(start, rows)], tiles_ref, sems.at[4]),
        ]
        for load in loads:
            load.start()

        def clear(i, carry):
            table[i] = 0
            return carry

        lax.fori_loop(0, edges * square, clear, 0, unroll=16)

        def place_slot(k, carry):
            owner, _ = split(k, cap)
            place = reversed_bits(owner ^ me_ref[0], bits)
            bases[k] = (place * blocks + touched_ref[k]) * blocks
            return carry

        lax.fori_loop(0, edges * cap, place_slot, 0, unroll=8)
        for load in loads[:3]:
            load.wait()

        def enter(k, carry):
            table[bases[slot_ref[k]] + col_ref[k]] = id_ref[k] + 1
            return carry

        lax.fori_loop(0, products, enter, 0, unroll=8)
        for load in loads[3:]:
            load.wait()

        def one_owner(i, carry):
            at = pl.multiple_of(i * blocks * rows, blocks * rows)
            lay_tiles(table, (first + i) * square, tiles_ref, lhs, [span], start, blocks, block, at)
            return carry

        lax.fori_loop(0, count, one_owner, 0)
        total = jnp.dot(lhs[...], x_out[...], preferred_element_type=jnp.float32)
        out[...] = total.astype(jnp.bfloat16).reshape(out.shape)

    return call(
        body,
        [
            jax.ShapeDtypeStruct((edges * square,), jnp.int32),
            jax.ShapeDtypeStruct((count, blocks, rows, width), jnp.bfloat16),
            jax.ShapeDtypeStruct(features.shape, jnp.bfloat16),
        ],
        [SMEM, HBM, HBM, HBM, SMEM, HBM, HBM, SMEM],
        [SMEM, VMEM, VMEM],
        (me, slot, col, tile_id, touched[me[0]].reshape(-1), tiles, features, after),
        [
            pltpu.SMEM((products,), jnp.int32),
            pltpu.SMEM((products,), jnp.int32),
            pltpu.SMEM((products,), jnp.int32),
            pltpu.VMEM((tiles.shape[0], rows, block), jnp.bfloat16),
            pltpu.VMEM((count * blocks * rows, blocks * block), jnp.bfloat16),
            pltpu.SMEM((edges * cap,), jnp.int32),
            pltpu.SemaphoreType.DMA((5,)),
        ],
        limit=62 * 1024 * 1024,
    )


def other_parts(table, tiles, inputs, jobs, weight=None):
    block = tiles.shape[1]
    blocks = inputs.shape[0] // block
    width = inputs.shape[1]
    most = max(sum(rows for _, rows in spans) for _, _, spans in jobs) * blocks
    given = [] if weight is None else [weight]
    shapes = [
        jax.ShapeDtypeStruct((count, blocks, rows, width), jnp.bfloat16) for _, count, spans in jobs for _, rows in spans
    ]

    def body(table_ref, tiles_hbm, x_ref, *refs):
        outs = refs[len(given) :]
        tiles_ref, lhs, sems = outs[-3:]
        load = pltpu.make_async_copy(tiles_hbm, tiles_ref, sems.at[0])
        load.start()
        if given:
            load_weight = pltpu.make_async_copy(refs[0], outs[-5], sems.at[1])
            load_weight.start()
            outs[-4][...] = jnp.zeros_like(outs[-4])
        load.wait()
        for first, count, spans in jobs:
            height = blocks * sum(rows for _, rows in spans)

            def one_owner(i, carry):
                lay_tiles(table_ref, (first + i) * blocks * blocks, tiles_ref, lhs, spans, 0, blocks, block)
                total = jnp.dot(lhs[pl.ds(0, height)], x_ref[...], preferred_element_type=jnp.float32)
                total = total.astype(jnp.bfloat16)
                at = 0
                for out, (_, rows) in zip(outs, spans):
                    out[i] = total[at : at + blocks * rows].reshape(blocks, rows, width)
                    at += blocks * rows
                return carry

            lax.fori_loop(0, count, one_owner, 0)
            outs = outs[len(spans) :]
        if given:
            load_weight.wait()

    extra = [jax.ShapeDtypeStruct(weight.shape, weight.dtype), TOKEN] if given else []
    results = call(
        body,
        shapes + extra,
        [SMEM, HBM, VMEM] + [HBM] * len(given),
        [VMEM] * (len(shapes) + len(extra)),
        (table, tiles, inputs, *given),
        [
            pltpu.VMEM(tiles.shape, jnp.bfloat16),
            pltpu.VMEM((most, blocks * block), jnp.bfloat16),
            pltpu.SemaphoreType.DMA((2,)),
        ],
    )
    grouped, at = [], 0
    for _, _, spans in jobs:
        grouped.append(results[at : at + len(spans)])
        at += len(spans)
    return (grouped, *results[at:]) if given else grouped


def combine(token, total, got):
    count, *shape = total.shape
    left = count // 2

    def body(token_ref, total_ref, got_ref, *outs):
        def add(i, carry):
            value = total_ref[i].astype(jnp.float32) + got_ref[i].astype(jnp.float32)
            if not left:
                outs[0][...] = value.astype(jnp.bfloat16)
            else:

                @pl.when(i < left)
                def _():
                    outs[0][jnp.minimum(i, left - 1)] = value

                @pl.when(i >= left)
                def _():
                    outs[1][jnp.maximum(i - left, 0)] = value.astype(jnp.bfloat16)

            return carry

        lax.fori_loop(0, count, add, 0)
        outs[-1][...] = token_ref[...]

    if left:
        out_shape = [
            jax.ShapeDtypeStruct((left, *shape), jnp.float32),
            jax.ShapeDtypeStruct((count - left, *shape), jnp.bfloat16),
        ]
    else:
        out_shape = [jax.ShapeDtypeStruct(tuple(shape), jnp.bfloat16)]
    out_shape.append(TOKEN)
    return call(body, out_shape, [VMEM] * 3, [VMEM] * len(out_shape), (token, total, got))


def join(token, held, got):
    def body(token_ref, held_ref, got_ref, out, token_out):
        out[pl.ds(0, held.shape[0])] = held_ref[...]
        out[pl.ds(held.shape[0], got.shape[0])] = got_ref[...]
        token_out[...] = token_ref[...]

    both = jax.ShapeDtypeStruct((held.shape[0] + got.shape[0], *held.shape[1:]), held.dtype)
    return call(body, [both, TOKEN], [VMEM] * 3, [VMEM] * 2, (token, held, got))


def mix(token, mine, offsets, held, got, weight):
    _, blocks, rows, depth = held.shape
    width = weight.shape[1]

    def body(token_ref, mine_ref, held_ref, got_ref, w_ref, out_ref, token_out):
        total = jnp.zeros((blocks * rows, width), jnp.float32)
        for n, offset in enumerate(offsets):
            piece = (held_ref if n < held.shape[0] else got_ref)[n % held.shape[0]]
            at = pl.multiple_of((mine_ref[0] ^ offset) * depth, depth)
            total += jnp.dot(
                piece.reshape(blocks * rows, depth), w_ref[pl.ds(at, depth)], preferred_element_type=jnp.float32
            )
        out_ref[0] = jnp.maximum(total, 0.0).astype(jnp.bfloat16).reshape(blocks, rows, width)
        token_out[...] = token_ref[...]

    return call(
        body,
        [jax.ShapeDtypeStruct((1, blocks, rows, width), jnp.bfloat16), TOKEN],
        [VMEM, SMEM, VMEM, VMEM, VMEM],
        [VMEM] * 2,
        (token, mine, held, got, weight),
    )


def pick(token, choice, held, got):
    count = choice.shape[0]

    def body(token_ref, choice_ref, held_ref, got_ref, out, token_out):
        for i in range(count):
            n = i // READ_CAP
            source = held_ref if n < held.shape[0] else got_ref
            out[i] = source[n % held.shape[0], choice_ref[i]]
        token_out[...] = token_ref[...]

    return call(
        body,
        [jax.ShapeDtypeStruct((count, *held.shape[2:]), held.dtype), TOKEN],
        [VMEM, SMEM, VMEM, VMEM],
        [VMEM] * 2,
        (token, choice, held, got),
    )


def lay_out(token, me, readers, entry, offsets, held, got, far, outputs, span, block):
    count = readers.shape[0]
    _, blocks, _, width = held.shape
    start, rows = span
    slots = 2 * len(offsets) * READ_CAP

    def body(token_ref, me_ref, readers_ref, entry_ref, held_ref, got_ref, far_ref, *refs):
        hidden_ref, ghost_ref, token_out, sems = refs[-4:]
        own = pltpu.make_async_copy(held_ref.at[0], hidden_ref.at[:, pl.ds(start, rows)], sems.at[slots])
        own.start()

        def each(act):
            for n, offset in enumerate(offsets):
                for j in range(READ_CAP):
                    i = n * READ_CAP + j
                    listed = entry_ref[(me_ref[0] ^ offset) * READ_CAP + j]
                    source = held_ref if n < held.shape[0] else got_ref

                    @pl.when(listed >= 0)
                    def _():
                        _, b = split(readers_ref[listed], blocks)
                        target = ghost_ref.at[listed, pl.ds(start, rows)]
                        act(pltpu.make_async_copy(source.at[n % held.shape[0], b], target, sems.at[i]))

                    across = entry_ref[(me_ref[0] ^ 1 ^ offset) * READ_CAP + j]

                    @pl.when(across >= 0)
                    def _():
                        target = ghost_ref.at[across, pl.ds(start, rows)]
                        act(pltpu.make_async_copy(far_ref.at[i], target, sems.at[slots // 2 + i]))

        each(lambda copy: copy.start())
        token_out[...] = token_ref[...]
        own.wait()
        each(lambda copy: copy.wait())

    operands = (token, me, readers, entry, held, got, far, *outputs)
    return call(
        body,
        [
            jax.ShapeDtypeStruct((blocks, block, width), jnp.bfloat16),
            jax.ShapeDtypeStruct((count, block, width), jnp.bfloat16),
            TOKEN,
        ],
        [VMEM] + [SMEM] * 3 + [VMEM] * 3 + [HBM] * len(outputs),
        [HBM, HBM, VMEM],
        operands,
        [pltpu.SemaphoreType.DMA((slots + 1,))],
        aliases={len(operands) - 2: 0, len(operands) - 1: 1} if outputs else None,
    )


def local(features, tiles, tile_slot, tile_col, tile_id, touched, weight, readers):
    edges, feats = lax.axis_size("edge"), lax.axis_size("feat")
    half = edges // 2
    me, mine = lax.axis_index("edge"), lax.axis_index("feat")
    block = tiles.shape[1]
    blocks = features.shape[0] // block
    width = features.shape[1]
    unit = block // sum(SHARES)
    spans = [(sum(SHARES[:i]) * unit, share * unit) for i, share in enumerate(SHARES)]

    def flip(value, bit, axis="edge"):
        return lax.ppermute(value, axis, [(d, d ^ bit) for d in range(lax.axis_size(axis))])

    count = readers.shape[0]
    order = jnp.arange(count, dtype=jnp.int32)
    columns = offsets_of(edges, 2)
    neighbour = flip(readers, 1)

    def listed(values, owners):
        owner = values // blocks
        rank = jnp.sum(((owner[:, None] == owner[None, :]) & (order[None, :] < order[:, None])).astype(jnp.int32), axis=1)
        wanted = jnp.repeat(owners, READ_CAP)
        turn = jnp.arange(wanted.shape[0], dtype=jnp.int32) % READ_CAP
        return (owner[None, :] == wanted[:, None]) & (rank[None, :] == turn[:, None])

    hit = listed(neighbour, lax.bitwise_xor(me, jnp.array(columns, jnp.int32)))
    choice = jnp.sum(jnp.where(hit, (neighbour % blocks)[None, :], 0), axis=1)
    hit = listed(readers, jnp.arange(edges, dtype=jnp.int32))
    entry = jnp.sum(jnp.where(hit, order[None, :] + 1, 0), axis=1) - 1
    me, mine = me.reshape(1), mine.reshape(1)

    table, early, inputs = first_part(
        me, tile_slot, tile_col, tile_id, touched, tiles, features, neighbour, half, half, spans[0]
    )
    later, first_kept = other_parts(table, tiles, inputs, [(half, half, spans[1:]), (0, half, spans[:1])])
    away = [early, *later]
    (kept,), weight, token = other_parts(table, tiles, inputs, [(0, half, spans[1:])], weight)
    kept = [*first_kept, *kept]
    outputs = ()

    def chained(function, *operands):
        nonlocal token
        *results, token = function(token, *operands)
        return results

    def spread(held, size, lowest, axis, link, units):
        bit = size // 2
        while True:
            got = flip(held, bit, axis)
            yield link, units
            if bit == lowest:
                return held, got
            (held,) = chained(join, held, got)
            bit, units = bit // 2, units * 2

    def one_part(part):
        nonlocal outputs
        share = spans[part][1] / block
        got = flip(away[part], 1)
        yield "low", share * half
        total, sent = chained(combine, kept[part], got)
        bit = 2
        while bit < edges:
            got = flip(sent, bit)
            yield "high", share * 2
            total, *sent = chained(combine, total, got)
            sent = sent[0] if sent else None
            bit *= 2
        held, got = yield from spread(total[None], feats, 1, "feat", "feat", share * 0.6)
        (mixed,) = chained(mix, mine, offsets_of(feats, 1), held, got, weight)
        held, got = yield from spread(mixed, edges, 2, "edge", "high", share * 1.5)
        (picked,) = chained(pick, choice, held, got)
        far = flip(picked, 1)
        yield "low", share * 2
        outputs = chained(lay_out, me, readers, entry, columns, held, got, far, outputs, spans[part], block)

    now, free, waiting = 0.0, {"low": 0.0, "high": 0.0, "feat": 0.0}, []

    def advance(part, steps):
        nonlocal now
        link, units = next(steps, (None, 0))
        now += STEP_TIME
        if link is not None:
            free[link] = max(free[link], now) + units * UNIT_TIME
            waiting.append((free[link] + LATENCY, part, steps))

    for part in range(len(spans)):
        advance(part, one_part(part))
    while waiting:
        ready, part, steps = min(waiting, key=lambda item: item[:2])
        waiting = [item for item in waiting if item[1] != part]
        now = max(now, ready)
        advance(part, steps)
    hidden, ghosts = outputs
    return hidden.reshape(blocks * block, width), ghosts.reshape(-1, width)


def solution(mesh):
    in_specs = (
        P("edge", "feat"),
        P("edge", None, None),
        P("edge"),
        P("edge"),
        P("edge"),
        P(),
        P(None, "feat"),
        P("edge"),
    )
    out_specs = (P("edge", "feat"), P("edge", "feat"))
    return jax.shard_map(local, mesh=mesh, in_specs=in_specs, out_specs=out_specs, check_vma=False)
```

```python
import jax
import jax.numpy as jnp
from jax import lax
from jax.experimental import pallas as pl
from jax.experimental.pallas import tpu as pltpu
from jax.sharding import PartitionSpec as P

SHARES = (2, 2, 2, 2)
READ_CAP = 2
VMEM_BYTES = 12 * 1024 * 1024
UNIT_TIME, START_TIME, STEP_TIME, LATENCY = 11.3, 0.9, 0.4, 0.6

SMEM = pl.BlockSpec(memory_space=pltpu.SMEM)
VMEM = pl.BlockSpec(memory_space=pltpu.VMEM)
HBM = pl.BlockSpec(memory_space=pltpu.HBM)
TOKEN = jax.ShapeDtypeStruct((8, 128), jnp.float32)


def call(body, out_shape, in_specs, out_specs, operands, scratch=(), aliases=None, limit=VMEM_BYTES):
    return pl.pallas_call(
        body,
        out_shape=out_shape,
        in_specs=in_specs,
        out_specs=out_specs,
        scratch_shapes=list(scratch),
        input_output_aliases=aliases or {},
        compiler_params=pltpu.CompilerParams(vmem_limit_bytes=limit),
        cost_estimate=pl.CostEstimate(flops=0, bytes_accessed=1, transcendentals=0),
    )(*operands)


def split(value, size):
    if size & (size - 1) == 0:
        return value >> (size.bit_length() - 1), value & (size - 1)
    return lax.div(value, size), lax.rem(value, size)


def reversed_bits(value, bits):
    result = value & 1
    for i in range(1, bits):
        result = (result << 1) | ((value >> i) & 1)
    return result


def planned_order(ways):
    now, order, flows, current, place = 0.0, [], [], {}, [0] * len(ways)

    def active():
        waiting = [f for f in flows if "x" in f["links"]][1:]
        running = [f for f in flows if not any(f is w for w in waiting)]
        load = {}
        for f in running:
            for link, weight in f["links"].items():
                load[link] = load.get(link, 0.0) + weight
        return [(f, min(1.0 / load[link] for link in f["links"])) for f in running]

    def advance(until):
        nonlocal now
        while now < until:
            running = active()
            step = min([until - now] + [f["left"] / rate for f, rate in running])
            now += max(step, 1e-3)
            for f, rate in running:
                f["left"] -= step * rate
                if f["left"] <= 1e-6:
                    f["end"] = now + LATENCY
            flows[:] = [f for f in flows if f["left"] > 1e-6]

    def begin(n):
        links, units = ways[n][place[n]]
        advance(now + START_TIME)
        current[n] = {"links": links, "left": units * UNIT_TIME, "end": None}
        flows.append(current[n])

    for n in range(len(ways)):
        begin(n)
    while current:
        ended = [(f["end"], n) for n, f in current.items() if f["end"] is not None and f["end"] <= now]
        if not ended:
            advance(now + 0.05)
            continue
        _, n = min(ended)
        order.append(n)
        del current[n]
        place[n] += 1
        advance(now + STEP_TIME)
        if place[n] < len(ways[n]):
            begin(n)
    return order


def offsets_of(size, lowest):
    offsets, bit = [0], size // 2
    while bit >= lowest:
        offsets += [offset | bit for offset in offsets]
        bit //= 2
    return offsets


def lay_tiles(table, base, tiles, lhs, spans, row_base, blocks, block, at=0):
    for b in range(blocks):
        for c in range(blocks):
            entry = table[base + b * blocks + c]
            tile = tiles[jnp.maximum(entry - 1, 0)]
            tile = jnp.where(entry > 0, tile, jnp.zeros_like(tile))
            top = at
            for first, rows in spans:
                lhs[pl.ds(top + b * rows, rows), pl.ds(c * block, block)] = tile[first - row_base : first - row_base + rows]
                top = top + blocks * rows


def first_part(me, slot, col, tile_id, touched, tiles, features, after, first, count, span):
    block = tiles.shape[1]
    blocks = features.shape[0] // block
    width = features.shape[1]
    edges, cap = touched.shape[1], touched.shape[2]
    bits = edges.bit_length() - 1
    products = slot.shape[0]
    start, rows = span
    square = blocks * blocks

    def body(me_ref, slot_hbm, col_hbm, id_hbm, touched_ref, tiles_hbm, x_hbm, after_ref, *refs):
        table, out, x_out, *scratch = refs
        slot_ref, col_ref, id_ref, tiles_ref, lhs, bases, sems = scratch
        loads = [
            pltpu.make_async_copy(slot_hbm, slot_ref, sems.at[0]),
            pltpu.make_async_copy(col_hbm, col_ref, sems.at[1]),
            pltpu.make_async_copy(id_hbm, id_ref, sems.at[2]),
            pltpu.make_async_copy(x_hbm, x_out, sems.at[3]),
            pltpu.make_async_copy(tiles_hbm.at[:, pl.ds(start, rows)], tiles_ref, sems.at[4]),
        ]
        for load in loads:
            load.start()

        def clear(i, carry):
            table[i] = 0
            return carry

        lax.fori_loop(0, edges * square, clear, 0, unroll=16)

        def place_slot(k, carry):
            owner, _ = split(k, cap)
            place = reversed_bits(owner ^ me_ref[0], bits)
            bases[k] = (place * blocks + touched_ref[k]) * blocks
            return carry

        lax.fori_loop(0, edges * cap, place_slot, 0, unroll=8)
        for load in loads[:3]:
            load.wait()

        def enter(k, carry):
            table[bases[slot_ref[k]] + col_ref[k]] = id_ref[k] + 1
            return carry

        lax.fori_loop(0, products, enter, 0, unroll=8)
        for load in loads[3:]:
            load.wait()

        def one_owner(i, carry):
            at = pl.multiple_of(i * blocks * rows, blocks * rows)
            lay_tiles(table, (first + i) * square, tiles_ref, lhs, [span], start, blocks, block, at)
            return carry

        lax.fori_loop(0, count, one_owner, 0)
        total = jnp.dot(lhs[...], x_out[...], preferred_element_type=jnp.float32)
        out[...] = total.astype(jnp.bfloat16).reshape(out.shape)

    return call(
        body,
        [
            jax.ShapeDtypeStruct((edges * square,), jnp.int32),
            jax.ShapeDtypeStruct((count, blocks, rows, width), jnp.bfloat16),
            jax.ShapeDtypeStruct(features.shape, jnp.bfloat16),
        ],
        [SMEM, HBM, HBM, HBM, SMEM, HBM, HBM, SMEM],
        [SMEM, VMEM, VMEM],
        (me, slot, col, tile_id, touched[me[0]].reshape(-1), tiles, features, after),
        [
            pltpu.SMEM((products,), jnp.int32),
            pltpu.SMEM((products,), jnp.int32),
            pltpu.SMEM((products,), jnp.int32),
            pltpu.VMEM((tiles.shape[0], rows, block), jnp.bfloat16),
            pltpu.VMEM((count * blocks * rows, blocks * block), jnp.bfloat16),
            pltpu.SMEM((edges * cap,), jnp.int32),
            pltpu.SemaphoreType.DMA((5,)),
        ],
        limit=62 * 1024 * 1024,
    )


def other_parts(table, tiles, inputs, jobs, weight=None):
    block = tiles.shape[1]
    blocks = inputs.shape[0] // block
    width = inputs.shape[1]
    most = max(sum(rows for _, rows in spans) for _, _, spans in jobs) * blocks
    given = [] if weight is None else [weight]
    shapes = [
        jax.ShapeDtypeStruct((count, blocks, rows, width), jnp.bfloat16) for _, count, spans in jobs for _, rows in spans
    ]

    def body(table_ref, tiles_hbm, x_ref, *refs):
        outs = refs[len(given) :]
        tiles_ref, lhs, sems = outs[-3:]
        load = pltpu.make_async_copy(tiles_hbm, tiles_ref, sems.at[0])
        load.start()
        if given:
            load_weight = pltpu.make_async_copy(refs[0], outs[-5], sems.at[1])
            load_weight.start()
            outs[-4][...] = jnp.zeros_like(outs[-4])
        load.wait()
        for first, count, spans in jobs:
            height = blocks * sum(rows for _, rows in spans)

            def one_owner(i, carry):
                lay_tiles(table_ref, (first + i) * blocks * blocks, tiles_ref, lhs, spans, 0, blocks, block)
                total = jnp.dot(lhs[pl.ds(0, height)], x_ref[...], preferred_element_type=jnp.float32)
                total = total.astype(jnp.bfloat16)
                at = 0
                for out, (_, rows) in zip(outs, spans):
                    out[i] = total[at : at + blocks * rows].reshape(blocks, rows, width)
                    at += blocks * rows
                return carry

            lax.fori_loop(0, count, one_owner, 0)
            outs = outs[len(spans) :]
        if given:
            load_weight.wait()

    extra = [jax.ShapeDtypeStruct(weight.shape, weight.dtype), TOKEN] if given else []
    results = call(
        body,
        shapes + extra,
        [SMEM, HBM, VMEM] + [HBM] * len(given),
        [VMEM] * (len(shapes) + len(extra)),
        (table, tiles, inputs, *given),
        [
            pltpu.VMEM(tiles.shape, jnp.bfloat16),
            pltpu.VMEM((most, blocks * block), jnp.bfloat16),
            pltpu.SemaphoreType.DMA((2,)),
        ],
    )
    grouped, at = [], 0
    for _, _, spans in jobs:
        grouped.append(results[at : at + len(spans)])
        at += len(spans)
    return (grouped, *results[at:]) if given else grouped


def combine(token, total, got, at_hand):
    count, *shape = total.shape
    left = count // 2

    def body(token_ref, total_ref, got_ref, at_hand_ref, *outs):
        def add(i, carry):
            value = total_ref[i].astype(jnp.float32) + got_ref[i].astype(jnp.float32)
            if not left:
                outs[0][...] = value.astype(jnp.bfloat16)
            else:

                @pl.when(i < left)
                def _():
                    outs[0][jnp.minimum(i, left - 1)] = value

                @pl.when(i >= left)
                def _():
                    outs[1][jnp.maximum(i - left, 0)] = value.astype(jnp.bfloat16)

            return carry

        lax.fori_loop(0, count, add, 0)
        outs[-1][...] = token_ref[...]

    if left:
        out_shape = [
            jax.ShapeDtypeStruct((left, *shape), jnp.float32),
            jax.ShapeDtypeStruct((count - left, *shape), jnp.bfloat16),
        ]
    else:
        out_shape = [jax.ShapeDtypeStruct(tuple(shape), jnp.bfloat16)]
    out_shape.append(TOKEN)
    return call(body, out_shape, [VMEM] * 4, [VMEM] * len(out_shape), (token, total, got, at_hand))


def join(token, held, got):
    def body(token_ref, held_ref, got_ref, out, token_out):
        out[pl.ds(0, held.shape[0])] = held_ref[...]
        out[pl.ds(held.shape[0], got.shape[0])] = got_ref[...]
        token_out[...] = token_ref[...]

    both = jax.ShapeDtypeStruct((held.shape[0] + got.shape[0], *held.shape[1:]), held.dtype)
    return call(body, [both, TOKEN], [VMEM] * 3, [VMEM] * 2, (token, held, got))


def mix(token, mine, offsets, held, got, weight):
    _, blocks, rows, depth = held.shape
    width = weight.shape[1]

    def body(token_ref, mine_ref, held_ref, got_ref, w_ref, out_ref, token_out):
        total = jnp.zeros((blocks * rows, width), jnp.float32)
        for n, offset in enumerate(offsets):
            piece = (held_ref if n < held.shape[0] else got_ref)[n % held.shape[0]]
            at = pl.multiple_of((mine_ref[0] ^ offset) * depth, depth)
            total += jnp.dot(
                piece.reshape(blocks * rows, depth), w_ref[pl.ds(at, depth)], preferred_element_type=jnp.float32
            )
        out_ref[0] = jnp.maximum(total, 0.0).astype(jnp.bfloat16).reshape(blocks, rows, width)
        token_out[...] = token_ref[...]

    return call(
        body,
        [jax.ShapeDtypeStruct((1, blocks, rows, width), jnp.bfloat16), TOKEN],
        [VMEM, SMEM, VMEM, VMEM, VMEM],
        [VMEM] * 2,
        (token, mine, held, got, weight),
    )


def pick(token, choice, held, got):
    count = choice.shape[0]

    def body(token_ref, choice_ref, held_ref, got_ref, out, token_out):
        for i in range(count):
            n = i // READ_CAP
            source = held_ref if n < held.shape[0] else got_ref
            out[i] = source[n % held.shape[0], choice_ref[i]]
        token_out[...] = token_ref[...]

    return call(
        body,
        [jax.ShapeDtypeStruct((count, *held.shape[2:]), held.dtype), TOKEN],
        [VMEM, SMEM, VMEM, VMEM],
        [VMEM] * 2,
        (token, choice, held, got),
    )


def lay_out(token, me, readers, entry, offsets, held, got, far, outputs, span, block):
    count = readers.shape[0]
    _, blocks, _, width = held.shape
    start, rows = span
    slots = 2 * len(offsets) * READ_CAP

    def body(token_ref, me_ref, readers_ref, entry_ref, held_ref, got_ref, far_ref, *refs):
        hidden_ref, ghost_ref, token_out, sems = refs[-4:]
        own = pltpu.make_async_copy(held_ref.at[0], hidden_ref.at[:, pl.ds(start, rows)], sems.at[slots])
        own.start()

        def each(act):
            for n, offset in enumerate(offsets):
                for j in range(READ_CAP):
                    i = n * READ_CAP + j
                    listed = entry_ref[(me_ref[0] ^ offset) * READ_CAP + j]
                    source = held_ref if n < held.shape[0] else got_ref

                    @pl.when(listed >= 0)
                    def _():
                        _, b = split(readers_ref[listed], blocks)
                        target = ghost_ref.at[listed, pl.ds(start, rows)]
                        act(pltpu.make_async_copy(source.at[n % held.shape[0], b], target, sems.at[i]))

                    across = entry_ref[(me_ref[0] ^ 1 ^ offset) * READ_CAP + j]

                    @pl.when(across >= 0)
                    def _():
                        target = ghost_ref.at[across, pl.ds(start, rows)]
                        act(pltpu.make_async_copy(far_ref.at[i], target, sems.at[slots // 2 + i]))

        each(lambda copy: copy.start())
        token_out[...] = token_ref[...]
        own.wait()
        each(lambda copy: copy.wait())

    operands = (token, me, readers, entry, held, got, far, *outputs)
    return call(
        body,
        [
            jax.ShapeDtypeStruct((blocks, block, width), jnp.bfloat16),
            jax.ShapeDtypeStruct((count, block, width), jnp.bfloat16),
            TOKEN,
        ],
        [VMEM] + [SMEM] * 3 + [VMEM] * 3 + [HBM] * len(outputs),
        [HBM, HBM, VMEM],
        operands,
        [pltpu.SemaphoreType.DMA((slots + 1,))],
        aliases={len(operands) - 2: 0, len(operands) - 1: 1} if outputs else None,
    )


def local(features, tiles, tile_slot, tile_col, tile_id, touched, weight, readers):
    edges, feats = lax.axis_size("edge"), lax.axis_size("feat")
    half = edges // 2
    me, mine = lax.axis_index("edge"), lax.axis_index("feat")
    block = tiles.shape[1]
    blocks = features.shape[0] // block
    width = features.shape[1]
    unit = block // sum(SHARES)
    spans = [(sum(SHARES[:i]) * unit, share * unit) for i, share in enumerate(SHARES)]

    def flip(value, bit, axis="edge"):
        return lax.ppermute(value, axis, [(d, d ^ bit) for d in range(lax.axis_size(axis))])

    count = readers.shape[0]
    order = jnp.arange(count, dtype=jnp.int32)
    columns = offsets_of(edges, 2)
    neighbour = flip(readers, 1)

    def listed(values, owners):
        owner = values // blocks
        rank = jnp.sum(((owner[:, None] == owner[None, :]) & (order[None, :] < order[:, None])).astype(jnp.int32), axis=1)
        wanted = jnp.repeat(owners, READ_CAP)
        turn = jnp.arange(wanted.shape[0], dtype=jnp.int32) % READ_CAP
        return (owner[None, :] == wanted[:, None]) & (rank[None, :] == turn[:, None])

    hit = listed(neighbour, lax.bitwise_xor(me, jnp.array(columns, jnp.int32)))
    choice = jnp.sum(jnp.where(hit, (neighbour % blocks)[None, :], 0), axis=1)
    hit = listed(readers, jnp.arange(edges, dtype=jnp.int32))
    entry = jnp.sum(jnp.where(hit, order[None, :] + 1, 0), axis=1) - 1
    me, mine = me.reshape(1), mine.reshape(1)

    table, early, inputs = first_part(
        me, tile_slot, tile_col, tile_id, touched, tiles, features, neighbour, half, half, spans[0]
    )
    later, first_kept = other_parts(table, tiles, inputs, [(half, half, spans[1:]), (0, half, spans[:1])])
    away = [early, *later]
    (kept,), weight, token = other_parts(table, tiles, inputs, [(0, half, spans[1:])], weight)
    kept = [*first_kept, *kept]
    outputs = ()

    def chained(function, *operands):
        nonlocal token
        *results, token = function(token, *operands)
        return results

    def spread(held, size, lowest, axis):
        bit = size // 2
        while True:
            got = flip(held, bit, axis)
            yield
            if bit == lowest:
                return held, got
            (held,) = chained(join, held, got)
            bit //= 2

    def one_part(part):
        nonlocal outputs
        got = flip(away[part], 1)
        yield
        total, sent = chained(combine, kept[part], got, weight)
        bit = 2
        while bit < edges:
            got = flip(sent, bit)
            yield
            total, *sent = chained(combine, total, got, weight)
            sent = sent[0] if sent else None
            bit *= 2
        held, got = yield from spread(total[None], feats, 1, "feat")
        (mixed,) = chained(mix, mine, offsets_of(feats, 1), held, got, weight)
        held, got = yield from spread(mixed, edges, 2, "edge")
        (picked,) = chained(pick, choice, held, got)
        far = flip(picked, 1)
        yield
        outputs = chained(lay_out, me, readers, entry, columns, held, got, far, outputs, spans[part], block)

    def links_of(bit):
        return {"end": 1.0} if bit == 2 else {"end": 1.0, "middle": 2.0}

    column_bits = [1 << i for i in range(1, edges.bit_length() - 1)]
    feat_bits = [1 << i for i in reversed(range(feats.bit_length() - 1))]
    ways = []
    for _, rows in spans:
        share = rows / block
        way = [({"x": 1.0}, share * half * 1.15)]
        way += [(links_of(bit), share * half / bit) for bit in column_bits]
        way += [({"chip" if bit == 1 else "feat": 1.0}, share * (1.0 if bit > 1 else 0.3)) for bit in feat_bits]
        way += [(links_of(bit), share * half / bit) for bit in reversed(column_bits)]
        ways.append(way + [({"x": 1.0}, share * READ_CAP / blocks * half)])
    steps = [one_part(part) for part in range(len(spans))]
    for step in steps:
        next(step)
    for part in planned_order(ways):
        next(steps[part], None)
    hidden, ghosts = outputs
    return hidden.reshape(blocks * block, width), ghosts.reshape(-1, width)


def solution(mesh):
    in_specs = (
        P("edge", "feat"),
        P("edge", None, None),
        P("edge"),
        P("edge"),
        P("edge"),
        P(),
        P(None, "feat"),
        P("edge"),
    )
    out_specs = (P("edge", "feat"), P("edge", "feat"))
    return jax.shard_map(local, mesh=mesh, in_specs=in_specs, out_specs=out_specs, check_vma=False)
```

```python
import jax
import jax.numpy as jnp
from jax import lax
from jax.experimental import pallas as pl
from jax.experimental.pallas import tpu as pltpu
from jax.sharding import PartitionSpec as P

SHARES = (2, 2, 1, 2, 1)
ORDER = (
    0, 0, 0, 1, 3, 1, 0, 3, 2, 0, 1, 4, 3, 2, 0, 2, 1, 4, 3, 1, 2, 3, 4, 1, 4, 3, 4, 2, 0, 1, 0, 4,
    3, 2, 1, 4, 2, 3, 4, 2,
)
READ_CAP = 2
VMEM_BYTES = 12 * 1024 * 1024
UNIT_TIME, START_TIME, STEP_TIME, LATENCY = 11.3, 0.9, 0.4, 0.6

SMEM = pl.BlockSpec(memory_space=pltpu.SMEM)
VMEM = pl.BlockSpec(memory_space=pltpu.VMEM)
HBM = pl.BlockSpec(memory_space=pltpu.HBM)
TOKEN = jax.ShapeDtypeStruct((8, 128), jnp.float32)


def call(body, out_shape, in_specs, out_specs, operands, scratch=(), aliases=None, limit=VMEM_BYTES):
    return pl.pallas_call(
        body,
        out_shape=out_shape,
        in_specs=in_specs,
        out_specs=out_specs,
        scratch_shapes=list(scratch),
        input_output_aliases=aliases or {},
        compiler_params=pltpu.CompilerParams(vmem_limit_bytes=limit),
        cost_estimate=pl.CostEstimate(flops=0, bytes_accessed=1, transcendentals=0),
    )(*operands)


def split(value, size):
    if size & (size - 1) == 0:
        return value >> (size.bit_length() - 1), value & (size - 1)
    return lax.div(value, size), lax.rem(value, size)


def reversed_bits(value, bits):
    result = value & 1
    for i in range(1, bits):
        result = (result << 1) | ((value >> i) & 1)
    return result


def planned_order(ways):
    now, order, flows, current, place = 0.0, [], [], {}, [0] * len(ways)

    def active():
        waiting = [f for f in flows if "x" in f["links"]][1:]
        running = [f for f in flows if not any(f is w for w in waiting)]
        load = {}
        for f in running:
            for link, weight in f["links"].items():
                load[link] = load.get(link, 0.0) + weight
        return [(f, min(1.0 / load[link] for link in f["links"])) for f in running]

    def advance(until):
        nonlocal now
        while now < until:
            running = active()
            step = min([until - now] + [f["left"] / rate for f, rate in running])
            now += max(step, 1e-3)
            for f, rate in running:
                f["left"] -= step * rate
                if f["left"] <= 1e-6:
                    f["end"] = now + LATENCY
            flows[:] = [f for f in flows if f["left"] > 1e-6]

    def begin(n):
        links, units = ways[n][place[n]]
        advance(now + START_TIME)
        current[n] = {"links": links, "left": units * UNIT_TIME, "end": None}
        flows.append(current[n])

    for n in range(len(ways)):
        begin(n)
    while current:
        ended = [(f["end"], n) for n, f in current.items() if f["end"] is not None and f["end"] <= now]
        if not ended:
            advance(now + 0.05)
            continue
        _, n = min(ended)
        order.append(n)
        del current[n]
        place[n] += 1
        advance(now + STEP_TIME)
        if place[n] < len(ways[n]):
            begin(n)
    return order


def offsets_of(size, lowest):
    offsets, bit = [0], size // 2
    while bit >= lowest:
        offsets += [offset | bit for offset in offsets]
        bit //= 2
    return offsets


def lay_tiles(table, base, tiles, lhs, spans, row_base, blocks, block, at=0):
    for b in range(blocks):
        for c in range(blocks):
            entry = table[base + b * blocks + c]
            tile = tiles[jnp.maximum(entry - 1, 0)]
            tile = jnp.where(entry > 0, tile, jnp.zeros_like(tile))
            top = at
            for first, rows in spans:
                lhs[pl.ds(top + b * rows, rows), pl.ds(c * block, block)] = tile[first - row_base : first - row_base + rows]
                top = top + blocks * rows


def first_part(me, slot, col, tile_id, touched, tiles, features, readers, neighbour, first, count, span):
    block = tiles.shape[1]
    blocks = features.shape[0] // block
    width = features.shape[1]
    edges, cap = touched.shape[1], touched.shape[2]
    bits = edges.bit_length() - 1
    products = slot.shape[0]
    half = edges // 2
    start, rows = span
    square = blocks * blocks

    listed = readers.shape[0]

    def body(me_ref, slot_hbm, col_hbm, id_hbm, touched_ref, tiles_hbm, x_hbm, readers_ref, neighbour_ref, *refs):
        table, choice, entry, out, x_out, *scratch = refs
        slot_ref, col_ref, id_ref, tiles_ref, lhs, bases, seen, sems = scratch
        loads = [
            pltpu.make_async_copy(slot_hbm, slot_ref, sems.at[0]),
            pltpu.make_async_copy(col_hbm, col_ref, sems.at[1]),
            pltpu.make_async_copy(id_hbm, id_ref, sems.at[2]),
            pltpu.make_async_copy(x_hbm, x_out, sems.at[3]),
            pltpu.make_async_copy(tiles_hbm.at[:, pl.ds(start, rows)], tiles_ref, sems.at[4]),
        ]
        for load in loads:
            load.start()

        def clear(i, carry):
            table[i] = 0
            return carry

        lax.fori_loop(0, edges * square, clear, 0, unroll=16)

        def place_slot(k, carry):
            owner, _ = split(k, cap)
            place = reversed_bits(owner ^ me_ref[0], bits)
            bases[k] = (place * blocks + touched_ref[k]) * blocks
            return carry

        lax.fori_loop(0, edges * cap, place_slot, 0, unroll=8)
        for load in loads[:3]:
            load.wait()

        for i in range(half * READ_CAP + 1):
            choice[i] = 0
        for i in range(edges * READ_CAP):
            entry[i] = -1
        for i in range(2 * edges):
            seen[i] = 0

        def enter_lists(r, carry):
            owner, _ = split(readers_ref[r], blocks)
            turn = seen[owner]
            seen[owner] = turn + 1
            entry[owner * READ_CAP + jnp.minimum(turn, READ_CAP - 1)] = r
            owner, b = split(neighbour_ref[r], blocks)
            turn = seen[edges + owner]
            seen[edges + owner] = turn + 1
            peer = owner ^ me_ref[0]
            row = reversed_bits(peer >> 1, bits - 1) * READ_CAP + jnp.minimum(turn, READ_CAP - 1)
            choice[jnp.where(peer & 1 == 0, row, half * READ_CAP)] = b
            return carry

        lax.fori_loop(0, listed, enter_lists, 0)

        def enter(k, carry):
            table[bases[slot_ref[k]] + col_ref[k]] = id_ref[k] + 1
            return carry

        lax.fori_loop(0, products, enter, 0, unroll=8)
        for load in loads[3:]:
            load.wait()

        def one_owner(i, carry):
            at = pl.multiple_of(i * blocks * rows, blocks * rows)
            lay_tiles(table, (first + i) * square, tiles_ref, lhs, [span], start, blocks, block, at)
            return carry

        lax.fori_loop(0, count, one_owner, 0)
        total = jnp.dot(lhs[...], x_out[...], preferred_element_type=jnp.float32)
        out[...] = total.astype(jnp.bfloat16).reshape(out.shape)

    return call(
        body,
        [
            jax.ShapeDtypeStruct((edges * square,), jnp.int32),
            jax.ShapeDtypeStruct((half * READ_CAP + 1,), jnp.int32),
            jax.ShapeDtypeStruct((edges * READ_CAP,), jnp.int32),
            jax.ShapeDtypeStruct((count, blocks, rows, width), jnp.bfloat16),
            jax.ShapeDtypeStruct(features.shape, jnp.bfloat16),
        ],
        [SMEM, HBM, HBM, HBM, SMEM, HBM, HBM, SMEM, SMEM],
        [SMEM, SMEM, SMEM, VMEM, VMEM],
        (me, slot, col, tile_id, touched[me[0]].reshape(-1), tiles, features, readers, neighbour),
        [
            pltpu.SMEM((products,), jnp.int32),
            pltpu.SMEM((products,), jnp.int32),
            pltpu.SMEM((products,), jnp.int32),
            pltpu.VMEM((tiles.shape[0], rows, block), jnp.bfloat16),
            pltpu.VMEM((count * blocks * rows, blocks * block), jnp.bfloat16),
            pltpu.SMEM((edges * cap,), jnp.int32),
            pltpu.SMEM((2 * edges,), jnp.int32),
            pltpu.SemaphoreType.DMA((5,)),
        ],
        limit=62 * 1024 * 1024,
    )


def other_parts(table, tiles, inputs, jobs):
    block = tiles.shape[1]
    blocks = inputs.shape[0] // block
    width = inputs.shape[1]
    most = max(sum(rows for _, rows in spans) for _, _, spans in jobs) * blocks
    shapes = [
        jax.ShapeDtypeStruct((count, blocks, rows, width), jnp.bfloat16) for _, count, spans in jobs for _, rows in spans
    ]

    def body(table_ref, tiles_hbm, x_ref, *refs):
        outs = refs
        token, tiles_ref, lhs, sems = outs[-4:]
        token[...] = jnp.zeros_like(token)
        load = pltpu.make_async_copy(tiles_hbm, tiles_ref, sems.at[0])
        load.start()
        load.wait()
        for first, count, spans in jobs:
            height = blocks * sum(rows for _, rows in spans)

            def one_owner(i, carry):
                lay_tiles(table_ref, (first + i) * blocks * blocks, tiles_ref, lhs, spans, 0, blocks, block)
                total = jnp.dot(lhs[pl.ds(0, height)], x_ref[...], preferred_element_type=jnp.float32)
                total = total.astype(jnp.bfloat16)
                at = 0
                for out, (_, rows) in zip(outs, spans):
                    out[i] = total[at : at + blocks * rows].reshape(blocks, rows, width)
                    at += blocks * rows
                return carry

            lax.fori_loop(0, count, one_owner, 0)
            outs = outs[len(spans) :]

    results = call(
        body,
        shapes + [TOKEN],
        [SMEM, HBM, VMEM],
        [VMEM] * (len(shapes) + 1),
        (table, tiles, inputs),
        [
            pltpu.VMEM(tiles.shape, jnp.bfloat16),
            pltpu.VMEM((most, blocks * block), jnp.bfloat16),
            pltpu.SemaphoreType.DMA((1,)),
        ],
    )
    grouped, at = [], 0
    for _, _, spans in jobs:
        grouped.append(results[at : at + len(spans)])
        at += len(spans)
    return (*grouped, results[-1])


def combine(token, total, got, at_hand):
    count, *shape = total.shape
    left = count // 2

    def body(token_ref, total_ref, got_ref, at_hand_ref, *outs):
        def add(i, carry):
            value = total_ref[i].astype(jnp.float32) + got_ref[i].astype(jnp.float32)
            if not left:
                outs[0][...] = value.astype(jnp.bfloat16)
            else:

                @pl.when(i < left)
                def _():
                    outs[0][jnp.minimum(i, left - 1)] = value

                @pl.when(i >= left)
                def _():
                    outs[1][jnp.maximum(i - left, 0)] = value.astype(jnp.bfloat16)

            return carry

        lax.fori_loop(0, count, add, 0)
        outs[-1][...] = token_ref[...]

    if left:
        out_shape = [
            jax.ShapeDtypeStruct((left, *shape), jnp.float32),
            jax.ShapeDtypeStruct((count - left, *shape), jnp.bfloat16),
        ]
    else:
        out_shape = [jax.ShapeDtypeStruct(tuple(shape), jnp.bfloat16)]
    out_shape.append(TOKEN)
    return call(body, out_shape, [VMEM] * 4, [VMEM] * len(out_shape), (token, total, got, at_hand))


def join(token, held, got):
    def body(token_ref, held_ref, got_ref, out, token_out):
        out[pl.ds(0, held.shape[0])] = held_ref[...]
        out[pl.ds(held.shape[0], got.shape[0])] = got_ref[...]
        token_out[...] = token_ref[...]

    both = jax.ShapeDtypeStruct((held.shape[0] + got.shape[0], *held.shape[1:]), held.dtype)
    return call(body, [both, TOKEN], [VMEM] * 3, [VMEM] * 2, (token, held, got))


def mix(token, mine, offsets, held, got, weight):
    _, blocks, rows, depth = held.shape
    width = weight.shape[1]

    def body(token_ref, mine_ref, held_ref, got_ref, w_ref, out_ref, token_out):
        total = jnp.zeros((blocks * rows, width), jnp.float32)
        for n, offset in enumerate(offsets):
            piece = (held_ref if n < held.shape[0] else got_ref)[n % held.shape[0]]
            at = pl.multiple_of((mine_ref[0] ^ offset) * depth, depth)
            total += jnp.dot(
                piece.reshape(blocks * rows, depth), w_ref[pl.ds(at, depth)], preferred_element_type=jnp.float32
            )
        out_ref[0] = jnp.maximum(total, 0.0).astype(jnp.bfloat16).reshape(blocks, rows, width)
        token_out[...] = token_ref[...]

    return call(
        body,
        [jax.ShapeDtypeStruct((1, blocks, rows, width), jnp.bfloat16), TOKEN],
        [VMEM, SMEM, VMEM, VMEM, VMEM],
        [VMEM] * 2,
        (token, mine, held, got, weight),
    )


def pick(token, choice, held, got):
    count = 2 * held.shape[0] * READ_CAP

    def body(token_ref, choice_ref, held_ref, got_ref, out, token_out):
        for i in range(count):
            n = i // READ_CAP
            source = held_ref if n < held.shape[0] else got_ref
            out[i] = source[n % held.shape[0], choice_ref[i]]
        token_out[...] = token_ref[...]

    return call(
        body,
        [jax.ShapeDtypeStruct((count, *held.shape[2:]), held.dtype), TOKEN],
        [VMEM, SMEM, VMEM, VMEM],
        [VMEM] * 2,
        (token, choice, held, got),
    )


def lay_out(token, me, readers, entry, offsets, held, got, far, outputs, span, block):
    count = readers.shape[0]
    _, blocks, _, width = held.shape
    start, rows = span
    slots = 2 * len(offsets) * READ_CAP

    def body(token_ref, me_ref, readers_ref, entry_ref, held_ref, got_ref, far_ref, *refs):
        hidden_ref, ghost_ref, token_out, sems = refs[-4:]
        own = pltpu.make_async_copy(held_ref.at[0], hidden_ref.at[:, pl.ds(start, rows)], sems.at[slots])
        own.start()

        def each(act):
            for n, offset in enumerate(offsets):
                for j in range(READ_CAP):
                    i = n * READ_CAP + j
                    listed = entry_ref[(me_ref[0] ^ offset) * READ_CAP + j]
                    source = held_ref if n < held.shape[0] else got_ref

                    @pl.when(listed >= 0)
                    def _():
                        _, b = split(readers_ref[listed], blocks)
                        target = ghost_ref.at[listed, pl.ds(start, rows)]
                        act(pltpu.make_async_copy(source.at[n % held.shape[0], b], target, sems.at[i]))

                    across = entry_ref[(me_ref[0] ^ 1 ^ offset) * READ_CAP + j]

                    @pl.when(across >= 0)
                    def _():
                        target = ghost_ref.at[across, pl.ds(start, rows)]
                        act(pltpu.make_async_copy(far_ref.at[i], target, sems.at[slots // 2 + i]))

        each(lambda copy: copy.start())
        token_out[...] = token_ref[...]
        own.wait()
        each(lambda copy: copy.wait())

    operands = (token, me, readers, entry, held, got, far, *outputs)
    return call(
        body,
        [
            jax.ShapeDtypeStruct((blocks, block, width), jnp.bfloat16),
            jax.ShapeDtypeStruct((count, block, width), jnp.bfloat16),
            TOKEN,
        ],
        [VMEM] + [SMEM] * 3 + [VMEM] * 3 + [HBM] * len(outputs),
        [HBM, HBM, VMEM],
        operands,
        [pltpu.SemaphoreType.DMA((slots + 1,))],
        aliases={len(operands) - 2: 0, len(operands) - 1: 1} if outputs else None,
    )


def local(features, tiles, tile_slot, tile_col, tile_id, touched, weight, readers):
    edges, feats = lax.axis_size("edge"), lax.axis_size("feat")
    half = edges // 2
    me, mine = lax.axis_index("edge"), lax.axis_index("feat")
    block = tiles.shape[1]
    blocks = features.shape[0] // block
    width = features.shape[1]
    unit = block // sum(SHARES)
    spans = [(sum(SHARES[:i]) * unit, share * unit) for i, share in enumerate(SHARES)]

    def flip(value, bit, axis="edge"):
        return lax.ppermute(value, axis, [(d, d ^ bit) for d in range(lax.axis_size(axis))])

    columns = offsets_of(edges, 2)
    me, mine = me.reshape(1), mine.reshape(1)
    neighbour = flip(readers, 1)
    table, choice, entry, early, inputs = first_part(
        me, tile_slot, tile_col, tile_id, touched, tiles, features, readers, neighbour, half, half, spans[0]
    )
    later, first_kept, _ = other_parts(table, tiles, inputs, [(half, half, spans[1:]), (0, half, spans[:1])])
    away = [early, *later]
    kept, token = other_parts(table, tiles, inputs, [(0, half, spans[1:])])
    kept = [*first_kept, *kept]
    outputs = ()

    def chained(function, *operands):
        nonlocal token
        *results, token = function(token, *operands)
        return results

    def spread(held, size, lowest, axis):
        bit = size // 2
        while True:
            got = flip(held, bit, axis)
            yield
            if bit == lowest:
                return held, got
            (held,) = chained(join, held, got)
            bit //= 2

    def one_part(part):
        nonlocal outputs
        got = flip(away[part], 1)
        yield
        total, sent = chained(combine, kept[part], got, weight)
        bit = 2
        while bit < edges:
            got = flip(sent, bit)
            yield
            total, *sent = chained(combine, total, got, weight)
            sent = sent[0] if sent else None
            bit *= 2
        held, got = yield from spread(total[None], feats, 1, "feat")
        (mixed,) = chained(mix, mine, offsets_of(feats, 1), held, got, weight)
        held, got = yield from spread(mixed, edges, 2, "edge")
        (picked,) = chained(pick, choice, held, got)
        far = flip(picked, 1)
        yield
        outputs = chained(lay_out, me, readers, entry, columns, held, got, far, outputs, spans[part], block)

    def links_of(bit):
        return {"end": 1.0} if bit == 2 else {"end": 1.0, "middle": 2.0}

    column_bits = [1 << i for i in range(1, edges.bit_length() - 1)]
    feat_bits = [1 << i for i in reversed(range(feats.bit_length() - 1))]
    ways = []
    for _, rows in spans:
        share = rows / block
        way = [({"x": 1.0}, share * half * 1.15)]
        way += [(links_of(bit), share * half / bit) for bit in column_bits]
        way += [({"chip" if bit == 1 else "feat": 1.0}, share * (1.0 if bit > 1 else 0.3)) for bit in feat_bits]
        way += [(links_of(bit), share * half / bit) for bit in reversed(column_bits)]
        ways.append(way + [({"x": 1.0}, share * READ_CAP / blocks * half)])
    steps = [one_part(part) for part in range(len(spans))]
    for step in steps:
        next(step)
    known = all(ORDER.count(part) == len(way) for part, way in enumerate(ways))
    for part in ORDER if known else planned_order(ways):
        next(steps[part], None)
    hidden, ghosts = outputs
    return hidden.reshape(blocks * block, width), ghosts.reshape(-1, width)


def solution(mesh):
    in_specs = (
        P("edge", "feat"),
        P("edge", None, None),
        P("edge"),
        P("edge"),
        P("edge"),
        P(),
        P(None, "feat"),
        P("edge"),
    )
    out_specs = (P("edge", "feat"), P("edge", "feat"))
    return jax.shard_map(local, mesh=mesh, in_specs=in_specs, out_specs=out_specs, check_vma=False)
```

```python
import jax
import jax.numpy as jnp
from jax import lax
from jax.experimental import pallas as pl
from jax.experimental.pallas import tpu as pltpu
from jax.sharding import PartitionSpec as P

SHARES = (2, 2, 2, 1, 1)
ORDER = (
    1, 0, 1, 2, 0, 2, 1, 3, 0, 2, 0, 3, 4, 1, 0, 1, 3, 4, 4, 0, 3, 2, 2, 1, 4, 0, 4, 4, 2, 1, 0, 3,
    2, 3, 1, 4, 3, 4, 2, 3,
)
READ_CAP = 2
VMEM_BYTES = 12 * 1024 * 1024
UNIT_TIME, START_TIME, STEP_TIME, LATENCY = 11.3, 0.9, 0.4, 0.6

SMEM = pl.BlockSpec(memory_space=pltpu.SMEM)
VMEM = pl.BlockSpec(memory_space=pltpu.VMEM)
HBM = pl.BlockSpec(memory_space=pltpu.HBM)
TOKEN = jax.ShapeDtypeStruct((8, 128), jnp.float32)


def call(body, out_shape, in_specs, out_specs, operands, scratch=(), aliases=None, limit=VMEM_BYTES):
    return pl.pallas_call(
        body,
        out_shape=out_shape,
        in_specs=in_specs,
        out_specs=out_specs,
        scratch_shapes=list(scratch),
        input_output_aliases=aliases or {},
        compiler_params=pltpu.CompilerParams(vmem_limit_bytes=limit),
        cost_estimate=pl.CostEstimate(flops=0, bytes_accessed=1, transcendentals=0),
    )(*operands)


def split(value, size):
    if size & (size - 1) == 0:
        return value >> (size.bit_length() - 1), value & (size - 1)
    return lax.div(value, size), lax.rem(value, size)


def place_of(peer, bits):
    place = 0
    for bit in bits:
        place = (place << 1) | ((peer >> (bit.bit_length() - 1)) & 1)
    return place


def planned_order(ways):
    now, order, flows, current, place = 0.0, [], [], {}, [0] * len(ways)

    def active():
        waiting = [f for f in flows if "x" in f["links"]][1:]
        running = [f for f in flows if not any(f is w for w in waiting)]
        load = {}
        for f in running:
            for link, weight in f["links"].items():
                load[link] = load.get(link, 0.0) + weight
        return [(f, min(1.0 / load[link] for link in f["links"])) for f in running]

    def advance(until):
        nonlocal now
        while now < until:
            running = active()
            step = min([until - now] + [f["left"] / rate for f, rate in running])
            now += max(step, 1e-3)
            for f, rate in running:
                f["left"] -= step * rate
                if f["left"] <= 1e-6:
                    f["end"] = now + LATENCY
            flows[:] = [f for f in flows if f["left"] > 1e-6]

    def begin(n):
        links, units = ways[n][place[n]]
        advance(now + START_TIME)
        current[n] = {"links": links, "left": units * UNIT_TIME, "end": None}
        flows.append(current[n])

    for n in range(len(ways)):
        begin(n)
    while current:
        ended = [(f["end"], n) for n, f in current.items() if f["end"] is not None and f["end"] <= now]
        if not ended:
            advance(now + 0.05)
            continue
        _, n = min(ended)
        order.append(n)
        del current[n]
        place[n] += 1
        advance(now + STEP_TIME)
        if place[n] < len(ways[n]):
            begin(n)
    return order


def offsets_of(size, lowest):
    offsets, bit = [0], size // 2
    while bit >= lowest:
        offsets += [offset | bit for offset in offsets]
        bit //= 2
    return offsets


def lay_tiles(table, base, tiles, lhs, spans, row_base, blocks, block, at=0):
    for b in range(blocks):
        for c in range(blocks):
            entry = table[base + b * blocks + c]
            tile = tiles[jnp.maximum(entry - 1, 0)]
            tile = jnp.where(entry > 0, tile, jnp.zeros_like(tile))
            top = at
            for first, rows in spans:
                lhs[pl.ds(top + b * rows, rows), pl.ds(c * block, block)] = tile[first - row_base : first - row_base + rows]
                top = top + blocks * rows


def first_part(me, slot, col, tile_id, touched, tiles, features, readers, neighbour, orders, first, count, spans):
    block = tiles.shape[1]
    blocks = features.shape[0] // block
    width = features.shape[1]
    edges, cap = touched.shape[1], touched.shape[2]
    column_bits = [1 << i for i in range(1, edges.bit_length() - 1)]
    products = slot.shape[0]
    half = edges // 2
    loaded = sum(rows for _, rows in spans)
    tallest = max(rows for _, rows in spans)
    square = blocks * blocks

    listed = readers.shape[0]

    def body(me_ref, slot_hbm, col_hbm, id_hbm, touched_ref, tiles_hbm, x_hbm, readers_ref, neighbour_ref, *refs):
        table, choice, entry, *outs = refs[: 3 + len(spans)]
        x_out, *scratch = refs[3 + len(spans) :]
        slot_ref, col_ref, id_ref, tiles_ref, lhs, bases, seen, sems = scratch
        loads = [
            pltpu.make_async_copy(slot_hbm, slot_ref, sems.at[0]),
            pltpu.make_async_copy(col_hbm, col_ref, sems.at[1]),
            pltpu.make_async_copy(id_hbm, id_ref, sems.at[2]),
            pltpu.make_async_copy(x_hbm, x_out, sems.at[3]),
            pltpu.make_async_copy(tiles_hbm.at[:, pl.ds(0, loaded)], tiles_ref, sems.at[4]),
        ]
        for load in loads:
            load.start()

        def clear(i, carry):
            table[i] = 0
            return carry

        lax.fori_loop(0, len(orders) * edges * square, clear, 0, unroll=16)

        def place_slot(k, carry):
            owner, _ = split(k, cap)
            for n, order in enumerate(orders):
                place = place_of(owner ^ me_ref[0], order)
                bases[n * edges * cap + k] = ((n * edges + place) * blocks + touched_ref[k]) * blocks
            return carry

        lax.fori_loop(0, edges * cap, place_slot, 0, unroll=8)
        for load in loads[:3]:
            load.wait()

        for i in range(half * READ_CAP + 1):
            choice[i] = 0
        for i in range(edges * READ_CAP):
            entry[i] = -1
        for i in range(2 * edges):
            seen[i] = 0

        def enter_lists(r, carry):
            owner, _ = split(readers_ref[r], blocks)
            turn = seen[owner]
            seen[owner] = turn + 1
            entry[owner * READ_CAP + jnp.minimum(turn, READ_CAP - 1)] = r
            owner, b = split(neighbour_ref[r], blocks)
            turn = seen[edges + owner]
            seen[edges + owner] = turn + 1
            peer = owner ^ me_ref[0]
            row = place_of(peer, column_bits) * READ_CAP + jnp.minimum(turn, READ_CAP - 1)
            choice[jnp.where(peer & 1 == 0, row, half * READ_CAP)] = b
            return carry

        lax.fori_loop(0, listed, enter_lists, 0)

        def enter(k, carry):
            for n in range(len(orders)):
                table[bases[n * edges * cap + slot_ref[k]] + col_ref[k]] = id_ref[k] + 1
            return carry

        lax.fori_loop(0, products, enter, 0, unroll=8)
        for load in loads[3:]:
            load.wait()

        for n, (span, out) in enumerate(zip(spans, outs)):
            height = blocks * span[1]

            def one_owner(i, carry):
                at = pl.multiple_of(i * height, height)
                base = (n * edges + first + i) * square
                lay_tiles(table, base, tiles_ref, lhs, [span], 0, blocks, block, at)
                return carry

            lax.fori_loop(0, count, one_owner, 0)
            total = jnp.dot(lhs[pl.ds(0, count * height)], x_out[...], preferred_element_type=jnp.float32)
            out[...] = total.astype(jnp.bfloat16).reshape(out.shape)

    return call(
        body,
        [
            jax.ShapeDtypeStruct((len(orders) * edges * square,), jnp.int32),
            jax.ShapeDtypeStruct((half * READ_CAP + 1,), jnp.int32),
            jax.ShapeDtypeStruct((edges * READ_CAP,), jnp.int32),
            *[jax.ShapeDtypeStruct((count, blocks, rows, width), jnp.bfloat16) for _, rows in spans],
            jax.ShapeDtypeStruct(features.shape, jnp.bfloat16),
        ],
        [SMEM, HBM, HBM, HBM, SMEM, HBM, HBM, SMEM, SMEM],
        [SMEM] * 3 + [VMEM] * (len(spans) + 1),
        (me, slot, col, tile_id, touched[me[0]].reshape(-1), tiles, features, readers, neighbour),
        [
            pltpu.SMEM((products,), jnp.int32),
            pltpu.SMEM((products,), jnp.int32),
            pltpu.SMEM((products,), jnp.int32),
            pltpu.VMEM((tiles.shape[0], loaded, block), jnp.bfloat16),
            pltpu.VMEM((count * blocks * tallest, blocks * block), jnp.bfloat16),
            pltpu.SMEM((len(orders) * edges * cap,), jnp.int32),
            pltpu.SMEM((2 * edges,), jnp.int32),
            pltpu.SemaphoreType.DMA((5,)),
        ],
        limit=62 * 1024 * 1024,
    )


def other_parts(table, tiles, inputs, jobs):
    block = tiles.shape[1]
    blocks = inputs.shape[0] // block
    width = inputs.shape[1]
    most = max(sum(rows for _, rows in spans) for _, _, spans in jobs) * blocks
    shapes = [
        jax.ShapeDtypeStruct((count, blocks, rows, width), jnp.bfloat16) for _, count, spans in jobs for _, rows in spans
    ]

    def body(table_ref, tiles_hbm, x_ref, *refs):
        outs = refs
        token, tiles_ref, lhs, sems = outs[-4:]
        token[...] = jnp.zeros_like(token)
        load = pltpu.make_async_copy(tiles_hbm, tiles_ref, sems.at[0])
        load.start()
        load.wait()
        for first, count, spans in jobs:
            height = blocks * sum(rows for _, rows in spans)

            def one_owner(i, carry):
                lay_tiles(table_ref, (first + i) * blocks * blocks, tiles_ref, lhs, spans, 0, blocks, block)
                total = jnp.dot(lhs[pl.ds(0, height)], x_ref[...], preferred_element_type=jnp.float32)
                total = total.astype(jnp.bfloat16)
                at = 0
                for out, (_, rows) in zip(outs, spans):
                    out[i] = total[at : at + blocks * rows].reshape(blocks, rows, width)
                    at += blocks * rows
                return carry

            lax.fori_loop(0, count, one_owner, 0)
            outs = outs[len(spans) :]

    results = call(
        body,
        shapes + [TOKEN],
        [SMEM, HBM, VMEM],
        [VMEM] * (len(shapes) + 1),
        (table, tiles, inputs),
        [
            pltpu.VMEM(tiles.shape, jnp.bfloat16),
            pltpu.VMEM((most, blocks * block), jnp.bfloat16),
            pltpu.SemaphoreType.DMA((1,)),
        ],
    )
    grouped, at = [], 0
    for _, _, spans in jobs:
        grouped.append(results[at : at + len(spans)])
        at += len(spans)
    return (*grouped, results[-1])


def combine(token, total, got, at_hand):
    count, *shape = total.shape
    left = count // 2

    def body(token_ref, total_ref, got_ref, at_hand_ref, *outs):
        def add(i, carry):
            value = total_ref[i].astype(jnp.float32) + got_ref[i].astype(jnp.float32)
            if not left:
                outs[0][...] = value.astype(jnp.bfloat16)
            else:

                @pl.when(i < left)
                def _():
                    outs[0][jnp.minimum(i, left - 1)] = value

                @pl.when(i >= left)
                def _():
                    outs[1][jnp.maximum(i - left, 0)] = value.astype(jnp.bfloat16)

            return carry

        lax.fori_loop(0, count, add, 0)
        outs[-1][...] = token_ref[...]

    if left:
        out_shape = [
            jax.ShapeDtypeStruct((left, *shape), jnp.float32),
            jax.ShapeDtypeStruct((count - left, *shape), jnp.bfloat16),
        ]
    else:
        out_shape = [jax.ShapeDtypeStruct(tuple(shape), jnp.bfloat16)]
    out_shape.append(TOKEN)
    return call(body, out_shape, [VMEM] * 4, [VMEM] * len(out_shape), (token, total, got, at_hand))


def join(token, held, got):
    def body(token_ref, held_ref, got_ref, out, token_out):
        out[pl.ds(0, held.shape[0])] = held_ref[...]
        out[pl.ds(held.shape[0], got.shape[0])] = got_ref[...]
        token_out[...] = token_ref[...]

    both = jax.ShapeDtypeStruct((held.shape[0] + got.shape[0], *held.shape[1:]), held.dtype)
    return call(body, [both, TOKEN], [VMEM] * 3, [VMEM] * 2, (token, held, got))


def mix(token, mine, offsets, held, got, weight):
    _, blocks, rows, depth = held.shape
    width = weight.shape[1]

    def body(token_ref, mine_ref, held_ref, got_ref, w_ref, out_ref, token_out):
        total = jnp.zeros((blocks * rows, width), jnp.float32)
        for n, offset in enumerate(offsets):
            piece = (held_ref if n < held.shape[0] else got_ref)[n % held.shape[0]]
            at = pl.multiple_of((mine_ref[0] ^ offset) * depth, depth)
            total += jnp.dot(
                piece.reshape(blocks * rows, depth), w_ref[pl.ds(at, depth)], preferred_element_type=jnp.float32
            )
        out_ref[0] = jnp.maximum(total, 0.0).astype(jnp.bfloat16).reshape(blocks, rows, width)
        token_out[...] = token_ref[...]

    return call(
        body,
        [jax.ShapeDtypeStruct((1, blocks, rows, width), jnp.bfloat16), TOKEN],
        [VMEM, SMEM, VMEM, VMEM, VMEM],
        [VMEM] * 2,
        (token, mine, held, got, weight),
    )


def pick(token, choice, held, got):
    count = 2 * held.shape[0] * READ_CAP

    def body(token_ref, choice_ref, held_ref, got_ref, out, token_out):
        for i in range(count):
            n = i // READ_CAP
            source = held_ref if n < held.shape[0] else got_ref
            out[i] = source[n % held.shape[0], choice_ref[i]]
        token_out[...] = token_ref[...]

    return call(
        body,
        [jax.ShapeDtypeStruct((count, *held.shape[2:]), held.dtype), TOKEN],
        [VMEM, SMEM, VMEM, VMEM],
        [VMEM] * 2,
        (token, choice, held, got),
    )


def touch(token, value):
    def body(token_ref, value_ref, token_out):
        token_out[...] = token_ref[...]

    return call(body, [TOKEN], [VMEM] * 2, [VMEM], (token, value))


def lay_out(token, me, readers, entry, offsets, items, outputs, block):
    count = readers.shape[0]
    half_held, blocks, _, width = items[0][0].shape
    slots = len(offsets) * READ_CAP
    arrays = [array for item in items for array in item[:3]]

    def body(token_ref, me_ref, readers_ref, entry_ref, *refs):
        hidden_ref, ghost_ref, token_out, sems = refs[-4:]

        def each(act):
            for number, item in enumerate(items):
                held_ref, got_ref, far_ref = refs[3 * number : 3 * number + 3]
                rows = pl.ds(*item[3])
                act(pltpu.make_async_copy(held_ref.at[0], hidden_ref.at[:, rows], sems.at[number, 2 * slots]))
                for i in range(slots):
                    n, j = i // READ_CAP, i % READ_CAP
                    near = entry_ref[(me_ref[0] ^ offsets[n]) * READ_CAP + j]
                    source = held_ref if n < half_held else got_ref

                    @pl.when(near >= 0)
                    def _():
                        _, b = split(readers_ref[near], blocks)
                        target = ghost_ref.at[near, rows]
                        act(pltpu.make_async_copy(source.at[n % half_held, b], target, sems.at[number, i]))

                    across = entry_ref[(me_ref[0] ^ 1 ^ offsets[n]) * READ_CAP + j]

                    @pl.when(across >= 0)
                    def _():
                        target = ghost_ref.at[across, rows]
                        act(pltpu.make_async_copy(far_ref.at[i], target, sems.at[number, slots + i]))

        each(lambda copy: copy.start())
        token_out[...] = token_ref[...]
        each(lambda copy: copy.wait())

    operands = (token, me, readers, entry, *arrays, *outputs)
    return call(
        body,
        [
            jax.ShapeDtypeStruct((blocks, block, width), jnp.bfloat16),
            jax.ShapeDtypeStruct((count, block, width), jnp.bfloat16),
            TOKEN,
        ],
        [VMEM] + [SMEM] * 3 + [VMEM] * len(arrays) + [HBM] * len(outputs),
        [HBM, HBM, VMEM],
        operands,
        [pltpu.SemaphoreType.DMA((len(items), 2 * slots + 1))],
        aliases={len(operands) - 2: 0, len(operands) - 1: 1} if outputs else None,
    )


def local(features, tiles, tile_slot, tile_col, tile_id, touched, weight, readers):
    edges, feats = lax.axis_size("edge"), lax.axis_size("feat")
    half = edges // 2
    me, mine = lax.axis_index("edge"), lax.axis_index("feat")
    block = tiles.shape[1]
    blocks = features.shape[0] // block
    width = features.shape[1]
    unit = block // sum(SHARES)
    spans = [(sum(SHARES[:i]) * unit, share * unit) for i, share in enumerate(SHARES)]

    def flip(value, bit, axis="edge"):
        return lax.ppermute(value, axis, [(d, d ^ bit) for d in range(lax.axis_size(axis))])

    columns = offsets_of(edges, 2)
    me, mine = me.reshape(1), mine.reshape(1)
    neighbour = flip(readers, 1)
    column_bits = [1 << i for i in range(1, edges.bit_length() - 1)]
    orders = [[*column_bits, 1], [1, *column_bits]]
    table, choice, entry, *early, inputs = first_part(
        me, tile_slot, tile_col, tile_id, touched, tiles, features, readers, neighbour, orders, half, half, spans[:2]
    )
    later, first_kept, _ = other_parts(
        table, tiles, inputs, [(edges + half, half, spans[2:]), (0, half, spans[:1])]
    )
    away = [*early, *later]
    kept, token = other_parts(table, tiles, inputs, [(edges, half, spans[1:])])
    kept = [*first_kept, *kept]

    def chained(function, *operands):
        nonlocal token
        *results, token = function(token, *operands)
        return results

    def spread(held, size, lowest, axis):
        bit = size // 2
        while True:
            got = flip(held, bit, axis)
            yield
            if bit == lowest:
                return held, got
            (held,) = chained(join, held, got)
            bit //= 2

    def one_part(part):
        first, *rest = orders[min(part, 1)]
        got = flip(away[part], first)
        yield
        total, sent = chained(combine, kept[part], got, weight)
        for bit in rest:
            got = flip(sent, bit)
            yield
            total, *sent = chained(combine, total, got, weight)
            sent = sent[0] if sent else None
        held, got = yield from spread(total[None], feats, 1, "feat")
        (mixed,) = chained(mix, mine, offsets_of(feats, 1), held, got, weight)
        held, got = yield from spread(mixed, edges, 2, "edge")
        (picked,) = chained(pick, choice, held, got)
        far = flip(picked, 1)
        yield
        return held, got, far, spans[part]

    def links_of(bit):
        return {"x": 1.0} if bit == 1 else {"end": 1.0} if bit == 2 else {"end": 1.0, "middle": 2.0}

    feat_bits = [1 << i for i in reversed(range(feats.bit_length() - 1))]
    ways = []
    for part, (_, rows) in enumerate(spans):
        share = rows / block
        way = [(links_of(bit), share * half / (1 << n)) for n, bit in enumerate(orders[min(part, 1)])]
        way += [({"chip" if bit == 1 else "feat": 1.0}, share * (1.0 if bit > 1 else 0.3)) for bit in feat_bits]
        way += [(links_of(bit), share * half / bit) for bit in reversed(column_bits)]
        ways.append(way + [({"x": 1.0}, share * READ_CAP / blocks * half)])
    steps = [one_part(part) for part in range(len(spans))]
    for step in steps:
        next(step)
    known = sorted(ORDER) == [part for part, way in enumerate(ways) for _ in way]
    *order, last = ORDER if known else planned_order(ways)
    ended = []
    for part in order:
        try:
            next(steps[part])
        except StopIteration as end:
            ended.append(end.value)
            chained(touch, end.value[2])
    outputs = chained(lay_out, me, readers, entry, columns, ended, (), block)
    try:
        next(steps[last])
    except StopIteration as end:
        outputs = chained(lay_out, me, readers, entry, columns, [end.value], outputs, block)
    hidden, ghosts = outputs
    return hidden.reshape(blocks * block, width), ghosts.reshape(-1, width)


def solution(mesh):
    in_specs = (
        P("edge", "feat"),
        P("edge", None, None),
        P("edge"),
        P("edge"),
        P("edge"),
        P(),
        P(None, "feat"),
        P("edge"),
    )
    out_specs = (P("edge", "feat"), P("edge", "feat"))
    return jax.shard_map(local, mesh=mesh, in_specs=in_specs, out_specs=out_specs, check_vma=False)
```

```python
import jax
import jax.numpy as jnp
from jax import lax
from jax.experimental import pallas as pl
from jax.experimental.pallas import tpu as pltpu
from jax.sharding import PartitionSpec as P

SHARES = (2, 2, 1, 2, 1)
ORDER = (
    1, 0, 3, 1, 4, 0, 1, 2, 3, 0, 2, 3, 1, 2, 4, 0, 0, 4, 2, 1, 4, 0, 3, 3, 1, 4, 2, 0, 3, 1, 4, 0,
    3, 4, 2, 4, 1, 2, 3, 2,
)
READ_CAP = 2
VMEM_BYTES = 12 * 1024 * 1024
UNIT_TIME, START_TIME, STEP_TIME, LATENCY = 11.3, 0.9, 0.4, 0.6

SMEM = pl.BlockSpec(memory_space=pltpu.SMEM)
VMEM = pl.BlockSpec(memory_space=pltpu.VMEM)
HBM = pl.BlockSpec(memory_space=pltpu.HBM)
TOKEN = jax.ShapeDtypeStruct((8, 128), jnp.float32)


def call(body, out_shape, in_specs, out_specs, operands, scratch=(), aliases=None, limit=VMEM_BYTES):
    return pl.pallas_call(
        body,
        out_shape=out_shape,
        in_specs=in_specs,
        out_specs=out_specs,
        scratch_shapes=list(scratch),
        input_output_aliases=aliases or {},
        compiler_params=pltpu.CompilerParams(vmem_limit_bytes=limit),
        cost_estimate=pl.CostEstimate(flops=0, bytes_accessed=1, transcendentals=0),
    )(*operands)


def split(value, size):
    if size & (size - 1) == 0:
        return value >> (size.bit_length() - 1), value & (size - 1)
    return lax.div(value, size), lax.rem(value, size)


def place_of(peer, bits):
    place = 0
    for bit in bits:
        place = (place << 1) | ((peer >> (bit.bit_length() - 1)) & 1)
    return place


def planned_order(ways):
    now, order, flows, current, place = 0.0, [], [], {}, [0] * len(ways)

    def active():
        waiting = [f for f in flows if "x" in f["links"]][1:]
        running = [f for f in flows if not any(f is w for w in waiting)]
        load = {}
        for f in running:
            for link, weight in f["links"].items():
                load[link] = load.get(link, 0.0) + weight
        return [(f, min(1.0 / load[link] for link in f["links"])) for f in running]

    def advance(until):
        nonlocal now
        while now < until:
            running = active()
            step = min([until - now] + [f["left"] / rate for f, rate in running])
            now += max(step, 1e-3)
            for f, rate in running:
                f["left"] -= step * rate
                if f["left"] <= 1e-6:
                    f["end"] = now + LATENCY
            flows[:] = [f for f in flows if f["left"] > 1e-6]

    def begin(n):
        links, units = ways[n][place[n]]
        advance(now + START_TIME)
        current[n] = {"links": links, "left": units * UNIT_TIME, "end": None}
        flows.append(current[n])

    for n in range(len(ways)):
        begin(n)
    while current:
        ended = [(f["end"], n) for n, f in current.items() if f["end"] is not None and f["end"] <= now]
        if not ended:
            advance(now + 0.05)
            continue
        _, n = min(ended)
        order.append(n)
        del current[n]
        place[n] += 1
        advance(now + STEP_TIME)
        if place[n] < len(ways[n]):
            begin(n)
    return order


def offsets_of(size, lowest):
    offsets, bit = [0], size // 2
    while bit >= lowest:
        offsets += [offset | bit for offset in offsets]
        bit //= 2
    return offsets


def lay_tiles(table, base, tiles, lhs, spans, row_base, blocks, block, at=0):
    for b in range(blocks):
        for c in range(blocks):
            entry = table[base + b * blocks + c]
            tile = tiles[jnp.maximum(entry - 1, 0)]
            tile = jnp.where(entry > 0, tile, jnp.zeros_like(tile))
            top = at
            for first, rows in spans:
                lhs[pl.ds(top + b * rows, rows), pl.ds(c * block, block)] = tile[first - row_base : first - row_base + rows]
                top = top + blocks * rows


def first_part(me, slot, col, tile_id, touched, tiles, features, readers, orders, first, count, spans):
    block = tiles.shape[1]
    blocks = features.shape[0] // block
    width = features.shape[1]
    edges, cap = touched.shape[1], touched.shape[2]
    column_bits = [1 << i for i in range(1, edges.bit_length() - 1)]
    products = slot.shape[0]
    half = edges // 2
    loaded = sum(rows for _, rows in spans)
    tallest = max(rows for _, rows in spans)
    square = blocks * blocks

    listed = readers.shape[0]
    extra = -(-half * READ_CAP // 16) * 16
    shapes = [(count, blocks, rows, width) for _, rows in spans]
    shapes[1] = (count * blocks * spans[1][1] + extra, width)

    def body(me_ref, slot_hbm, col_hbm, id_hbm, touched_hbm, readers_hbm, tiles_hbm, x_hbm, *refs):
        table, entry, *outs = refs[: 2 + len(spans)]
        x_out, *scratch = refs[2 + len(spans) :]
        slot_ref, col_ref, id_ref, touched_ref, readers_ref, choice, tiles_ref, lhs, bases, seen, sems = scratch
        loads = [
            pltpu.make_async_copy(slot_hbm, slot_ref, sems.at[0]),
            pltpu.make_async_copy(col_hbm, col_ref, sems.at[1]),
            pltpu.make_async_copy(id_hbm, id_ref, sems.at[2]),
            pltpu.make_async_copy(touched_hbm.at[me_ref[0]], touched_ref, sems.at[5]),
            pltpu.make_async_copy(readers_hbm, readers_ref, sems.at[6]),
            pltpu.make_async_copy(x_hbm, x_out, sems.at[3]),
            pltpu.make_async_copy(tiles_hbm.at[:, pl.ds(0, loaded)], tiles_ref, sems.at[4]),
        ]
        for load in loads:
            load.start()

        def clear(i, carry):
            table[i] = 0
            return carry

        lax.fori_loop(0, len(orders) * edges * square, clear, 0, unroll=16)

        def place_slot(k, carry):
            owner, slot_at = split(k, cap)
            for n, order in enumerate(orders):
                place = place_of(owner ^ me_ref[0], order)
                bases[n * edges * cap + k] = ((n * edges + place) * blocks + touched_ref[slot_at, owner]) * blocks
            return carry

        for load in loads[:5]:
            load.wait()
        lax.fori_loop(0, edges * cap, place_slot, 0, unroll=8)

        for i in range(extra + 1):
            choice[i] = 0
        for i in range(edges * READ_CAP):
            entry[i] = -1
        for i in range(edges):
            seen[i] = 0

        def enter_lists(r, carry):
            owner, b = split(readers_ref[r], blocks)
            turn = seen[owner]
            seen[owner] = turn + 1
            turn = jnp.minimum(turn, READ_CAP - 1)
            entry[owner * READ_CAP + turn] = r
            peer = owner ^ me_ref[0] ^ 1
            row = place_of(peer, column_bits) * READ_CAP + turn
            choice[jnp.where(peer & 1 == 0, row, extra)] = b
            return carry

        lax.fori_loop(0, listed, enter_lists, 0)

        def enter(k, carry):
            for n in range(len(orders)):
                table[bases[n * edges * cap + slot_ref[k]] + col_ref[k]] = id_ref[k] + 1
            return carry

        lax.fori_loop(0, products, enter, 0, unroll=8)
        for load in loads[5:]:
            load.wait()

        for n, (span, out) in enumerate(zip(spans, outs)):
            height = blocks * span[1]

            def one_owner(i, carry):
                at = pl.multiple_of(i * height, height)
                base = (n * edges + first + i) * square
                lay_tiles(table, base, tiles_ref, lhs, [span], 0, blocks, block, at)
                return carry

            lax.fori_loop(0, count, one_owner, 0)
            total = jnp.dot(lhs[pl.ds(0, count * height)], x_out[...], preferred_element_type=jnp.float32)
            if n == 1:
                out[pl.ds(0, count * height)] = total.astype(jnp.bfloat16)
                for i in range(extra):
                    line = jnp.full((1, width), choice[i].astype(jnp.float32), jnp.float32)
                    out[pl.ds(count * height + i, 1)] = line.astype(jnp.bfloat16)
            else:
                out[...] = total.astype(jnp.bfloat16).reshape(out.shape)

    return call(
        body,
        [
            jax.ShapeDtypeStruct((len(orders) * edges * square,), jnp.int32),
            jax.ShapeDtypeStruct((edges * READ_CAP,), jnp.int32),
            *[jax.ShapeDtypeStruct(shape, jnp.bfloat16) for shape in shapes],
            jax.ShapeDtypeStruct(features.shape, jnp.bfloat16),
        ],
        [SMEM] + [HBM] * 7,
        [SMEM] * 2 + [VMEM] * (len(spans) + 1),
        (me, slot, col, tile_id, touched.transpose(0, 2, 1), readers, tiles, features),
        [
            pltpu.SMEM((products,), jnp.int32),
            pltpu.SMEM((products,), jnp.int32),
            pltpu.SMEM((products,), jnp.int32),
            pltpu.SMEM((cap, edges), jnp.int32),
            pltpu.SMEM((listed,), jnp.int32),
            pltpu.SMEM((extra + 1,), jnp.int32),
            pltpu.VMEM((tiles.shape[0], loaded, block), jnp.bfloat16),
            pltpu.VMEM((count * blocks * tallest, blocks * block), jnp.bfloat16),
            pltpu.SMEM((len(orders) * edges * cap,), jnp.int32),
            pltpu.SMEM((edges,), jnp.int32),
            pltpu.SemaphoreType.DMA((7,)),
        ],
        limit=62 * 1024 * 1024,
    )


def other_parts(table, tiles, inputs, jobs):
    block = tiles.shape[1]
    blocks = inputs.shape[0] // block
    width = inputs.shape[1]
    most = max(sum(rows for _, rows in spans) for _, _, spans in jobs) * blocks
    shapes = [
        jax.ShapeDtypeStruct((count, blocks, rows, width), jnp.bfloat16) for _, count, spans in jobs for _, rows in spans
    ]

    def body(table_ref, tiles_hbm, x_ref, *refs):
        outs = refs
        token, tiles_ref, lhs, sems = outs[-4:]
        token[...] = jnp.zeros_like(token)
        load = pltpu.make_async_copy(tiles_hbm, tiles_ref, sems.at[0])
        load.start()
        load.wait()
        for first, count, spans in jobs:
            height = blocks * sum(rows for _, rows in spans)

            def one_owner(i, carry):
                lay_tiles(table_ref, (first + i) * blocks * blocks, tiles_ref, lhs, spans, 0, blocks, block)
                total = jnp.dot(lhs[pl.ds(0, height)], x_ref[...], preferred_element_type=jnp.float32)
                total = total.astype(jnp.bfloat16)
                at = 0
                for out, (_, rows) in zip(outs, spans):
                    out[i] = total[at : at + blocks * rows].reshape(blocks, rows, width)
                    at += blocks * rows
                return carry

            lax.fori_loop(0, count, one_owner, 0)
            outs = outs[len(spans) :]

    results = call(
        body,
        shapes + [TOKEN],
        [SMEM, HBM, VMEM],
        [VMEM] * (len(shapes) + 1),
        (table, tiles, inputs),
        [
            pltpu.VMEM(tiles.shape, jnp.bfloat16),
            pltpu.VMEM((most, blocks * block), jnp.bfloat16),
            pltpu.SemaphoreType.DMA((1,)),
        ],
    )
    grouped, at = [], 0
    for _, _, spans in jobs:
        grouped.append(results[at : at + len(spans)])
        at += len(spans)
    return (*grouped, results[-1])


def combine(token, total, got, at_hand):
    count, *shape = total.shape
    left = count // 2

    def body(token_ref, total_ref, got_ref, at_hand_ref, *outs):
        def add(i, carry):
            if got.ndim == total.ndim:
                value = got_ref[i]
            else:
                height = shape[0] * shape[1]
                value = got_ref[pl.ds(pl.multiple_of(i * height, height), height)].reshape(shape)
            value = total_ref[i].astype(jnp.float32) + value.astype(jnp.float32)
            if not left:
                outs[0][...] = value.astype(jnp.bfloat16)
            else:

                @pl.when(i < left)
                def _():
                    outs[0][jnp.minimum(i, left - 1)] = value

                @pl.when(i >= left)
                def _():
                    outs[1][jnp.maximum(i - left, 0)] = value.astype(jnp.bfloat16)

            return carry

        lax.fori_loop(0, count, add, 0)
        outs[-1][...] = token_ref[...]

    if left:
        out_shape = [
            jax.ShapeDtypeStruct((left, *shape), jnp.float32),
            jax.ShapeDtypeStruct((count - left, *shape), jnp.bfloat16),
        ]
    else:
        out_shape = [jax.ShapeDtypeStruct(tuple(shape), jnp.bfloat16)]
    out_shape.append(TOKEN)
    return call(body, out_shape, [VMEM] * 4, [VMEM] * len(out_shape), (token, total, got, at_hand))


def join(token, held, got):
    def body(token_ref, held_ref, got_ref, out, token_out):
        out[pl.ds(0, held.shape[0])] = held_ref[...]
        out[pl.ds(held.shape[0], got.shape[0])] = got_ref[...]
        token_out[...] = token_ref[...]

    both = jax.ShapeDtypeStruct((held.shape[0] + got.shape[0], *held.shape[1:]), held.dtype)
    return call(body, [both, TOKEN], [VMEM] * 3, [VMEM] * 2, (token, held, got))


def mix(token, mine, offsets, held, got, weight):
    _, blocks, rows, depth = held.shape
    width = weight.shape[1]

    def body(token_ref, mine_ref, held_ref, got_ref, w_ref, out_ref, token_out):
        total = jnp.zeros((blocks * rows, width), jnp.float32)
        for n, offset in enumerate(offsets):
            piece = (held_ref if n < held.shape[0] else got_ref)[n % held.shape[0]]
            at = pl.multiple_of((mine_ref[0] ^ offset) * depth, depth)
            total += jnp.dot(
                piece.reshape(blocks * rows, depth), w_ref[pl.ds(at, depth)], preferred_element_type=jnp.float32
            )
        out_ref[0] = jnp.maximum(total, 0.0).astype(jnp.bfloat16).reshape(blocks, rows, width)
        token_out[...] = token_ref[...]

    return call(
        body,
        [jax.ShapeDtypeStruct((1, blocks, rows, width), jnp.bfloat16), TOKEN],
        [VMEM, SMEM, VMEM, VMEM, VMEM],
        [VMEM] * 2,
        (token, mine, held, got, weight),
    )


def pick(token, choice, held, got):
    count = 2 * held.shape[0] * READ_CAP

    def body(token_ref, choice_ref, held_ref, got_ref, out, token_out):
        for i in range(count):
            n = i // READ_CAP
            source = held_ref if n < held.shape[0] else got_ref
            out[i] = source[n % held.shape[0], choice_ref[i]]
        token_out[...] = token_ref[...]

    return call(
        body,
        [jax.ShapeDtypeStruct((count, *held.shape[2:]), held.dtype), TOKEN],
        [VMEM, SMEM, VMEM, VMEM],
        [VMEM] * 2,
        (token, choice, held, got),
    )


def read_choice(token, got, count):
    extra = -(-count // 16) * 16
    first = got.shape[0] - extra

    def body(token_ref, got_ref, choice, token_out):
        lines = got_ref[pl.ds(first, extra)].astype(jnp.float32)
        for i in range(count):
            choice[i] = jnp.max(lines[i : i + 1]).astype(jnp.int32)
        token_out[...] = token_ref[...]

    return call(
        body, [jax.ShapeDtypeStruct((count,), jnp.int32), TOKEN], [VMEM] * 2, [SMEM, VMEM], (token, got)
    )


def touch(token, value):
    def body(token_ref, value_ref, token_out):
        token_out[...] = token_ref[...]

    return call(body, [TOKEN], [VMEM] * 2, [VMEM], (token, value))


def lay_out(token, me, readers, entry, offsets, items, outputs, block):
    count = readers.shape[0]
    half_held, blocks, _, width = items[0][0].shape
    slots = len(offsets) * READ_CAP
    arrays = [array for item in items for array in item[:3]]

    def body(token_ref, me_ref, readers_ref, entry_ref, *refs):
        hidden_ref, ghost_ref, token_out, sems = refs[-4:]

        def each(act):
            for number, item in enumerate(items):
                held_ref, got_ref, far_ref = refs[3 * number : 3 * number + 3]
                rows = pl.ds(*item[3])
                act(pltpu.make_async_copy(held_ref.at[0], hidden_ref.at[:, rows], sems.at[number, 2 * slots]))
                for i in range(slots):
                    n, j = i // READ_CAP, i % READ_CAP
                    near = entry_ref[(me_ref[0] ^ offsets[n]) * READ_CAP + j]
                    source = held_ref if n < half_held else got_ref

                    @pl.when(near >= 0)
                    def _():
                        _, b = split(readers_ref[near], blocks)
                        target = ghost_ref.at[near, rows]
                        act(pltpu.make_async_copy(source.at[n % half_held, b], target, sems.at[number, i]))

                    across = entry_ref[(me_ref[0] ^ 1 ^ offsets[n]) * READ_CAP + j]

                    @pl.when(across >= 0)
                    def _():
                        target = ghost_ref.at[across, rows]
                        act(pltpu.make_async_copy(far_ref.at[i], target, sems.at[number, slots + i]))

        each(lambda copy: copy.start())
        token_out[...] = token_ref[...]
        each(lambda copy: copy.wait())

    operands = (token, me, readers, entry, *arrays, *outputs)
    return call(
        body,
        [
            jax.ShapeDtypeStruct((blocks, block, width), jnp.bfloat16),
            jax.ShapeDtypeStruct((count, block, width), jnp.bfloat16),
            TOKEN,
        ],
        [VMEM] + [SMEM] * 3 + [VMEM] * len(arrays) + [HBM] * len(outputs),
        [HBM, HBM, VMEM],
        operands,
        [pltpu.SemaphoreType.DMA((len(items), 2 * slots + 1))],
        aliases={len(operands) - 2: 0, len(operands) - 1: 1} if outputs else None,
    )


def local(features, tiles, tile_slot, tile_col, tile_id, touched, weight, readers):
    edges, feats = lax.axis_size("edge"), lax.axis_size("feat")
    half = edges // 2
    me, mine = lax.axis_index("edge"), lax.axis_index("feat")
    block = tiles.shape[1]
    blocks = features.shape[0] // block
    width = features.shape[1]
    unit = block // sum(SHARES)
    spans = [(sum(SHARES[:i]) * unit, share * unit) for i, share in enumerate(SHARES)]

    def flip(value, bit, axis="edge"):
        return lax.ppermute(value, axis, [(d, d ^ bit) for d in range(lax.axis_size(axis))])

    columns = offsets_of(edges, 2)
    me, mine = me.reshape(1), mine.reshape(1)
    column_bits = [1 << i for i in range(1, edges.bit_length() - 1)]
    orders = [[*column_bits, 1], [1, *column_bits]]
    table, entry, *early, inputs = first_part(
        me, tile_slot, tile_col, tile_id, touched, tiles, features, readers, orders, half, half, spans[:2]
    )
    later, first_kept, _ = other_parts(
        table, tiles, inputs, [(edges + half, half, spans[2:]), (0, half, spans[:1])]
    )
    away = [*early, *later]
    kept, token = other_parts(table, tiles, inputs, [(edges, half, spans[1:])])
    kept = [*first_kept, *kept]

    def chained(function, *operands):
        nonlocal token
        *results, token = function(token, *operands)
        return results

    def spread(held, size, lowest, axis):
        bit = size // 2
        while True:
            got = flip(held, bit, axis)
            yield
            if bit == lowest:
                return held, got
            (held,) = chained(join, held, got)
            bit //= 2

    choice = None

    def one_part(part):
        nonlocal choice
        first, *rest = orders[min(part, 1)]
        got = flip(away[part], first)
        yield
        total, sent = chained(combine, kept[part], got, weight)
        if part == 1:
            (choice,) = chained(read_choice, got, half * READ_CAP)
        for bit in rest:
            got = flip(sent, bit)
            yield
            total, *sent = chained(combine, total, got, weight)
            sent = sent[0] if sent else None
        held, got = yield from spread(total[None], feats, 1, "feat")
        (mixed,) = chained(mix, mine, offsets_of(feats, 1), held, got, weight)
        held, got = yield from spread(mixed, edges, 2, "edge")
        (picked,) = chained(pick, choice, held, got)
        far = flip(picked, 1)
        yield
        return held, got, far, spans[part]

    def links_of(bit):
        return {"x": 1.0} if bit == 1 else {"end": 1.0} if bit == 2 else {"end": 1.0, "middle": 2.0}

    feat_bits = [1 << i for i in reversed(range(feats.bit_length() - 1))]
    ways = []
    for part, (_, rows) in enumerate(spans):
        share = rows / block
        way = [(links_of(bit), share * half / (1 << n)) for n, bit in enumerate(orders[min(part, 1)])]
        way += [({"chip" if bit == 1 else "feat": 1.0}, share * (1.0 if bit > 1 else 0.3)) for bit in feat_bits]
        way += [(links_of(bit), share * half / bit) for bit in reversed(column_bits)]
        ways.append(way + [({"x": 1.0}, share * READ_CAP / blocks * half)])
    steps = [one_part(part) for part in range(len(spans))]
    for step in steps:
        next(step)
    known = sorted(ORDER) == [part for part, way in enumerate(ways) for _ in way]
    *order, last = ORDER if known else planned_order(ways)
    ended = []
    for part in order:
        try:
            next(steps[part])
        except StopIteration as end:
            ended.append(end.value)
            chained(touch, end.value[2])
    outputs = chained(lay_out, me, readers, entry, columns, ended, (), block)
    try:
        next(steps[last])
    except StopIteration as end:
        outputs = chained(lay_out, me, readers, entry, columns, [end.value], outputs, block)
    hidden, ghosts = outputs
    return hidden.reshape(blocks * block, width), ghosts.reshape(-1, width)


def solution(mesh):
    in_specs = (
        P("edge", "feat"),
        P("edge", None, None),
        P("edge"),
        P("edge"),
        P("edge"),
        P(),
        P(None, "feat"),
        P("edge"),
    )
    out_specs = (P("edge", "feat"), P("edge", "feat"))
    return jax.shard_map(local, mesh=mesh, in_specs=in_specs, out_specs=out_specs, check_vma=False)
```

```python
import jax
import jax.numpy as jnp
from jax import lax
from jax.experimental import pallas as pl
from jax.experimental.pallas import tpu as pltpu
from jax.sharding import PartitionSpec as P

SHARES = (2, 2, 1, 2, 1)
ORDER = (
    1, 0, 3, 2, 1, 0, 4, 3, 1, 2, 0, 3, 1, 4, 0, 0, 2, 1, 2, 0, 3, 4, 4, 3, 1, 0, 3, 4, 1, 4, 2, 0,
    3, 2, 4, 1, 2, 3, 4, 2,
)
READ_CAP = 2
VMEM_BYTES = 12 * 1024 * 1024
UNIT_TIME, START_TIME, STEP_TIME, LATENCY = 11.3, 0.9, 0.4, 0.6

SMEM = pl.BlockSpec(memory_space=pltpu.SMEM)
VMEM = pl.BlockSpec(memory_space=pltpu.VMEM)
HBM = pl.BlockSpec(memory_space=pltpu.HBM)
TOKEN = jax.ShapeDtypeStruct((8, 128), jnp.float32)


def call(body, out_shape, in_specs, out_specs, operands, scratch=(), aliases=None, limit=VMEM_BYTES):
    return pl.pallas_call(
        body,
        out_shape=out_shape,
        in_specs=in_specs,
        out_specs=out_specs,
        scratch_shapes=list(scratch),
        input_output_aliases=aliases or {},
        compiler_params=pltpu.CompilerParams(vmem_limit_bytes=limit),
        cost_estimate=pl.CostEstimate(flops=0, bytes_accessed=1, transcendentals=0),
    )(*operands)


def split(value, size):
    if size & (size - 1) == 0:
        return value >> (size.bit_length() - 1), value & (size - 1)
    return lax.div(value, size), lax.rem(value, size)


def place_of(peer, bits):
    place = 0
    for bit in bits:
        place = (place << 1) | ((peer >> (bit.bit_length() - 1)) & 1)
    return place


def planned_order(ways):
    now, order, flows, current, place = 0.0, [], [], {}, [0] * len(ways)

    def active():
        waiting = [f for f in flows if "x" in f["links"]][1:]
        running = [f for f in flows if not any(f is w for w in waiting)]
        load = {}
        for f in running:
            for link, weight in f["links"].items():
                load[link] = load.get(link, 0.0) + weight
        return [(f, min(1.0 / load[link] for link in f["links"])) for f in running]

    def advance(until):
        nonlocal now
        while now < until:
            running = active()
            step = min([until - now] + [f["left"] / rate for f, rate in running])
            now += max(step, 1e-3)
            for f, rate in running:
                f["left"] -= step * rate
                if f["left"] <= 1e-6:
                    f["end"] = now + LATENCY
            flows[:] = [f for f in flows if f["left"] > 1e-6]

    def begin(n):
        links, units = ways[n][place[n]]
        advance(now + START_TIME)
        current[n] = {"links": links, "left": units * UNIT_TIME, "end": None}
        flows.append(current[n])

    for n in range(len(ways)):
        begin(n)
    while current:
        ended = [(f["end"], n) for n, f in current.items() if f["end"] is not None and f["end"] <= now]
        if not ended:
            advance(now + 0.05)
            continue
        _, n = min(ended)
        order.append(n)
        del current[n]
        place[n] += 1
        advance(now + STEP_TIME)
        if place[n] < len(ways[n]):
            begin(n)
    return order


def offsets_of(size, lowest):
    offsets, bit = [0], size // 2
    while bit >= lowest:
        offsets += [offset | bit for offset in offsets]
        bit //= 2
    return offsets


def lay_tiles(table, base, tiles, lhs, spans, row_base, blocks, block, at=0):
    for b in range(blocks):
        for c in range(blocks):
            entry = table[base + b * blocks + c]
            tile = tiles[jnp.maximum(entry - 1, 0)]
            tile = jnp.where(entry > 0, tile, jnp.zeros_like(tile))
            top = at
            for first, rows in spans:
                lhs[pl.ds(top + b * rows, rows), pl.ds(c * block, block)] = tile[first - row_base : first - row_base + rows]
                top = top + blocks * rows


def first_part(me, slot, col, tile_id, touched, tiles, features, readers, orders, first, count, spans):
    block = tiles.shape[1]
    blocks = features.shape[0] // block
    width = features.shape[1]
    edges, cap = touched.shape[1], touched.shape[2]
    column_bits = [1 << i for i in range(1, edges.bit_length() - 1)]
    products = slot.shape[0]
    half = edges // 2
    loaded = sum(rows for _, rows in spans)
    tallest = max(rows for _, rows in spans)
    square = blocks * blocks

    listed = readers.shape[0]
    extra = -(-half * READ_CAP // 16) * 16
    shapes = [(count, blocks, rows, width) for _, rows in spans]
    shapes[1] = (count * blocks * spans[1][1] + extra, width)

    def body(me_ref, slot_hbm, col_hbm, id_hbm, touched_hbm, readers_hbm, tiles_hbm, x_hbm, *refs):
        table, entry, *outs = refs[: 2 + len(spans)]
        x_out, *scratch = refs[2 + len(spans) :]
        slot_ref, col_ref, id_ref, touched_ref, readers_ref, choice, tiles_ref, lhs, bases, seen, sems = scratch
        loads = [
            pltpu.make_async_copy(slot_hbm, slot_ref, sems.at[0]),
            pltpu.make_async_copy(col_hbm, col_ref, sems.at[1]),
            pltpu.make_async_copy(id_hbm, id_ref, sems.at[2]),
            pltpu.make_async_copy(touched_hbm.at[me_ref[0]], touched_ref, sems.at[5]),
            pltpu.make_async_copy(readers_hbm, readers_ref, sems.at[6]),
            pltpu.make_async_copy(x_hbm, x_out, sems.at[3]),
            pltpu.make_async_copy(tiles_hbm.at[:, pl.ds(0, loaded)], tiles_ref, sems.at[4]),
        ]
        for load in loads:
            load.start()

        def clear(i, carry):
            table[i] = 0
            return carry

        lax.fori_loop(0, len(orders) * edges * square, clear, 0, unroll=16)

        def place_slot(k, carry):
            owner, slot_at = split(k, cap)
            for n, order in enumerate(orders):
                place = place_of(owner ^ me_ref[0], order)
                bases[n * edges * cap + k] = ((n * edges + place) * blocks + touched_ref[slot_at, owner]) * blocks
            return carry

        for load in loads[:5]:
            load.wait()
        lax.fori_loop(0, edges * cap, place_slot, 0, unroll=8)

        for i in range(extra + 1):
            choice[i] = 0
        for i in range(edges * READ_CAP):
            entry[i] = -1
        for i in range(edges):
            seen[i] = 0

        def enter_lists(r, carry):
            owner, b = split(readers_ref[r], blocks)
            turn = seen[owner]
            seen[owner] = turn + 1
            turn = jnp.minimum(turn, READ_CAP - 1)
            entry[owner * READ_CAP + turn] = r
            peer = owner ^ me_ref[0] ^ 1
            row = place_of(peer, column_bits) * READ_CAP + turn
            choice[jnp.where(peer & 1 == 0, row, extra)] = b
            return carry

        lax.fori_loop(0, listed, enter_lists, 0)

        def enter(k, carry):
            for n in range(len(orders)):
                table[bases[n * edges * cap + slot_ref[k]] + col_ref[k]] = id_ref[k] + 1
            return carry

        lax.fori_loop(0, products, enter, 0, unroll=8)
        for load in loads[5:]:
            load.wait()

        for n, (span, out) in enumerate(zip(spans, outs)):
            height = blocks * span[1]

            def one_owner(i, carry):
                at = pl.multiple_of(i * height, height)
                base = (n * edges + first + i) * square
                lay_tiles(table, base, tiles_ref, lhs, [span], 0, blocks, block, at)
                return carry

            lax.fori_loop(0, count, one_owner, 0)
            total = jnp.dot(lhs[pl.ds(0, count * height)], x_out[...], preferred_element_type=jnp.float32)
            if n == 1:
                out[pl.ds(0, count * height)] = total.astype(jnp.bfloat16)
                for i in range(extra):
                    line = jnp.full((1, width), choice[i].astype(jnp.float32), jnp.float32)
                    out[pl.ds(count * height + i, 1)] = line.astype(jnp.bfloat16)
            else:
                out[...] = total.astype(jnp.bfloat16).reshape(out.shape)

    return call(
        body,
        [
            jax.ShapeDtypeStruct((len(orders) * edges * square,), jnp.int32),
            jax.ShapeDtypeStruct((edges * READ_CAP,), jnp.int32),
            *[jax.ShapeDtypeStruct(shape, jnp.bfloat16) for shape in shapes],
            jax.ShapeDtypeStruct(features.shape, jnp.bfloat16),
        ],
        [SMEM] + [HBM] * 7,
        [SMEM] * 2 + [VMEM] * (len(spans) + 1),
        (me, slot, col, tile_id, touched.transpose(0, 2, 1), readers, tiles, features),
        [
            pltpu.SMEM((products,), jnp.int32),
            pltpu.SMEM((products,), jnp.int32),
            pltpu.SMEM((products,), jnp.int32),
            pltpu.SMEM((cap, edges), jnp.int32),
            pltpu.SMEM((listed,), jnp.int32),
            pltpu.SMEM((extra + 1,), jnp.int32),
            pltpu.VMEM((tiles.shape[0], loaded, block), jnp.bfloat16),
            pltpu.VMEM((count * blocks * tallest, blocks * block), jnp.bfloat16),
            pltpu.SMEM((len(orders) * edges * cap,), jnp.int32),
            pltpu.SMEM((edges,), jnp.int32),
            pltpu.SemaphoreType.DMA((7,)),
        ],
        limit=62 * 1024 * 1024,
    )


def other_parts(table, tiles, inputs, jobs):
    block = tiles.shape[1]
    blocks = inputs.shape[0] // block
    width = inputs.shape[1]
    most = max(sum(rows for _, rows in spans) for _, _, spans in jobs) * blocks
    shapes = [
        jax.ShapeDtypeStruct((count, blocks, rows, width), jnp.bfloat16) for _, count, spans in jobs for _, rows in spans
    ]

    def body(table_ref, tiles_hbm, x_ref, *refs):
        outs = refs
        token, tiles_ref, lhs, sems = outs[-4:]
        token[...] = jnp.zeros_like(token)
        load = pltpu.make_async_copy(tiles_hbm, tiles_ref, sems.at[0])
        load.start()
        load.wait()
        for first, count, spans in jobs:
            height = blocks * sum(rows for _, rows in spans)

            def one_owner(i, carry):
                lay_tiles(table_ref, (first + i) * blocks * blocks, tiles_ref, lhs, spans, 0, blocks, block)
                total = jnp.dot(lhs[pl.ds(0, height)], x_ref[...], preferred_element_type=jnp.float32)
                total = total.astype(jnp.bfloat16)
                at = 0
                for out, (_, rows) in zip(outs, spans):
                    out[i] = total[at : at + blocks * rows].reshape(blocks, rows, width)
                    at += blocks * rows
                return carry

            lax.fori_loop(0, count, one_owner, 0)
            outs = outs[len(spans) :]

    results = call(
        body,
        shapes + [TOKEN],
        [SMEM, HBM, VMEM],
        [VMEM] * (len(shapes) + 1),
        (table, tiles, inputs),
        [
            pltpu.VMEM(tiles.shape, jnp.bfloat16),
            pltpu.VMEM((most, blocks * block), jnp.bfloat16),
            pltpu.SemaphoreType.DMA((1,)),
        ],
    )
    grouped, at = [], 0
    for _, _, spans in jobs:
        grouped.append(results[at : at + len(spans)])
        at += len(spans)
    return (*grouped, results[-1])


def combine(token, total, got, at_hand):
    count, *shape = total.shape
    left = count // 2

    def body(token_ref, total_ref, got_ref, at_hand_ref, *outs):
        def add(i, carry):
            if got.ndim == total.ndim:
                value = got_ref[i]
            else:
                height = shape[0] * shape[1]
                value = got_ref[pl.ds(pl.multiple_of(i * height, height), height)].reshape(shape)
            value = total_ref[i].astype(jnp.float32) + value.astype(jnp.float32)
            if not left:
                outs[0][...] = value.astype(jnp.bfloat16)
            else:

                @pl.when(i < left)
                def _():
                    outs[0][jnp.minimum(i, left - 1)] = value

                @pl.when(i >= left)
                def _():
                    outs[1][jnp.maximum(i - left, 0)] = value.astype(jnp.bfloat16)

            return carry

        lax.fori_loop(0, count, add, 0)
        outs[-1][...] = token_ref[...]

    if left:
        out_shape = [
            jax.ShapeDtypeStruct((left, *shape), jnp.float32),
            jax.ShapeDtypeStruct((count - left, *shape), jnp.bfloat16),
        ]
    else:
        out_shape = [jax.ShapeDtypeStruct(tuple(shape), jnp.bfloat16)]
    out_shape.append(TOKEN)
    return call(body, out_shape, [VMEM] * 4, [VMEM] * len(out_shape), (token, total, got, at_hand))


def join(token, held, got):
    def body(token_ref, held_ref, got_ref, out, token_out):
        out[pl.ds(0, held.shape[0])] = held_ref[...]
        out[pl.ds(held.shape[0], got.shape[0])] = got_ref[...]
        token_out[...] = token_ref[...]

    both = jax.ShapeDtypeStruct((held.shape[0] + got.shape[0], *held.shape[1:]), held.dtype)
    return call(body, [both, TOKEN], [VMEM] * 3, [VMEM] * 2, (token, held, got))


def mix(token, mine, offsets, held, got, weight):
    _, blocks, rows, depth = held.shape
    width = weight.shape[1]

    def body(token_ref, mine_ref, held_ref, got_ref, w_ref, out_ref, token_out):
        total = jnp.zeros((blocks * rows, width), jnp.float32)
        for n, offset in enumerate(offsets):
            piece = (held_ref if n < held.shape[0] else got_ref)[n % held.shape[0]]
            at = pl.multiple_of((mine_ref[0] ^ offset) * depth, depth)
            total += jnp.dot(
                piece.reshape(blocks * rows, depth), w_ref[pl.ds(at, depth)], preferred_element_type=jnp.float32
            )
        out_ref[0] = jnp.maximum(total, 0.0).astype(jnp.bfloat16).reshape(blocks, rows, width)
        token_out[...] = token_ref[...]

    return call(
        body,
        [jax.ShapeDtypeStruct((1, blocks, rows, width), jnp.bfloat16), TOKEN],
        [VMEM, SMEM, VMEM, VMEM, VMEM],
        [VMEM] * 2,
        (token, mine, held, got, weight),
    )


def pick(token, choice, held, got):
    count = 2 * held.shape[0] * READ_CAP

    def body(token_ref, choice_ref, held_ref, got_ref, out, token_out):
        for i in range(count):
            n = i // READ_CAP
            source = held_ref if n < held.shape[0] else got_ref
            out[i] = source[n % held.shape[0], choice_ref[i]]
        token_out[...] = token_ref[...]

    return call(
        body,
        [jax.ShapeDtypeStruct((count, *held.shape[2:]), held.dtype), TOKEN],
        [VMEM, SMEM, VMEM, VMEM],
        [VMEM] * 2,
        (token, choice, held, got),
    )


def read_choice(token, got, count):
    extra = -(-count // 16) * 16
    first = got.shape[0] - extra

    def body(token_ref, got_ref, choice, token_out):
        lines = got_ref[pl.ds(first, extra)].astype(jnp.float32)
        for i in range(count):
            choice[i] = jnp.max(lines[i : i + 1]).astype(jnp.int32)
        token_out[...] = token_ref[...]

    return call(
        body, [jax.ShapeDtypeStruct((count,), jnp.int32), TOKEN], [VMEM] * 2, [SMEM, VMEM], (token, got)
    )


def touch(token, value):
    def body(token_ref, value_ref, token_out):
        token_out[...] = token_ref[...]

    return call(body, [TOKEN], [VMEM] * 2, [VMEM], (token, value))


def lay_out(token, me, readers, entry, offsets, items, outputs, block):
    count = readers.shape[0]
    half_held, blocks, _, width = items[0][0].shape
    slots = len(offsets) * READ_CAP
    arrays = [array for item in items for array in item[:3]]

    def body(token_ref, me_ref, readers_ref, entry_ref, *refs):
        hidden_ref, ghost_ref, token_out, sems = refs[-4:]

        def each(act):
            for number, item in enumerate(items):
                held_ref, got_ref, far_ref = refs[3 * number : 3 * number + 3]
                rows = pl.ds(*item[3])
                act(pltpu.make_async_copy(held_ref.at[0], hidden_ref.at[:, rows], sems.at[number, 2 * slots]))
                for i in range(slots):
                    n, j = i // READ_CAP, i % READ_CAP
                    near = entry_ref[(me_ref[0] ^ offsets[n]) * READ_CAP + j]
                    source = held_ref if n < half_held else got_ref

                    @pl.when(near >= 0)
                    def _():
                        _, b = split(readers_ref[near], blocks)
                        target = ghost_ref.at[near, rows]
                        act(pltpu.make_async_copy(source.at[n % half_held, b], target, sems.at[number, i]))

                    across = entry_ref[(me_ref[0] ^ 1 ^ offsets[n]) * READ_CAP + j]

                    @pl.when(across >= 0)
                    def _():
                        target = ghost_ref.at[across, rows]
                        act(pltpu.make_async_copy(far_ref.at[i], target, sems.at[number, slots + i]))

        each(lambda copy: copy.start())
        token_out[...] = token_ref[...]
        each(lambda copy: copy.wait())

    operands = (token, me, readers, entry, *arrays, *outputs)
    return call(
        body,
        [
            jax.ShapeDtypeStruct((blocks, block, width), jnp.bfloat16),
            jax.ShapeDtypeStruct((count, block, width), jnp.bfloat16),
            TOKEN,
        ],
        [VMEM] + [SMEM] * 3 + [VMEM] * len(arrays) + [HBM] * len(outputs),
        [HBM, HBM, VMEM],
        operands,
        [pltpu.SemaphoreType.DMA((len(items), 2 * slots + 1))],
        aliases={len(operands) - 2: 0, len(operands) - 1: 1} if outputs else None,
    )


def local(features, tiles, tile_slot, tile_col, tile_id, touched, weight, readers):
    edges, feats = lax.axis_size("edge"), lax.axis_size("feat")
    half = edges // 2
    me, mine = lax.axis_index("edge"), lax.axis_index("feat")
    block = tiles.shape[1]
    blocks = features.shape[0] // block
    width = features.shape[1]
    unit = block // sum(SHARES)
    spans = [(sum(SHARES[:i]) * unit, share * unit) for i, share in enumerate(SHARES)]

    def flip(value, bit, axis="edge"):
        return lax.ppermute(value, axis, [(d, d ^ bit) for d in range(lax.axis_size(axis))])

    columns = offsets_of(edges, 2)
    me, mine = me.reshape(1), mine.reshape(1)
    column_bits = [1 << i for i in range(1, edges.bit_length() - 1)]
    orders = [[*column_bits, 1], [1, *column_bits]]
    table, entry, *early, inputs = first_part(
        me, tile_slot, tile_col, tile_id, touched, tiles, features, readers, orders, half, half, spans[:2]
    )
    later, first_kept, _ = other_parts(
        table, tiles, inputs, [(edges + half, half, spans[2:]), (0, half, spans[:1])]
    )
    away = [*early, *later]
    kept, token = other_parts(table, tiles, inputs, [(edges, half, spans[1:])])
    kept = [*first_kept, *kept]

    def chained(function, *operands):
        nonlocal token
        *results, token = function(token, *operands)
        return results

    def spread(held, size, lowest, axis):
        bit = size // 2
        while True:
            got = flip(held, bit, axis)
            yield
            if bit == lowest:
                return held, got
            (held,) = chained(join, held, got)
            bit //= 2

    choice = None

    def one_part(part):
        nonlocal choice
        first, *rest = orders[min(part, 1)]
        got = flip(away[part], first)
        yield
        total, sent = chained(combine, kept[part], got, weight)
        if part == 1:
            (choice,) = chained(read_choice, got, half * READ_CAP)
        for bit in rest:
            got = flip(sent, bit)
            yield
            total, *sent = chained(combine, total, got, weight)
            sent = sent[0] if sent else None
        held, got = yield from spread(total[None], feats, 1, "feat")
        (mixed,) = chained(mix, mine, offsets_of(feats, 1), held, got, weight)
        held, got = yield from spread(mixed, edges, 2, "edge")
        (picked,) = chained(pick, choice, held, got)
        far = flip(picked, 1)
        yield
        return held, got, far, spans[part]

    def links_of(bit):
        return {"x": 1.0} if bit == 1 else {"end": 1.0} if bit == 2 else {"end": 1.0, "middle": 2.0}

    feat_bits = [1 << i for i in reversed(range(feats.bit_length() - 1))]
    ways = []
    for part, (_, rows) in enumerate(spans):
        share = rows / block
        way = [(links_of(bit), share * half / (1 << n)) for n, bit in enumerate(orders[min(part, 1)])]
        way += [({"chip" if bit == 1 else "feat": 1.0}, share * (1.0 if bit > 1 else 0.3)) for bit in feat_bits]
        way += [(links_of(bit), share * half / bit) for bit in reversed(column_bits)]
        ways.append(way + [({"x": 1.0}, share * READ_CAP / blocks * half)])
    steps = [one_part(part) for part in range(len(spans))]
    for step in steps:
        next(step)
    known = sorted(ORDER) == [part for part, way in enumerate(ways) for _ in way]
    *order, last = ORDER if known else planned_order(ways)
    ended = []
    for part in order:
        try:
            next(steps[part])
        except StopIteration as end:
            ended.append(end.value)
            chained(touch, end.value[2])
    outputs = chained(lay_out, me, readers, entry, columns, ended, (), block)
    try:
        next(steps[last])
    except StopIteration as end:
        outputs = chained(lay_out, me, readers, entry, columns, [end.value], outputs, block)
    hidden, ghosts = outputs
    return hidden.reshape(blocks * block, width), ghosts.reshape(-1, width)


def solution(mesh):
    in_specs = (
        P("edge", "feat"),
        P("edge", None, None),
        P("edge"),
        P("edge"),
        P("edge"),
        P(),
        P(None, "feat"),
        P("edge"),
    )
    out_specs = (P("edge", "feat"), P("edge", "feat"))
    return jax.shard_map(local, mesh=mesh, in_specs=in_specs, out_specs=out_specs, check_vma=False)
```

```python
import jax
import jax.numpy as jnp
from jax import lax
from jax.experimental import pallas as pl
from jax.experimental.pallas import tpu as pltpu
from jax.sharding import PartitionSpec as P

SHARES = (2, 2, 2, 1, 1)
ORDER = (
    0, 1, 2, 0, 1, 2, 1, 3, 4, 0, 2, 1, 1, 4, 1, 2, 3, 4, 0, 2, 0, 3, 3, 2, 4, 1, 0, 4, 2, 4, 3, 1,
    0, 3, 4, 2, 3, 0, 4, 3,
)
READ_CAP = 2
VMEM_BYTES = 12 * 1024 * 1024
UNIT_TIME, START_TIME, STEP_TIME, LATENCY = 11.3, 0.9, 0.4, 0.6

SMEM = pl.BlockSpec(memory_space=pltpu.SMEM)
VMEM = pl.BlockSpec(memory_space=pltpu.VMEM)
HBM = pl.BlockSpec(memory_space=pltpu.HBM)
TOKEN = jax.ShapeDtypeStruct((8, 128), jnp.float32)


def call(body, out_shape, in_specs, out_specs, operands, scratch=(), aliases=None, limit=VMEM_BYTES):
    return pl.pallas_call(
        body,
        out_shape=out_shape,
        in_specs=in_specs,
        out_specs=out_specs,
        scratch_shapes=list(scratch),
        input_output_aliases=aliases or {},
        compiler_params=pltpu.CompilerParams(vmem_limit_bytes=limit),
        cost_estimate=pl.CostEstimate(flops=0, bytes_accessed=1, transcendentals=0),
    )(*operands)


def split(value, size):
    if size & (size - 1) == 0:
        return value >> (size.bit_length() - 1), value & (size - 1)
    return lax.div(value, size), lax.rem(value, size)


def place_of(peer, bits):
    place = 0
    for bit in bits:
        place = (place << 1) | ((peer >> (bit.bit_length() - 1)) & 1)
    return place


def planned_order(ways):
    now, order, flows, current, place = 0.0, [], [], {}, [0] * len(ways)

    def active():
        waiting = [f for f in flows if "x" in f["links"]][1:]
        running = [f for f in flows if not any(f is w for w in waiting)]
        load = {}
        for f in running:
            for link, weight in f["links"].items():
                load[link] = load.get(link, 0.0) + weight
        return [(f, min(1.0 / load[link] for link in f["links"])) for f in running]

    def advance(until):
        nonlocal now
        while now < until:
            running = active()
            step = min([until - now] + [f["left"] / rate for f, rate in running])
            now += max(step, 1e-3)
            for f, rate in running:
                f["left"] -= step * rate
                if f["left"] <= 1e-6:
                    f["end"] = now + LATENCY
            flows[:] = [f for f in flows if f["left"] > 1e-6]

    def begin(n):
        links, units = ways[n][place[n]]
        advance(now + START_TIME)
        current[n] = {"links": links, "left": units * UNIT_TIME, "end": None}
        flows.append(current[n])

    for n in range(len(ways)):
        begin(n)
    while current:
        ended = [(f["end"], n) for n, f in current.items() if f["end"] is not None and f["end"] <= now]
        if not ended:
            advance(now + 0.05)
            continue
        _, n = min(ended)
        order.append(n)
        del current[n]
        place[n] += 1
        advance(now + STEP_TIME)
        if place[n] < len(ways[n]):
            begin(n)
    return order


def offsets_of(size, lowest):
    offsets, bit = [0], size // 2
    while bit >= lowest:
        offsets += [offset | bit for offset in offsets]
        bit //= 2
    return offsets


def lay_tiles(table, base, tiles, lhs, spans, row_base, blocks, block, at=0):
    for b in range(blocks):
        for c in range(blocks):
            entry = table[base + b * blocks + c]
            tile = tiles[jnp.maximum(entry - 1, 0)]
            tile = jnp.where(entry > 0, tile, jnp.zeros_like(tile))
            top = at
            for first, rows in spans:
                lhs[pl.ds(top + b * rows, rows), pl.ds(c * block, block)] = tile[first - row_base : first - row_base + rows]
                top = top + blocks * rows


def first_part(me, slot, col, tile_id, touched, tiles, features, readers, orders, first, count, spans):
    block = tiles.shape[1]
    blocks = features.shape[0] // block
    width = features.shape[1]
    edges, cap = touched.shape[1], touched.shape[2]
    column_bits = [1 << i for i in range(1, edges.bit_length() - 1)]
    products = slot.shape[0]
    half = edges // 2
    loaded = sum(rows for _, rows in spans)
    tallest = max(rows for _, rows in spans)
    square = blocks * blocks

    listed = readers.shape[0]
    extra = -(-half * READ_CAP // 16) * 16
    shapes = [(count, blocks, rows, width) for _, rows in spans]
    shapes[1] = (count * blocks * spans[1][1] + extra, width)

    def body(me_ref, slot_hbm, col_hbm, id_hbm, touched_hbm, readers_hbm, tiles_hbm, x_hbm, *refs):
        table, entry, *outs = refs[: 2 + len(spans)]
        x_out, *scratch = refs[2 + len(spans) :]
        slot_ref, col_ref, id_ref, touched_ref, readers_ref, choice, tiles_ref, lhs, bases, seen, sems = scratch
        loads = [
            pltpu.make_async_copy(slot_hbm, slot_ref, sems.at[0]),
            pltpu.make_async_copy(col_hbm, col_ref, sems.at[1]),
            pltpu.make_async_copy(id_hbm, id_ref, sems.at[2]),
            pltpu.make_async_copy(touched_hbm.at[me_ref[0]], touched_ref, sems.at[5]),
            pltpu.make_async_copy(readers_hbm, readers_ref, sems.at[6]),
            pltpu.make_async_copy(x_hbm, x_out, sems.at[3]),
            pltpu.make_async_copy(tiles_hbm.at[:, pl.ds(0, loaded)], tiles_ref, sems.at[4]),
        ]
        for load in loads:
            load.start()

        def clear(i, carry):
            table[i] = 0
            return carry

        lax.fori_loop(0, len(orders) * edges * square, clear, 0, unroll=16)

        def place_slot(k, carry):
            owner, slot_at = split(k, cap)
            for n, order in enumerate(orders):
                place = place_of(owner ^ me_ref[0], order)
                bases[n * edges * cap + k] = ((n * edges + place) * blocks + touched_ref[slot_at, owner]) * blocks
            return carry

        for load in loads[:5]:
            load.wait()
        lax.fori_loop(0, edges * cap, place_slot, 0, unroll=8)

        for i in range(extra + 1):
            choice[i] = 0
        for i in range(edges * READ_CAP):
            entry[i] = -1
        for i in range(edges):
            seen[i] = 0

        def enter_lists(r, carry):
            owner, b = split(readers_ref[r], blocks)
            turn = seen[owner]
            seen[owner] = turn + 1
            turn = jnp.minimum(turn, READ_CAP - 1)
            entry[owner * READ_CAP + turn] = r
            peer = owner ^ me_ref[0] ^ 1
            row = place_of(peer, column_bits) * READ_CAP + turn
            choice[jnp.where(peer & 1 == 0, row, extra)] = b
            return carry

        lax.fori_loop(0, listed, enter_lists, 0)

        def enter(k, carry):
            for n in range(len(orders)):
                table[bases[n * edges * cap + slot_ref[k]] + col_ref[k]] = id_ref[k] + 1
            return carry

        lax.fori_loop(0, products, enter, 0, unroll=8)
        for load in loads[5:]:
            load.wait()

        for n, (span, out) in enumerate(zip(spans, outs)):
            height = blocks * span[1]

            def one_owner(i, carry):
                at = pl.multiple_of(i * height, height)
                base = (n * edges + first + i) * square
                lay_tiles(table, base, tiles_ref, lhs, [span], 0, blocks, block, at)
                return carry

            lax.fori_loop(0, count, one_owner, 0)
            total = jnp.dot(lhs[pl.ds(0, count * height)], x_out[...], preferred_element_type=jnp.float32)
            if n == 1:
                out[pl.ds(0, count * height)] = total.astype(jnp.bfloat16)
                for i in range(extra):
                    line = jnp.full((1, width), choice[i].astype(jnp.float32), jnp.float32)
                    out[pl.ds(count * height + i, 1)] = line.astype(jnp.bfloat16)
            else:
                out[...] = total.astype(jnp.bfloat16).reshape(out.shape)

    return call(
        body,
        [
            jax.ShapeDtypeStruct((len(orders) * edges * square,), jnp.int32),
            jax.ShapeDtypeStruct((edges * READ_CAP,), jnp.int32),
            *[jax.ShapeDtypeStruct(shape, jnp.bfloat16) for shape in shapes],
            jax.ShapeDtypeStruct(features.shape, jnp.bfloat16),
        ],
        [SMEM] + [HBM] * 7,
        [SMEM] * 2 + [VMEM] * (len(spans) + 1),
        (me, slot, col, tile_id, touched.transpose(0, 2, 1), readers, tiles, features),
        [
            pltpu.SMEM((products,), jnp.int32),
            pltpu.SMEM((products,), jnp.int32),
            pltpu.SMEM((products,), jnp.int32),
            pltpu.SMEM((cap, edges), jnp.int32),
            pltpu.SMEM((listed,), jnp.int32),
            pltpu.SMEM((extra + 1,), jnp.int32),
            pltpu.VMEM((tiles.shape[0], loaded, block), jnp.bfloat16),
            pltpu.VMEM((count * blocks * tallest, blocks * block), jnp.bfloat16),
            pltpu.SMEM((len(orders) * edges * cap,), jnp.int32),
            pltpu.SMEM((edges,), jnp.int32),
            pltpu.SemaphoreType.DMA((7,)),
        ],
        limit=62 * 1024 * 1024,
    )


def other_parts(table, tiles, inputs, jobs):
    block = tiles.shape[1]
    blocks = inputs.shape[0] // block
    width = inputs.shape[1]
    most = max(sum(rows for _, rows in spans) for _, _, spans in jobs) * blocks
    shapes = [
        jax.ShapeDtypeStruct((count, blocks, rows, width), jnp.bfloat16) for _, count, spans in jobs for _, rows in spans
    ]

    def body(table_ref, tiles_hbm, x_ref, *refs):
        outs = refs
        token, tiles_ref, lhs, sems = outs[-4:]
        token[...] = jnp.zeros_like(token)
        load = pltpu.make_async_copy(tiles_hbm, tiles_ref, sems.at[0])
        load.start()
        load.wait()
        for first, count, spans in jobs:
            height = blocks * sum(rows for _, rows in spans)

            def one_owner(i, carry):
                lay_tiles(table_ref, (first + i) * blocks * blocks, tiles_ref, lhs, spans, 0, blocks, block)
                total = jnp.dot(lhs[pl.ds(0, height)], x_ref[...], preferred_element_type=jnp.float32)
                total = total.astype(jnp.bfloat16)
                at = 0
                for out, (_, rows) in zip(outs, spans):
                    out[i] = total[at : at + blocks * rows].reshape(blocks, rows, width)
                    at += blocks * rows
                return carry

            lax.fori_loop(0, count, one_owner, 0)
            outs = outs[len(spans) :]

    results = call(
        body,
        shapes + [TOKEN],
        [SMEM, HBM, VMEM],
        [VMEM] * (len(shapes) + 1),
        (table, tiles, inputs),
        [
            pltpu.VMEM(tiles.shape, jnp.bfloat16),
            pltpu.VMEM((most, blocks * block), jnp.bfloat16),
            pltpu.SemaphoreType.DMA((1,)),
        ],
    )
    grouped, at = [], 0
    for _, _, spans in jobs:
        grouped.append(results[at : at + len(spans)])
        at += len(spans)
    return (*grouped, results[-1])


def combine(token, total, got, at_hand):
    count, *shape = total.shape
    left = count // 2

    def body(token_ref, total_ref, got_ref, at_hand_ref, *outs):
        def add(i, carry):
            if got.ndim == total.ndim:
                value = got_ref[i]
            else:
                height = shape[0] * shape[1]
                value = got_ref[pl.ds(pl.multiple_of(i * height, height), height)].reshape(shape)
            value = total_ref[i].astype(jnp.float32) + value.astype(jnp.float32)
            if not left:
                outs[0][...] = value.astype(jnp.bfloat16)
            else:

                @pl.when(i < left)
                def _():
                    outs[0][jnp.minimum(i, left - 1)] = value

                @pl.when(i >= left)
                def _():
                    outs[1][jnp.maximum(i - left, 0)] = value.astype(jnp.bfloat16)

            return carry

        lax.fori_loop(0, count, add, 0)
        outs[-1][...] = token_ref[...]

    if left:
        out_shape = [
            jax.ShapeDtypeStruct((left, *shape), jnp.float32),
            jax.ShapeDtypeStruct((count - left, *shape), jnp.bfloat16),
        ]
    else:
        out_shape = [jax.ShapeDtypeStruct(tuple(shape), jnp.bfloat16)]
    out_shape.append(TOKEN)
    return call(body, out_shape, [VMEM] * 4, [VMEM] * len(out_shape), (token, total, got, at_hand))


def join(token, held, got):
    def body(token_ref, held_ref, got_ref, out, token_out):
        out[pl.ds(0, held.shape[0])] = held_ref[...]
        out[pl.ds(held.shape[0], got.shape[0])] = got_ref[...]
        token_out[...] = token_ref[...]

    both = jax.ShapeDtypeStruct((held.shape[0] + got.shape[0], *held.shape[1:]), held.dtype)
    return call(body, [both, TOKEN], [VMEM] * 3, [VMEM] * 2, (token, held, got))


def mix(token, mine, offsets, held, got, weight):
    _, blocks, rows, depth = held.shape
    width = weight.shape[1]

    def body(token_ref, mine_ref, held_ref, got_ref, w_ref, out_ref, token_out):
        total = jnp.zeros((blocks * rows, width), jnp.float32)
        for n, offset in enumerate(offsets):
            piece = (held_ref if n < held.shape[0] else got_ref)[n % held.shape[0]]
            at = pl.multiple_of((mine_ref[0] ^ offset) * depth, depth)
            total += jnp.dot(
                piece.reshape(blocks * rows, depth), w_ref[pl.ds(at, depth)], preferred_element_type=jnp.float32
            )
        out_ref[0] = jnp.maximum(total, 0.0).astype(jnp.bfloat16).reshape(blocks, rows, width)
        token_out[...] = token_ref[...]

    return call(
        body,
        [jax.ShapeDtypeStruct((1, blocks, rows, width), jnp.bfloat16), TOKEN],
        [VMEM, SMEM, VMEM, VMEM, VMEM],
        [VMEM] * 2,
        (token, mine, held, got, weight),
    )


def pick(token, choice, held, got):
    count = 2 * held.shape[0] * READ_CAP

    def body(token_ref, choice_ref, held_ref, got_ref, out, token_out):
        for i in range(count):
            n = i // READ_CAP
            source = held_ref if n < held.shape[0] else got_ref
            out[i] = source[n % held.shape[0], choice_ref[i]]
        token_out[...] = token_ref[...]

    return call(
        body,
        [jax.ShapeDtypeStruct((count, *held.shape[2:]), held.dtype), TOKEN],
        [VMEM, SMEM, VMEM, VMEM],
        [VMEM] * 2,
        (token, choice, held, got),
    )


def read_choice(token, got, count):
    extra = -(-count // 16) * 16
    first = got.shape[0] - extra

    def body(token_ref, got_ref, choice, token_out):
        lines = got_ref[pl.ds(first, extra)].astype(jnp.float32)
        for i in range(count):
            choice[i] = jnp.max(lines[i : i + 1]).astype(jnp.int32)
        token_out[...] = token_ref[...]

    return call(
        body, [jax.ShapeDtypeStruct((count,), jnp.int32), TOKEN], [VMEM] * 2, [SMEM, VMEM], (token, got)
    )


def touch(token, value):
    def body(token_ref, value_ref, token_out):
        token_out[...] = token_ref[...]

    return call(body, [TOKEN], [VMEM] * 2, [VMEM], (token, value))


def lay_out(token, me, readers, entry, offsets, items, outputs, block):
    count = readers.shape[0]
    half_held, blocks, _, width = items[0][0].shape
    slots = len(offsets) * READ_CAP
    arrays = [array for item in items for array in item[:3]]

    def body(token_ref, me_ref, readers_ref, entry_ref, *refs):
        hidden_ref, ghost_ref, token_out, sems = refs[-4:]

        def each(act):
            for number, item in enumerate(items):
                held_ref, got_ref, far_ref = refs[3 * number : 3 * number + 3]
                rows = pl.ds(*item[3])
                act(pltpu.make_async_copy(held_ref.at[0], hidden_ref.at[:, rows], sems.at[number, 2 * slots]))
                for i in range(slots):
                    n, j = i // READ_CAP, i % READ_CAP
                    near = entry_ref[(me_ref[0] ^ offsets[n]) * READ_CAP + j]
                    source = held_ref if n < half_held else got_ref

                    @pl.when(near >= 0)
                    def _():
                        _, b = split(readers_ref[near], blocks)
                        target = ghost_ref.at[near, rows]
                        act(pltpu.make_async_copy(source.at[n % half_held, b], target, sems.at[number, i]))

                    across = entry_ref[(me_ref[0] ^ 1 ^ offsets[n]) * READ_CAP + j]

                    @pl.when(across >= 0)
                    def _():
                        target = ghost_ref.at[across, rows]
                        act(pltpu.make_async_copy(far_ref.at[i], target, sems.at[number, slots + i]))

        each(lambda copy: copy.start())
        token_out[...] = token_ref[...]
        each(lambda copy: copy.wait())

    operands = (token, me, readers, entry, *arrays, *outputs)
    return call(
        body,
        [
            jax.ShapeDtypeStruct((blocks, block, width), jnp.bfloat16),
            jax.ShapeDtypeStruct((count, block, width), jnp.bfloat16),
            TOKEN,
        ],
        [VMEM] + [SMEM] * 3 + [VMEM] * len(arrays) + [HBM] * len(outputs),
        [HBM, HBM, VMEM],
        operands,
        [pltpu.SemaphoreType.DMA((len(items), 2 * slots + 1))],
        aliases={len(operands) - 2: 0, len(operands) - 1: 1} if outputs else None,
    )


def local(features, tiles, tile_slot, tile_col, tile_id, touched, weight, readers):
    edges, feats = lax.axis_size("edge"), lax.axis_size("feat")
    half = edges // 2
    me, mine = lax.axis_index("edge"), lax.axis_index("feat")
    block = tiles.shape[1]
    blocks = features.shape[0] // block
    width = features.shape[1]
    unit = block // sum(SHARES)
    spans = [(sum(SHARES[:i]) * unit, share * unit) for i, share in enumerate(SHARES)]

    def flip(value, bit, axis="edge"):
        return lax.ppermute(value, axis, [(d, d ^ bit) for d in range(lax.axis_size(axis))])

    columns = offsets_of(edges, 2)
    me, mine = me.reshape(1), mine.reshape(1)
    column_bits = [1 << i for i in range(1, edges.bit_length() - 1)]
    orders = [[*column_bits, 1], [1, *column_bits]]
    table, entry, *early, inputs = first_part(
        me, tile_slot, tile_col, tile_id, touched, tiles, features, readers, orders, half, half, spans[:2]
    )
    later, first_kept, _ = other_parts(
        table, tiles, inputs, [(edges + half, half, spans[2:]), (0, half, spans[:1])]
    )
    away = [*early, *later]
    kept, token = other_parts(table, tiles, inputs, [(edges, half, spans[1:])])
    kept = [*first_kept, *kept]

    def chained(function, *operands):
        nonlocal token
        *results, token = function(token, *operands)
        return results

    def spread(held, size, lowest, axis):
        bit = size // 2
        while True:
            got = flip(held, bit, axis)
            yield
            if bit == lowest:
                return held, got
            (held,) = chained(join, held, got)
            bit //= 2

    choice = None

    def one_part(part):
        nonlocal choice
        first, *rest = orders[min(part, 1)]
        got = flip(away[part], first)
        yield
        total, sent = chained(combine, kept[part], got, weight)
        if part == 1:
            (choice,) = chained(read_choice, got, half * READ_CAP)
        for bit in rest:
            got = flip(sent, bit)
            yield
            total, *sent = chained(combine, total, got, weight)
            sent = sent[0] if sent else None
        held, got = yield from spread(total[None], feats, 1, "feat")
        (mixed,) = chained(mix, mine, offsets_of(feats, 1), held, got, weight)
        held, got = yield from spread(mixed, edges, 2, "edge")
        (picked,) = chained(pick, choice, held, got)
        far = flip(picked, 1)
        yield
        return held, got, far, spans[part]

    def links_of(bit):
        return {"x": 1.0} if bit == 1 else {"end": 1.0} if bit == 2 else {"end": 1.0, "middle": 2.0}

    feat_bits = [1 << i for i in reversed(range(feats.bit_length() - 1))]
    ways = []
    for part, (_, rows) in enumerate(spans):
        share = rows / block
        way = [(links_of(bit), share * half / (1 << n)) for n, bit in enumerate(orders[min(part, 1)])]
        way += [({"chip" if bit == 1 else "feat": 1.0}, share * (1.0 if bit > 1 else 0.3)) for bit in feat_bits]
        way += [(links_of(bit), share * half / bit) for bit in reversed(column_bits)]
        ways.append(way + [({"x": 1.0}, share * READ_CAP / blocks * half)])
    steps = [one_part(part) for part in range(len(spans))]
    for step in steps:
        next(step)
    known = sorted(ORDER) == [part for part, way in enumerate(ways) for _ in way]
    *order, last = ORDER if known else planned_order(ways)
    ended = []
    for part in order:
        try:
            next(steps[part])
        except StopIteration as end:
            ended.append(end.value)
            chained(touch, end.value[2])
    outputs = chained(lay_out, me, readers, entry, columns, ended, (), block)
    try:
        next(steps[last])
    except StopIteration as end:
        outputs = chained(lay_out, me, readers, entry, columns, [end.value], outputs, block)
    hidden, ghosts = outputs
    return hidden.reshape(blocks * block, width), ghosts.reshape(-1, width)


def solution(mesh):
    in_specs = (
        P("edge", "feat"),
        P("edge", None, None),
        P("edge"),
        P("edge"),
        P("edge"),
        P(),
        P(None, "feat"),
        P("edge"),
    )
    out_specs = (P("edge", "feat"), P("edge", "feat"))
    return jax.shard_map(local, mesh=mesh, in_specs=in_specs, out_specs=out_specs, check_vma=False)
```

```python
import jax
import jax.numpy as jnp
from jax import lax
from jax.experimental import pallas as pl
from jax.experimental.pallas import tpu as pltpu
from jax.sharding import PartitionSpec as P

SHARES = (2, 3, 2, 1)
ORDER = (
    0, 1, 0, 2, 0, 1, 3, 2, 1, 0, 0, 2, 1, 1, 0, 3, 2, 1, 0, 2, 3, 3, 2, 0, 3, 1, 3, 2, 3, 1, 2, 3,
)
READ_CAP = 2
VMEM_BYTES = 12 * 1024 * 1024
UNIT_TIME, START_TIME, STEP_TIME, LATENCY = 11.3, 0.9, 0.4, 0.6

SMEM = pl.BlockSpec(memory_space=pltpu.SMEM)
VMEM = pl.BlockSpec(memory_space=pltpu.VMEM)
HBM = pl.BlockSpec(memory_space=pltpu.HBM)
TOKEN = jax.ShapeDtypeStruct((8, 128), jnp.float32)


def call(body, out_shape, in_specs, out_specs, operands, scratch=(), aliases=None, limit=VMEM_BYTES):
    return pl.pallas_call(
        body,
        out_shape=out_shape,
        in_specs=in_specs,
        out_specs=out_specs,
        scratch_shapes=list(scratch),
        input_output_aliases=aliases or {},
        compiler_params=pltpu.CompilerParams(vmem_limit_bytes=limit),
        cost_estimate=pl.CostEstimate(flops=0, bytes_accessed=1, transcendentals=0),
    )(*operands)


def split(value, size):
    if size & (size - 1) == 0:
        return value >> (size.bit_length() - 1), value & (size - 1)
    return lax.div(value, size), lax.rem(value, size)


def place_of(peer, bits):
    place = 0
    for bit in bits:
        place = (place << 1) | ((peer >> (bit.bit_length() - 1)) & 1)
    return place


def planned_order(ways):
    now, order, flows, current, place = 0.0, [], [], {}, [0] * len(ways)

    def active():
        waiting = [f for f in flows if "x" in f["links"]][1:]
        running = [f for f in flows if not any(f is w for w in waiting)]
        load = {}
        for f in running:
            for link, weight in f["links"].items():
                load[link] = load.get(link, 0.0) + weight
        return [(f, min(1.0 / load[link] for link in f["links"])) for f in running]

    def advance(until):
        nonlocal now
        while now < until:
            running = active()
            step = min([until - now] + [f["left"] / rate for f, rate in running])
            now += max(step, 1e-3)
            for f, rate in running:
                f["left"] -= step * rate
                if f["left"] <= 1e-6:
                    f["end"] = now + LATENCY
            flows[:] = [f for f in flows if f["left"] > 1e-6]

    def begin(n):
        links, units = ways[n][place[n]]
        advance(now + START_TIME)
        current[n] = {"links": links, "left": units * UNIT_TIME, "end": None}
        flows.append(current[n])

    for n in range(len(ways)):
        begin(n)
    while current:
        ended = [(f["end"], n) for n, f in current.items() if f["end"] is not None and f["end"] <= now]
        if not ended:
            advance(now + 0.05)
            continue
        _, n = min(ended)
        order.append(n)
        del current[n]
        place[n] += 1
        advance(now + STEP_TIME)
        if place[n] < len(ways[n]):
            begin(n)
    return order


def offsets_of(size, lowest):
    offsets, bit = [0], size // 2
    while bit >= lowest:
        offsets += [offset | bit for offset in offsets]
        bit //= 2
    return offsets


def lay_tiles(table, base, tiles, lhs, spans, row_base, blocks, block, at=0):
    for b in range(blocks):
        for c in range(blocks):
            entry = table[base + b * blocks + c]
            tile = tiles[jnp.maximum(entry - 1, 0)]
            tile = jnp.where(entry > 0, tile, jnp.zeros_like(tile))
            top = at
            for first, rows in spans:
                lhs[pl.ds(top + b * rows, rows), pl.ds(c * block, block)] = tile[first - row_base : first - row_base + rows]
                top = top + blocks * rows


def first_part(me, slot, col, tile_id, touched, tiles, features, readers, orders, first, count, spans):
    block = tiles.shape[1]
    blocks = features.shape[0] // block
    width = features.shape[1]
    edges, cap = touched.shape[1], touched.shape[2]
    column_bits = [1 << i for i in range(1, edges.bit_length() - 1)]
    products = slot.shape[0]
    half = edges // 2
    loaded = sum(rows for _, rows in spans)
    tallest = max(rows for _, rows in spans)
    square = blocks * blocks

    listed = readers.shape[0]
    extra = -(-half * READ_CAP // 16) * 16
    shapes = [(count, blocks, rows, width) for _, rows in spans]
    shapes[1] = (count * blocks * spans[1][1] + extra, width)

    def body(me_ref, slot_hbm, col_hbm, id_hbm, touched_hbm, readers_hbm, tiles_hbm, x_hbm, *refs):
        table, entry, *outs = refs[: 2 + len(spans)]
        x_out, *scratch = refs[2 + len(spans) :]
        slot_ref, col_ref, id_ref, touched_ref, readers_ref, choice, tiles_ref, lhs, bases, seen, sems = scratch
        loads = [
            pltpu.make_async_copy(slot_hbm, slot_ref, sems.at[0]),
            pltpu.make_async_copy(col_hbm, col_ref, sems.at[1]),
            pltpu.make_async_copy(id_hbm, id_ref, sems.at[2]),
            pltpu.make_async_copy(touched_hbm.at[me_ref[0]], touched_ref, sems.at[5]),
            pltpu.make_async_copy(readers_hbm, readers_ref, sems.at[6]),
            pltpu.make_async_copy(x_hbm, x_out, sems.at[3]),
            pltpu.make_async_copy(tiles_hbm.at[:, pl.ds(0, loaded)], tiles_ref, sems.at[4]),
        ]
        for load in loads:
            load.start()

        def clear(i, carry):
            table[i] = 0
            return carry

        lax.fori_loop(0, len(orders) * edges * square, clear, 0, unroll=16)

        def place_slot(k, carry):
            owner, slot_at = split(k, cap)
            for n, order in enumerate(orders):
                place = place_of(owner ^ me_ref[0], order)
                bases[n * edges * cap + k] = ((n * edges + place) * blocks + touched_ref[slot_at, owner]) * blocks
            return carry

        for load in loads[:5]:
            load.wait()
        lax.fori_loop(0, edges * cap, place_slot, 0, unroll=8)

        for i in range(extra + 1):
            choice[i] = 0
        for i in range(edges * READ_CAP):
            entry[i] = -1
        for i in range(edges):
            seen[i] = 0

        def enter_lists(r, carry):
            owner, b = split(readers_ref[r], blocks)
            turn = seen[owner]
            seen[owner] = turn + 1
            turn = jnp.minimum(turn, READ_CAP - 1)
            entry[owner * READ_CAP + turn] = r
            peer = owner ^ me_ref[0] ^ 1
            row = place_of(peer, column_bits) * READ_CAP + turn
            choice[jnp.where(peer & 1 == 0, row, extra)] = b
            return carry

        lax.fori_loop(0, listed, enter_lists, 0)

        def enter(k, carry):
            for n in range(len(orders)):
                table[bases[n * edges * cap + slot_ref[k]] + col_ref[k]] = id_ref[k] + 1
            return carry

        lax.fori_loop(0, products, enter, 0, unroll=8)
        for load in loads[5:]:
            load.wait()

        for n, (span, out) in enumerate(zip(spans, outs)):
            height = blocks * span[1]

            def one_owner(i, carry):
                at = pl.multiple_of(i * height, height)
                base = (n * edges + first + i) * square
                lay_tiles(table, base, tiles_ref, lhs, [span], 0, blocks, block, at)
                return carry

            lax.fori_loop(0, count, one_owner, 0)
            total = jnp.dot(lhs[pl.ds(0, count * height)], x_out[...], preferred_element_type=jnp.float32)
            if n == 1:
                out[pl.ds(0, count * height)] = total.astype(jnp.bfloat16)
                for i in range(extra):
                    line = jnp.full((1, width), choice[i].astype(jnp.float32), jnp.float32)
                    out[pl.ds(count * height + i, 1)] = line.astype(jnp.bfloat16)
            else:
                out[...] = total.astype(jnp.bfloat16).reshape(out.shape)

    return call(
        body,
        [
            jax.ShapeDtypeStruct((len(orders) * edges * square,), jnp.int32),
            jax.ShapeDtypeStruct((edges * READ_CAP,), jnp.int32),
            *[jax.ShapeDtypeStruct(shape, jnp.bfloat16) for shape in shapes],
            jax.ShapeDtypeStruct(features.shape, jnp.bfloat16),
        ],
        [SMEM] + [HBM] * 7,
        [SMEM] * 2 + [VMEM] * (len(spans) + 1),
        (me, slot, col, tile_id, touched.transpose(0, 2, 1), readers, tiles, features),
        [
            pltpu.SMEM((products,), jnp.int32),
            pltpu.SMEM((products,), jnp.int32),
            pltpu.SMEM((products,), jnp.int32),
            pltpu.SMEM((cap, edges), jnp.int32),
            pltpu.SMEM((listed,), jnp.int32),
            pltpu.SMEM((extra + 1,), jnp.int32),
            pltpu.VMEM((tiles.shape[0], loaded, block), jnp.bfloat16),
            pltpu.VMEM((count * blocks * tallest, blocks * block), jnp.bfloat16),
            pltpu.SMEM((len(orders) * edges * cap,), jnp.int32),
            pltpu.SMEM((edges,), jnp.int32),
            pltpu.SemaphoreType.DMA((7,)),
        ],
        limit=62 * 1024 * 1024,
    )


def other_parts(table, tiles, inputs, jobs):
    block = tiles.shape[1]
    blocks = inputs.shape[0] // block
    width = inputs.shape[1]
    most = max(sum(rows for _, rows in spans) for _, _, spans in jobs) * blocks
    shapes = [
        jax.ShapeDtypeStruct((count, blocks, rows, width), jnp.bfloat16) for _, count, spans in jobs for _, rows in spans
    ]

    def body(table_ref, tiles_hbm, x_ref, *refs):
        outs = refs
        token, tiles_ref, lhs, sems = outs[-4:]
        token[...] = jnp.zeros_like(token)
        load = pltpu.make_async_copy(tiles_hbm, tiles_ref, sems.at[0])
        load.start()
        load.wait()
        for first, count, spans in jobs:
            height = blocks * sum(rows for _, rows in spans)

            def one_owner(i, carry):
                lay_tiles(table_ref, (first + i) * blocks * blocks, tiles_ref, lhs, spans, 0, blocks, block)
                total = jnp.dot(lhs[pl.ds(0, height)], x_ref[...], preferred_element_type=jnp.float32)
                total = total.astype(jnp.bfloat16)
                at = 0
                for out, (_, rows) in zip(outs, spans):
                    out[i] = total[at : at + blocks * rows].reshape(blocks, rows, width)
                    at += blocks * rows
                return carry

            lax.fori_loop(0, count, one_owner, 0)
            outs = outs[len(spans) :]

    results = call(
        body,
        shapes + [TOKEN],
        [SMEM, HBM, VMEM],
        [VMEM] * (len(shapes) + 1),
        (table, tiles, inputs),
        [
            pltpu.VMEM(tiles.shape, jnp.bfloat16),
            pltpu.VMEM((most, blocks * block), jnp.bfloat16),
            pltpu.SemaphoreType.DMA((1,)),
        ],
    )
    grouped, at = [], 0
    for _, _, spans in jobs:
        grouped.append(results[at : at + len(spans)])
        at += len(spans)
    return (*grouped, results[-1])


def combine(token, total, got, at_hand):
    count, *shape = total.shape
    left = count // 2

    def body(token_ref, total_ref, got_ref, at_hand_ref, *outs):
        def add(i, carry):
            if got.ndim == total.ndim:
                value = got_ref[i]
            else:
                height = shape[0] * shape[1]
                value = got_ref[pl.ds(pl.multiple_of(i * height, height), height)].reshape(shape)
            value = total_ref[i].astype(jnp.float32) + value.astype(jnp.float32)
            if not left:
                outs[0][...] = value.astype(jnp.bfloat16)
            else:

                @pl.when(i < left)
                def _():
                    outs[0][jnp.minimum(i, left - 1)] = value

                @pl.when(i >= left)
                def _():
                    outs[1][jnp.maximum(i - left, 0)] = value.astype(jnp.bfloat16)

            return carry

        lax.fori_loop(0, count, add, 0)
        outs[-1][...] = token_ref[...]

    if left:
        out_shape = [
            jax.ShapeDtypeStruct((left, *shape), jnp.float32),
            jax.ShapeDtypeStruct((count - left, *shape), jnp.bfloat16),
        ]
    else:
        out_shape = [jax.ShapeDtypeStruct(tuple(shape), jnp.bfloat16)]
    out_shape.append(TOKEN)
    return call(body, out_shape, [VMEM] * 4, [VMEM] * len(out_shape), (token, total, got, at_hand))


def join(token, held, got):
    def body(token_ref, held_ref, got_ref, out, token_out):
        out[pl.ds(0, held.shape[0])] = held_ref[...]
        out[pl.ds(held.shape[0], got.shape[0])] = got_ref[...]
        token_out[...] = token_ref[...]

    both = jax.ShapeDtypeStruct((held.shape[0] + got.shape[0], *held.shape[1:]), held.dtype)
    return call(body, [both, TOKEN], [VMEM] * 3, [VMEM] * 2, (token, held, got))


def mix(token, mine, offsets, held, got, weight):
    _, blocks, rows, depth = held.shape
    width = weight.shape[1]

    def body(token_ref, mine_ref, held_ref, got_ref, w_ref, out_ref, token_out):
        total = jnp.zeros((blocks * rows, width), jnp.float32)
        for n, offset in enumerate(offsets):
            piece = (held_ref if n < held.shape[0] else got_ref)[n % held.shape[0]]
            at = pl.multiple_of((mine_ref[0] ^ offset) * depth, depth)
            total += jnp.dot(
                piece.reshape(blocks * rows, depth), w_ref[pl.ds(at, depth)], preferred_element_type=jnp.float32
            )
        out_ref[0] = jnp.maximum(total, 0.0).astype(jnp.bfloat16).reshape(blocks, rows, width)
        token_out[...] = token_ref[...]

    return call(
        body,
        [jax.ShapeDtypeStruct((1, blocks, rows, width), jnp.bfloat16), TOKEN],
        [VMEM, SMEM, VMEM, VMEM, VMEM],
        [VMEM] * 2,
        (token, mine, held, got, weight),
    )


def pick(token, choice, held, got):
    count = 2 * held.shape[0] * READ_CAP

    def body(token_ref, choice_ref, held_ref, got_ref, out, token_out):
        for i in range(count):
            n = i // READ_CAP
            source = held_ref if n < held.shape[0] else got_ref
            out[i] = source[n % held.shape[0], choice_ref[i]]
        token_out[...] = token_ref[...]

    return call(
        body,
        [jax.ShapeDtypeStruct((count, *held.shape[2:]), held.dtype), TOKEN],
        [VMEM, SMEM, VMEM, VMEM],
        [VMEM] * 2,
        (token, choice, held, got),
    )


def read_choice(token, got, count):
    extra = -(-count // 16) * 16
    first = got.shape[0] - extra

    def body(token_ref, got_ref, choice, token_out):
        lines = got_ref[pl.ds(first, extra)].astype(jnp.float32)
        for i in range(count):
            choice[i] = jnp.max(lines[i : i + 1]).astype(jnp.int32)
        token_out[...] = token_ref[...]

    return call(
        body, [jax.ShapeDtypeStruct((count,), jnp.int32), TOKEN], [VMEM] * 2, [SMEM, VMEM], (token, got)
    )


def touch(token, value):
    def body(token_ref, value_ref, token_out):
        token_out[...] = token_ref[...]

    return call(body, [TOKEN], [VMEM] * 2, [VMEM], (token, value))


def lay_out(token, me, readers, entry, offsets, nears, fars, outputs, block):
    count = readers.shape[0]
    width = fars[0][0].shape[2]
    blocks = outputs[0].shape[0] if outputs else nears[0][0].shape[1]
    slots = len(offsets) * READ_CAP
    arrays = [array for held, got, _ in nears for array in (held, got)] + [far for far, _ in fars]

    def body(token_ref, me_ref, readers_ref, entry_ref, *refs):
        hidden_ref, ghost_ref, token_out, near_sems, far_sems = refs[-5:]
        near_refs, far_refs = refs[: 2 * len(nears)], refs[2 * len(nears) : len(arrays)]

        def each(act):
            for number, (held, _, span) in enumerate(nears):
                held_ref, got_ref = near_refs[2 * number : 2 * number + 2]
                part = pl.ds(*span)
                act(pltpu.make_async_copy(held_ref.at[0], hidden_ref.at[:, part], near_sems.at[number, slots]))
                for i in range(slots):
                    n, j = i // READ_CAP, i % READ_CAP
                    listed = entry_ref[(me_ref[0] ^ offsets[n]) * READ_CAP + j]
                    source = held_ref if n < held.shape[0] else got_ref
                    row = n % held.shape[0]

                    @pl.when(listed >= 0)
                    def _():
                        _, b = split(readers_ref[listed], blocks)
                        target = ghost_ref.at[listed, part]
                        act(pltpu.make_async_copy(source.at[row, b], target, near_sems.at[number, i]))

            for number, (_, span) in enumerate(fars):
                part = pl.ds(*span)
                for i in range(slots):
                    n, j = i // READ_CAP, i % READ_CAP
                    listed = entry_ref[(me_ref[0] ^ 1 ^ offsets[n]) * READ_CAP + j]

                    @pl.when(listed >= 0)
                    def _():
                        target = ghost_ref.at[listed, part]
                        act(pltpu.make_async_copy(far_refs[number].at[i], target, far_sems.at[number, i]))

        each(lambda copy: copy.start())
        token_out[...] = token_ref[...]
        each(lambda copy: copy.wait())

    operands = (token, me, readers, entry, *arrays, *outputs)
    return call(
        body,
        [
            jax.ShapeDtypeStruct((blocks, block, width), jnp.bfloat16),
            jax.ShapeDtypeStruct((count, block, width), jnp.bfloat16),
            TOKEN,
        ],
        [VMEM] + [SMEM] * 3 + [VMEM] * len(arrays) + [HBM] * len(outputs),
        [HBM, HBM, VMEM],
        operands,
        [
            pltpu.SemaphoreType.DMA((max(len(nears), 1), slots + 1)),
            pltpu.SemaphoreType.DMA((len(fars), slots)),
        ],
        aliases={len(operands) - 2: 0, len(operands) - 1: 1} if outputs else None,
    )


def local(features, tiles, tile_slot, tile_col, tile_id, touched, weight, readers):
    edges, feats = lax.axis_size("edge"), lax.axis_size("feat")
    half = edges // 2
    me, mine = lax.axis_index("edge"), lax.axis_index("feat")
    block = tiles.shape[1]
    blocks = features.shape[0] // block
    width = features.shape[1]
    unit = block // sum(SHARES)
    spans = [(sum(SHARES[:i]) * unit, share * unit) for i, share in enumerate(SHARES)]

    def flip(value, bit, axis="edge"):
        return lax.ppermute(value, axis, [(d, d ^ bit) for d in range(lax.axis_size(axis))])

    columns = offsets_of(edges, 2)
    me, mine = me.reshape(1), mine.reshape(1)
    column_bits = [1 << i for i in range(1, edges.bit_length() - 1)]
    orders = [[*column_bits, 1], [1, *column_bits]]
    table, entry, *early, inputs = first_part(
        me, tile_slot, tile_col, tile_id, touched, tiles, features, readers, orders, half, half, spans[:2]
    )
    later, first_kept, _ = other_parts(
        table, tiles, inputs, [(edges + half, half, spans[2:]), (0, half, spans[:1])]
    )
    away = [*early, *later]
    kept, token = other_parts(table, tiles, inputs, [(edges, half, spans[1:])])
    kept = [*first_kept, *kept]

    def chained(function, *operands):
        nonlocal token
        *results, token = function(token, *operands)
        return results

    def spread(held, size, lowest, axis):
        bit = size // 2
        while True:
            got = flip(held, bit, axis)
            yield
            if bit == lowest:
                return held, got
            (held,) = chained(join, held, got)
            bit //= 2

    choice, nears, fars = None, [], []
    ended = object()

    def one_part(part):
        nonlocal choice
        first, *rest = orders[min(part, 1)]
        got = flip(away[part], first)
        yield
        total, sent = chained(combine, kept[part], got, weight)
        if part == 1:
            (choice,) = chained(read_choice, got, half * READ_CAP)
        for bit in rest:
            got = flip(sent, bit)
            yield
            total, *sent = chained(combine, total, got, weight)
            sent = sent[0] if sent else None
        held, got = yield from spread(total[None], feats, 1, "feat")
        (mixed,) = chained(mix, mine, offsets_of(feats, 1), held, got, weight)
        held, got = yield from spread(mixed, edges, 2, "edge")
        (picked,) = chained(pick, choice, held, got)
        nears.append((held, got, spans[part]))
        far = flip(picked, 1)
        yield
        fars.append((far, spans[part]))

    def links_of(bit):
        return {"x": 1.0} if bit == 1 else {"end": 1.0} if bit == 2 else {"end": 1.0, "middle": 2.0}

    feat_bits = [1 << i for i in reversed(range(feats.bit_length() - 1))]
    ways = []
    for part, (_, rows) in enumerate(spans):
        share = rows / block
        way = [(links_of(bit), share * half / (1 << n)) for n, bit in enumerate(orders[min(part, 1)])]
        way += [({"chip" if bit == 1 else "feat": 1.0}, share * (1.0 if bit > 1 else 0.3)) for bit in feat_bits]
        way += [(links_of(bit), share * half / bit) for bit in reversed(column_bits)]
        ways.append(way + [({"x": 1.0}, share * READ_CAP / blocks * half)])
    steps = [one_part(part) for part in range(len(spans))]
    for step in steps:
        next(step)
    known = sorted(ORDER) == [part for part, way in enumerate(ways) for _ in way]
    *order, last = ORDER if known else planned_order(ways)
    for part in order:
        if next(steps[part], ended) is ended:
            chained(touch, fars[-1][0])
    outputs = chained(lay_out, me, readers, entry, columns, nears, fars, (), block)
    next(steps[last], None)
    outputs = chained(lay_out, me, readers, entry, columns, [], fars[-1:], outputs, block)
    hidden, ghosts = outputs
    return hidden.reshape(blocks * block, width), ghosts.reshape(-1, width)


def solution(mesh):
    in_specs = (
        P("edge", "feat"),
        P("edge", None, None),
        P("edge"),
        P("edge"),
        P("edge"),
        P(),
        P(None, "feat"),
        P("edge"),
    )
    out_specs = (P("edge", "feat"), P("edge", "feat"))
    return jax.shard_map(local, mesh=mesh, in_specs=in_specs, out_specs=out_specs, check_vma=False)
```

```python
import jax
import jax.numpy as jnp
from jax import lax
from jax.experimental import pallas as pl
from jax.experimental.pallas import tpu as pltpu
from jax.sharding import PartitionSpec as P

SHARES = (2, 2, 2, 1, 1)
ORDER = (
    0, 1, 2, 0, 1, 4, 2, 3, 1, 0, 3, 2, 3, 0, 4, 1, 0, 2, 1, 4, 4, 0, 3, 1, 2, 0, 2, 3, 1, 3, 4, 0,
    2, 4, 3, 1, 4, 2, 3, 4,
)
READ_CAP = 2
VMEM_BYTES = 12 * 1024 * 1024
UNIT_TIME, START_TIME, STEP_TIME, LATENCY = 11.3, 0.9, 0.4, 0.6

SMEM = pl.BlockSpec(memory_space=pltpu.SMEM)
VMEM = pl.BlockSpec(memory_space=pltpu.VMEM)
HBM = pl.BlockSpec(memory_space=pltpu.HBM)
TOKEN = jax.ShapeDtypeStruct((8, 128), jnp.float32)


def call(body, out_shape, in_specs, out_specs, operands, scratch=(), aliases=None, limit=VMEM_BYTES):
    return pl.pallas_call(
        body,
        out_shape=out_shape,
        in_specs=in_specs,
        out_specs=out_specs,
        scratch_shapes=list(scratch),
        input_output_aliases=aliases or {},
        compiler_params=pltpu.CompilerParams(vmem_limit_bytes=limit),
        cost_estimate=pl.CostEstimate(flops=0, bytes_accessed=1, transcendentals=0),
    )(*operands)


def split(value, size):
    if size & (size - 1) == 0:
        return value >> (size.bit_length() - 1), value & (size - 1)
    return lax.div(value, size), lax.rem(value, size)


def place_of(peer, bits):
    place = 0
    for bit in bits:
        place = (place << 1) | ((peer >> (bit.bit_length() - 1)) & 1)
    return place


def planned_order(ways):
    now, order, flows, current, place = 0.0, [], [], {}, [0] * len(ways)

    def active():
        waiting = [f for f in flows if "x" in f["links"]][1:]
        running = [f for f in flows if not any(f is w for w in waiting)]
        load = {}
        for f in running:
            for link, weight in f["links"].items():
                load[link] = load.get(link, 0.0) + weight
        return [(f, min(1.0 / load[link] for link in f["links"])) for f in running]

    def advance(until):
        nonlocal now
        while now < until:
            running = active()
            step = min([until - now] + [f["left"] / rate for f, rate in running])
            now += max(step, 1e-3)
            for f, rate in running:
                f["left"] -= step * rate
                if f["left"] <= 1e-6:
                    f["end"] = now + LATENCY
            flows[:] = [f for f in flows if f["left"] > 1e-6]

    def begin(n):
        links, units = ways[n][place[n]]
        advance(now + START_TIME)
        current[n] = {"links": links, "left": units * UNIT_TIME, "end": None}
        flows.append(current[n])

    for n in range(len(ways)):
        begin(n)
    while current:
        ended = [(f["end"], n) for n, f in current.items() if f["end"] is not None and f["end"] <= now]
        if not ended:
            advance(now + 0.05)
            continue
        _, n = min(ended)
        order.append(n)
        del current[n]
        place[n] += 1
        advance(now + STEP_TIME)
        if place[n] < len(ways[n]):
            begin(n)
    return order


def offsets_of(size, lowest):
    offsets, bit = [0], size // 2
    while bit >= lowest:
        offsets += [offset | bit for offset in offsets]
        bit //= 2
    return offsets


def lay_tiles(table, base, tiles, lhs, spans, row_base, blocks, block, at=0):
    for b in range(blocks):
        for c in range(blocks):
            entry = table[base + b * blocks + c]
            tile = tiles[jnp.maximum(entry - 1, 0)]
            tile = jnp.where(entry > 0, tile, jnp.zeros_like(tile))
            top = at
            for first, rows in spans:
                lhs[pl.ds(top + b * rows, rows), pl.ds(c * block, block)] = tile[first - row_base : first - row_base + rows]
                top = top + blocks * rows


def first_part(me, slot, col, tile_id, touched, tiles, features, readers, orders, first, count, spans):
    block = tiles.shape[1]
    blocks = features.shape[0] // block
    width = features.shape[1]
    edges, cap = touched.shape[1], touched.shape[2]
    column_bits = [1 << i for i in range(1, edges.bit_length() - 1)]
    products = slot.shape[0]
    half = edges // 2
    loaded = sum(rows for _, rows in spans)
    tallest = max(rows for _, rows in spans)
    square = blocks * blocks

    listed = readers.shape[0]
    extra = -(-half * READ_CAP // 16) * 16
    shapes = [(count, blocks, rows, width) for _, rows in spans]
    shapes[1] = (count * blocks * spans[1][1] + extra, width)

    def body(me_ref, slot_hbm, col_hbm, id_hbm, touched_hbm, readers_hbm, tiles_hbm, x_hbm, *refs):
        table, entry, *outs = refs[: 2 + len(spans)]
        x_out, *scratch = refs[2 + len(spans) :]
        slot_ref, col_ref, id_ref, touched_ref, readers_ref, choice, tiles_ref, lhs, bases, seen, sems = scratch
        loads = [
            pltpu.make_async_copy(slot_hbm, slot_ref, sems.at[0]),
            pltpu.make_async_copy(col_hbm, col_ref, sems.at[1]),
            pltpu.make_async_copy(id_hbm, id_ref, sems.at[2]),
            pltpu.make_async_copy(touched_hbm.at[me_ref[0]], touched_ref, sems.at[5]),
            pltpu.make_async_copy(readers_hbm, readers_ref, sems.at[6]),
            pltpu.make_async_copy(x_hbm, x_out, sems.at[3]),
            pltpu.make_async_copy(tiles_hbm.at[:, pl.ds(0, loaded)], tiles_ref, sems.at[4]),
        ]
        for load in loads:
            load.start()

        def clear(i, carry):
            table[i] = 0
            return carry

        lax.fori_loop(0, len(orders) * edges * square, clear, 0, unroll=16)

        def place_slot(k, carry):
            owner, slot_at = split(k, cap)
            for n, order in enumerate(orders):
                place = place_of(owner ^ me_ref[0], order)
                bases[n * edges * cap + k] = ((n * edges + place) * blocks + touched_ref[slot_at, owner]) * blocks
            return carry

        for load in loads[:5]:
            load.wait()
        lax.fori_loop(0, edges * cap, place_slot, 0, unroll=8)

        for i in range(extra + 1):
            choice[i] = 0
        for i in range(edges * READ_CAP):
            entry[i] = -1
        for i in range(edges):
            seen[i] = 0

        def enter_lists(r, carry):
            owner, b = split(readers_ref[r], blocks)
            turn = seen[owner]
            seen[owner] = turn + 1
            turn = jnp.minimum(turn, READ_CAP - 1)
            entry[owner * READ_CAP + turn] = r
            peer = owner ^ me_ref[0] ^ 1
            row = place_of(peer, column_bits) * READ_CAP + turn
            choice[jnp.where(peer & 1 == 0, row, extra)] = b
            return carry

        lax.fori_loop(0, listed, enter_lists, 0)

        def enter(k, carry):
            for n in range(len(orders)):
                table[bases[n * edges * cap + slot_ref[k]] + col_ref[k]] = id_ref[k] + 1
            return carry

        lax.fori_loop(0, products, enter, 0, unroll=8)
        for load in loads[5:]:
            load.wait()

        for n, (span, out) in enumerate(zip(spans, outs)):
            height = blocks * span[1]

            def one_owner(i, carry):
                at = pl.multiple_of(i * height, height)
                base = (n * edges + first + i) * square
                lay_tiles(table, base, tiles_ref, lhs, [span], 0, blocks, block, at)
                return carry

            lax.fori_loop(0, count, one_owner, 0)
            total = jnp.dot(lhs[pl.ds(0, count * height)], x_out[...], preferred_element_type=jnp.float32)
            if n == 1:
                out[pl.ds(0, count * height)] = total.astype(jnp.bfloat16)
                for i in range(extra):
                    line = jnp.full((1, width), choice[i].astype(jnp.float32), jnp.float32)
                    out[pl.ds(count * height + i, 1)] = line.astype(jnp.bfloat16)
            else:
                out[...] = total.astype(jnp.bfloat16).reshape(out.shape)

    return call(
        body,
        [
            jax.ShapeDtypeStruct((len(orders) * edges * square,), jnp.int32),
            jax.ShapeDtypeStruct((edges * READ_CAP,), jnp.int32),
            *[jax.ShapeDtypeStruct(shape, jnp.bfloat16) for shape in shapes],
            jax.ShapeDtypeStruct(features.shape, jnp.bfloat16),
        ],
        [SMEM] + [HBM] * 7,
        [SMEM] * 2 + [VMEM] * (len(spans) + 1),
        (me, slot, col, tile_id, touched.transpose(0, 2, 1), readers, tiles, features),
        [
            pltpu.SMEM((products,), jnp.int32),
            pltpu.SMEM((products,), jnp.int32),
            pltpu.SMEM((products,), jnp.int32),
            pltpu.SMEM((cap, edges), jnp.int32),
            pltpu.SMEM((listed,), jnp.int32),
            pltpu.SMEM((extra + 1,), jnp.int32),
            pltpu.VMEM((tiles.shape[0], loaded, block), jnp.bfloat16),
            pltpu.VMEM((count * blocks * tallest, blocks * block), jnp.bfloat16),
            pltpu.SMEM((len(orders) * edges * cap,), jnp.int32),
            pltpu.SMEM((edges,), jnp.int32),
            pltpu.SemaphoreType.DMA((7,)),
        ],
        limit=62 * 1024 * 1024,
    )


def other_parts(table, tiles, inputs, jobs):
    block = tiles.shape[1]
    blocks = inputs.shape[0] // block
    width = inputs.shape[1]
    most = max(sum(rows for _, rows in spans) for _, _, spans in jobs) * blocks
    shapes = [
        jax.ShapeDtypeStruct((count, blocks, rows, width), jnp.bfloat16) for _, count, spans in jobs for _, rows in spans
    ]

    def body(table_ref, tiles_hbm, x_ref, *refs):
        outs = refs
        token, tiles_ref, lhs, sems = outs[-4:]
        token[...] = jnp.zeros_like(token)
        load = pltpu.make_async_copy(tiles_hbm, tiles_ref, sems.at[0])
        load.start()
        load.wait()
        for first, count, spans in jobs:
            height = blocks * sum(rows for _, rows in spans)

            def one_owner(i, carry):
                lay_tiles(table_ref, (first + i) * blocks * blocks, tiles_ref, lhs, spans, 0, blocks, block)
                total = jnp.dot(lhs[pl.ds(0, height)], x_ref[...], preferred_element_type=jnp.float32)
                total = total.astype(jnp.bfloat16)
                at = 0
                for out, (_, rows) in zip(outs, spans):
                    out[i] = total[at : at + blocks * rows].reshape(blocks, rows, width)
                    at += blocks * rows
                return carry

            lax.fori_loop(0, count, one_owner, 0)
            outs = outs[len(spans) :]

    results = call(
        body,
        shapes + [TOKEN],
        [SMEM, HBM, VMEM],
        [VMEM] * (len(shapes) + 1),
        (table, tiles, inputs),
        [
            pltpu.VMEM(tiles.shape, jnp.bfloat16),
            pltpu.VMEM((most, blocks * block), jnp.bfloat16),
            pltpu.SemaphoreType.DMA((1,)),
        ],
    )
    grouped, at = [], 0
    for _, _, spans in jobs:
        grouped.append(results[at : at + len(spans)])
        at += len(spans)
    return (*grouped, results[-1])


def combine(token, total, got, at_hand):
    count, *shape = total.shape
    left = count // 2

    def body(token_ref, total_ref, got_ref, at_hand_ref, *outs):
        def add(i, carry):
            if got.ndim == total.ndim:
                value = got_ref[i]
            else:
                height = shape[0] * shape[1]
                value = got_ref[pl.ds(pl.multiple_of(i * height, height), height)].reshape(shape)
            value = total_ref[i].astype(jnp.float32) + value.astype(jnp.float32)
            if not left:
                outs[0][...] = value.astype(jnp.bfloat16)
            else:

                @pl.when(i < left)
                def _():
                    outs[0][jnp.minimum(i, left - 1)] = value

                @pl.when(i >= left)
                def _():
                    outs[1][jnp.maximum(i - left, 0)] = value.astype(jnp.bfloat16)

            return carry

        lax.fori_loop(0, count, add, 0)
        outs[-1][...] = token_ref[...]

    if left:
        out_shape = [
            jax.ShapeDtypeStruct((left, *shape), jnp.float32),
            jax.ShapeDtypeStruct((count - left, *shape), jnp.bfloat16),
        ]
    else:
        out_shape = [jax.ShapeDtypeStruct(tuple(shape), jnp.bfloat16)]
    out_shape.append(TOKEN)
    return call(body, out_shape, [VMEM] * 4, [VMEM] * len(out_shape), (token, total, got, at_hand))


def join(token, held, got):
    def body(token_ref, held_ref, got_ref, out, token_out):
        out[pl.ds(0, held.shape[0])] = held_ref[...]
        out[pl.ds(held.shape[0], got.shape[0])] = got_ref[...]
        token_out[...] = token_ref[...]

    both = jax.ShapeDtypeStruct((held.shape[0] + got.shape[0], *held.shape[1:]), held.dtype)
    return call(body, [both, TOKEN], [VMEM] * 3, [VMEM] * 2, (token, held, got))


def mix(token, mine, offsets, held, got, weight):
    _, blocks, rows, depth = held.shape
    width = weight.shape[1]

    def body(token_ref, mine_ref, held_ref, got_ref, w_ref, out_ref, token_out):
        total = jnp.zeros((blocks * rows, width), jnp.float32)
        for n, offset in enumerate(offsets):
            piece = (held_ref if n < held.shape[0] else got_ref)[n % held.shape[0]]
            at = pl.multiple_of((mine_ref[0] ^ offset) * depth, depth)
            total += jnp.dot(
                piece.reshape(blocks * rows, depth), w_ref[pl.ds(at, depth)], preferred_element_type=jnp.float32
            )
        out_ref[0] = jnp.maximum(total, 0.0).astype(jnp.bfloat16).reshape(blocks, rows, width)
        token_out[...] = token_ref[...]

    return call(
        body,
        [jax.ShapeDtypeStruct((1, blocks, rows, width), jnp.bfloat16), TOKEN],
        [VMEM, SMEM, VMEM, VMEM, VMEM],
        [VMEM] * 2,
        (token, mine, held, got, weight),
    )


def pick(token, choice, held, got):
    count = 2 * held.shape[0] * READ_CAP

    def body(token_ref, choice_ref, held_ref, got_ref, out, token_out):
        for i in range(count):
            n = i // READ_CAP
            source = held_ref if n < held.shape[0] else got_ref
            out[i] = source[n % held.shape[0], choice_ref[i]]
        token_out[...] = token_ref[...]

    return call(
        body,
        [jax.ShapeDtypeStruct((count, *held.shape[2:]), held.dtype), TOKEN],
        [VMEM, SMEM, VMEM, VMEM],
        [VMEM] * 2,
        (token, choice, held, got),
    )


def read_choice(token, got, count):
    extra = -(-count // 16) * 16
    first = got.shape[0] - extra

    def body(token_ref, got_ref, choice, token_out):
        lines = got_ref[pl.ds(first, extra)].astype(jnp.float32)
        for i in range(count):
            choice[i] = jnp.max(lines[i : i + 1]).astype(jnp.int32)
        token_out[...] = token_ref[...]

    return call(
        body, [jax.ShapeDtypeStruct((count,), jnp.int32), TOKEN], [VMEM] * 2, [SMEM, VMEM], (token, got)
    )


def touch(token, value):
    def body(token_ref, value_ref, token_out):
        token_out[...] = token_ref[...]

    return call(body, [TOKEN], [VMEM] * 2, [VMEM], (token, value))


def lay_out(token, me, readers, entry, offsets, nears, fars, outputs, block):
    count = readers.shape[0]
    width = fars[0][0].shape[2]
    blocks = outputs[0].shape[0] if outputs else nears[0][0].shape[1]
    slots = len(offsets) * READ_CAP
    arrays = [array for held, got, _ in nears for array in (held, got)] + [far for far, _ in fars]

    def body(token_ref, me_ref, readers_ref, entry_ref, *refs):
        hidden_ref, ghost_ref, token_out, near_sems, far_sems = refs[-5:]
        near_refs, far_refs = refs[: 2 * len(nears)], refs[2 * len(nears) : len(arrays)]

        def each(act):
            for number, (held, _, span) in enumerate(nears):
                held_ref, got_ref = near_refs[2 * number : 2 * number + 2]
                part = pl.ds(*span)
                act(pltpu.make_async_copy(held_ref.at[0], hidden_ref.at[:, part], near_sems.at[number, slots]))
                for i in range(slots):
                    n, j = i // READ_CAP, i % READ_CAP
                    listed = entry_ref[(me_ref[0] ^ offsets[n]) * READ_CAP + j]
                    source = held_ref if n < held.shape[0] else got_ref
                    row = n % held.shape[0]

                    @pl.when(listed >= 0)
                    def _():
                        _, b = split(readers_ref[listed], blocks)
                        target = ghost_ref.at[listed, part]
                        act(pltpu.make_async_copy(source.at[row, b], target, near_sems.at[number, i]))

            for number, (_, span) in enumerate(fars):
                part = pl.ds(*span)
                for i in range(slots):
                    n, j = i // READ_CAP, i % READ_CAP
                    listed = entry_ref[(me_ref[0] ^ 1 ^ offsets[n]) * READ_CAP + j]

                    @pl.when(listed >= 0)
                    def _():
                        target = ghost_ref.at[listed, part]
                        act(pltpu.make_async_copy(far_refs[number].at[i], target, far_sems.at[number, i]))

        each(lambda copy: copy.start())
        token_out[...] = token_ref[...]
        each(lambda copy: copy.wait())

    operands = (token, me, readers, entry, *arrays, *outputs)
    return call(
        body,
        [
            jax.ShapeDtypeStruct((blocks, block, width), jnp.bfloat16),
            jax.ShapeDtypeStruct((count, block, width), jnp.bfloat16),
            TOKEN,
        ],
        [VMEM] + [SMEM] * 3 + [VMEM] * len(arrays) + [HBM] * len(outputs),
        [HBM, HBM, VMEM],
        operands,
        [
            pltpu.SemaphoreType.DMA((max(len(nears), 1), slots + 1)),
            pltpu.SemaphoreType.DMA((len(fars), slots)),
        ],
        aliases={len(operands) - 2: 0, len(operands) - 1: 1} if outputs else None,
    )


def local(features, tiles, tile_slot, tile_col, tile_id, touched, weight, readers):
    edges, feats = lax.axis_size("edge"), lax.axis_size("feat")
    half = edges // 2
    me, mine = lax.axis_index("edge"), lax.axis_index("feat")
    block = tiles.shape[1]
    blocks = features.shape[0] // block
    width = features.shape[1]
    unit = block // sum(SHARES)
    spans = [(sum(SHARES[:i]) * unit, share * unit) for i, share in enumerate(SHARES)]

    def flip(value, bit, axis="edge"):
        return lax.ppermute(value, axis, [(d, d ^ bit) for d in range(lax.axis_size(axis))])

    columns = offsets_of(edges, 2)
    me, mine = me.reshape(1), mine.reshape(1)
    column_bits = [1 << i for i in range(1, edges.bit_length() - 1)]
    orders = [[*column_bits, 1], [1, *column_bits]]
    table, entry, *early, inputs = first_part(
        me, tile_slot, tile_col, tile_id, touched, tiles, features, readers, orders, half, half, spans[:2]
    )
    later, first_kept, _ = other_parts(
        table, tiles, inputs, [(edges + half, half, spans[2:]), (0, half, spans[:1])]
    )
    away = [*early, *later]
    kept, token = other_parts(table, tiles, inputs, [(edges, half, spans[1:])])
    kept = [*first_kept, *kept]

    def chained(function, *operands):
        nonlocal token
        *results, token = function(token, *operands)
        return results

    def spread(held, size, lowest, axis):
        bit = size // 2
        while True:
            got = flip(held, bit, axis)
            yield
            if bit == lowest:
                return held, got
            (held,) = chained(join, held, got)
            bit //= 2

    choice, nears, fars = None, [], []
    ended = object()

    def one_part(part):
        nonlocal choice
        first, *rest = orders[min(part, 1)]
        got = flip(away[part], first)
        yield
        total, sent = chained(combine, kept[part], got, weight)
        if part == 1:
            (choice,) = chained(read_choice, got, half * READ_CAP)
        for bit in rest:
            got = flip(sent, bit)
            yield
            total, *sent = chained(combine, total, got, weight)
            sent = sent[0] if sent else None
        held, got = yield from spread(total[None], feats, 1, "feat")
        (mixed,) = chained(mix, mine, offsets_of(feats, 1), held, got, weight)
        held, got = yield from spread(mixed, edges, 2, "edge")
        (picked,) = chained(pick, choice, held, got)
        nears.append((held, got, spans[part]))
        far = flip(picked, 1)
        yield
        fars.append((far, spans[part]))

    def links_of(bit):
        return {"x": 1.0} if bit == 1 else {"end": 1.0} if bit == 2 else {"end": 1.0, "middle": 2.0}

    feat_bits = [1 << i for i in reversed(range(feats.bit_length() - 1))]
    ways = []
    for part, (_, rows) in enumerate(spans):
        share = rows / block
        way = [(links_of(bit), share * half / (1 << n)) for n, bit in enumerate(orders[min(part, 1)])]
        way += [({"chip" if bit == 1 else "feat": 1.0}, share * (1.0 if bit > 1 else 0.3)) for bit in feat_bits]
        way += [(links_of(bit), share * half / bit) for bit in reversed(column_bits)]
        ways.append(way + [({"x": 1.0}, share * READ_CAP / blocks * half)])
    steps = [one_part(part) for part in range(len(spans))]
    for step in steps:
        next(step)
    known = sorted(ORDER) == [part for part, way in enumerate(ways) for _ in way]
    *order, last = ORDER if known else planned_order(ways)
    for part in order:
        if next(steps[part], ended) is ended:
            chained(touch, fars[-1][0])
    outputs = chained(lay_out, me, readers, entry, columns, nears, fars, (), block)
    next(steps[last], None)
    outputs = chained(lay_out, me, readers, entry, columns, [], fars[-1:], outputs, block)
    hidden, ghosts = outputs
    return hidden.reshape(blocks * block, width), ghosts.reshape(-1, width)


def solution(mesh):
    in_specs = (
        P("edge", "feat"),
        P("edge", None, None),
        P("edge"),
        P("edge"),
        P("edge"),
        P(),
        P(None, "feat"),
        P("edge"),
    )
    out_specs = (P("edge", "feat"), P("edge", "feat"))
    return jax.shard_map(local, mesh=mesh, in_specs=in_specs, out_specs=out_specs, check_vma=False)
```

```python
import jax
import jax.numpy as jnp
from jax import lax
from jax.experimental import pallas as pl
from jax.experimental.pallas import tpu as pltpu
from jax.sharding import PartitionSpec as P

SHARES = (2, 2, 2, 1, 1)
ORDER = (
    0, 1, 2, 0, 1, 2, 1, 3, 4, 0, 2, 1, 1, 4, 1, 2, 3, 4, 0, 2, 0, 3, 3, 2, 4, 1, 0, 4, 2, 4, 3, 1,
    0, 3, 4, 2, 3, 0, 4, 3,
)
READ_CAP = 2
VMEM_BYTES = 12 * 1024 * 1024
UNIT_TIME, START_TIME, STEP_TIME, LATENCY = 11.3, 0.9, 0.4, 0.6

SMEM = pl.BlockSpec(memory_space=pltpu.SMEM)
VMEM = pl.BlockSpec(memory_space=pltpu.VMEM)
HBM = pl.BlockSpec(memory_space=pltpu.HBM)
TOKEN = jax.ShapeDtypeStruct((8, 128), jnp.float32)


def call(body, out_shape, in_specs, out_specs, operands, scratch=(), aliases=None, limit=VMEM_BYTES):
    return pl.pallas_call(
        body,
        out_shape=out_shape,
        in_specs=in_specs,
        out_specs=out_specs,
        scratch_shapes=list(scratch),
        input_output_aliases=aliases or {},
        compiler_params=pltpu.CompilerParams(vmem_limit_bytes=limit),
        cost_estimate=pl.CostEstimate(flops=0, bytes_accessed=1, transcendentals=0),
    )(*operands)


def split(value, size):
    if size & (size - 1) == 0:
        return value >> (size.bit_length() - 1), value & (size - 1)
    return lax.div(value, size), lax.rem(value, size)


def place_of(peer, bits):
    place = 0
    for bit in bits:
        place = (place << 1) | ((peer >> (bit.bit_length() - 1)) & 1)
    return place


def planned_order(ways):
    now, order, flows, current, place = 0.0, [], [], {}, [0] * len(ways)

    def active():
        waiting = [f for f in flows if "x" in f["links"]][1:]
        running = [f for f in flows if not any(f is w for w in waiting)]
        load = {}
        for f in running:
            for link, weight in f["links"].items():
                load[link] = load.get(link, 0.0) + weight
        return [(f, min(1.0 / load[link] for link in f["links"])) for f in running]

    def advance(until):
        nonlocal now
        while now < until:
            running = active()
            step = min([until - now] + [f["left"] / rate for f, rate in running])
            now += max(step, 1e-3)
            for f, rate in running:
                f["left"] -= step * rate
                if f["left"] <= 1e-6:
                    f["end"] = now + LATENCY
            flows[:] = [f for f in flows if f["left"] > 1e-6]

    def begin(n):
        links, units = ways[n][place[n]]
        advance(now + START_TIME)
        current[n] = {"links": links, "left": units * UNIT_TIME, "end": None}
        flows.append(current[n])

    for n in range(len(ways)):
        begin(n)
    while current:
        ended = [(f["end"], n) for n, f in current.items() if f["end"] is not None and f["end"] <= now]
        if not ended:
            advance(now + 0.05)
            continue
        _, n = min(ended)
        order.append(n)
        del current[n]
        place[n] += 1
        advance(now + STEP_TIME)
        if place[n] < len(ways[n]):
            begin(n)
    return order


def offsets_of(size, lowest):
    offsets, bit = [0], size // 2
    while bit >= lowest:
        offsets += [offset | bit for offset in offsets]
        bit //= 2
    return offsets


def lay_tiles(table, base, tiles, lhs, spans, row_base, blocks, block, at=0):
    for b in range(blocks):
        for c in range(blocks):
            entry = table[base + b * blocks + c]
            tile = tiles[jnp.maximum(entry - 1, 0)]
            tile = jnp.where(entry > 0, tile, jnp.zeros_like(tile))
            top = at
            for first, rows in spans:
                lhs[pl.ds(top + b * rows, rows), pl.ds(c * block, block)] = tile[first - row_base : first - row_base + rows]
                top = top + blocks * rows


def first_part(me, slot, col, tile_id, touched, tiles, features, readers, orders, first, count, spans):
    block = tiles.shape[1]
    blocks = features.shape[0] // block
    width = features.shape[1]
    edges, cap = touched.shape[1], touched.shape[2]
    column_bits = [1 << i for i in range(1, edges.bit_length() - 1)]
    products = slot.shape[0]
    half = edges // 2
    loaded = sum(rows for _, rows in spans)
    tallest = max(rows for _, rows in spans)
    square = blocks * blocks

    listed = readers.shape[0]
    extra = -(-half * READ_CAP // 16) * 16
    shapes = [(count, blocks, rows, width) for _, rows in spans]
    shapes[1] = (count * blocks * spans[1][1] + extra, width)

    def body(me_ref, slot_hbm, col_hbm, id_hbm, touched_hbm, readers_hbm, tiles_hbm, x_hbm, *refs):
        table, entry, *outs = refs[: 2 + len(spans)]
        x_out, *scratch = refs[2 + len(spans) :]
        slot_ref, col_ref, id_ref, touched_ref, readers_ref, choice, tiles_ref, lhs, bases, seen, sems = scratch
        loads = [
            pltpu.make_async_copy(slot_hbm, slot_ref, sems.at[0]),
            pltpu.make_async_copy(col_hbm, col_ref, sems.at[1]),
            pltpu.make_async_copy(id_hbm, id_ref, sems.at[2]),
            pltpu.make_async_copy(touched_hbm.at[me_ref[0]], touched_ref, sems.at[5]),
            pltpu.make_async_copy(readers_hbm, readers_ref, sems.at[6]),
            pltpu.make_async_copy(x_hbm, x_out, sems.at[3]),
            pltpu.make_async_copy(tiles_hbm.at[:, pl.ds(0, loaded)], tiles_ref, sems.at[4]),
        ]
        for load in loads:
            load.start()

        def clear(i, carry):
            table[i] = 0
            return carry

        lax.fori_loop(0, len(orders) * edges * square, clear, 0, unroll=16)

        def place_slot(k, carry):
            owner, slot_at = split(k, cap)
            for n, order in enumerate(orders):
                place = place_of(owner ^ me_ref[0], order)
                bases[n * edges * cap + k] = ((n * edges + place) * blocks + touched_ref[slot_at, owner]) * blocks
            return carry

        for load in loads[:5]:
            load.wait()
        lax.fori_loop(0, edges * cap, place_slot, 0, unroll=8)

        for i in range(extra + 1):
            choice[i] = 0
        for i in range(edges * READ_CAP):
            entry[i] = -1
        for i in range(edges):
            seen[i] = 0

        def enter_lists(r, carry):
            owner, b = split(readers_ref[r], blocks)
            turn = seen[owner]
            seen[owner] = turn + 1
            turn = jnp.minimum(turn, READ_CAP - 1)
            entry[owner * READ_CAP + turn] = r
            peer = owner ^ me_ref[0] ^ 1
            row = place_of(peer, column_bits) * READ_CAP + turn
            choice[jnp.where(peer & 1 == 0, row, extra)] = b
            return carry

        lax.fori_loop(0, listed, enter_lists, 0)

        def enter(k, carry):
            for n in range(len(orders)):
                table[bases[n * edges * cap + slot_ref[k]] + col_ref[k]] = id_ref[k] + 1
            return carry

        lax.fori_loop(0, products, enter, 0, unroll=8)
        for load in loads[5:]:
            load.wait()

        for n, (span, out) in enumerate(zip(spans, outs)):
            height = blocks * span[1]

            def one_owner(i, carry):
                at = pl.multiple_of(i * height, height)
                base = (n * edges + first + i) * square
                lay_tiles(table, base, tiles_ref, lhs, [span], 0, blocks, block, at)
                return carry

            lax.fori_loop(0, count, one_owner, 0)
            total = jnp.dot(lhs[pl.ds(0, count * height)], x_out[...], preferred_element_type=jnp.float32)
            if n == 1:
                out[pl.ds(0, count * height)] = total.astype(jnp.bfloat16)
                for i in range(extra):
                    line = jnp.full((1, width), choice[i].astype(jnp.float32), jnp.float32)
                    out[pl.ds(count * height + i, 1)] = line.astype(jnp.bfloat16)
            else:
                out[...] = total.astype(jnp.bfloat16).reshape(out.shape)

    return call(
        body,
        [
            jax.ShapeDtypeStruct((len(orders) * edges * square,), jnp.int32),
            jax.ShapeDtypeStruct((edges * READ_CAP,), jnp.int32),
            *[jax.ShapeDtypeStruct(shape, jnp.bfloat16) for shape in shapes],
            jax.ShapeDtypeStruct(features.shape, jnp.bfloat16),
        ],
        [SMEM] + [HBM] * 7,
        [SMEM] * 2 + [VMEM] * (len(spans) + 1),
        (me, slot, col, tile_id, touched.transpose(0, 2, 1), readers, tiles, features),
        [
            pltpu.SMEM((products,), jnp.int32),
            pltpu.SMEM((products,), jnp.int32),
            pltpu.SMEM((products,), jnp.int32),
            pltpu.SMEM((cap, edges), jnp.int32),
            pltpu.SMEM((listed,), jnp.int32),
            pltpu.SMEM((extra + 1,), jnp.int32),
            pltpu.VMEM((tiles.shape[0], loaded, block), jnp.bfloat16),
            pltpu.VMEM((count * blocks * tallest, blocks * block), jnp.bfloat16),
            pltpu.SMEM((len(orders) * edges * cap,), jnp.int32),
            pltpu.SMEM((edges,), jnp.int32),
            pltpu.SemaphoreType.DMA((7,)),
        ],
        limit=62 * 1024 * 1024,
    )


def other_parts(table, tiles, inputs, jobs):
    block = tiles.shape[1]
    blocks = inputs.shape[0] // block
    width = inputs.shape[1]
    most = max(sum(rows for _, rows in spans) for _, _, spans in jobs) * blocks
    shapes = [
        jax.ShapeDtypeStruct((count, blocks, rows, width), jnp.bfloat16) for _, count, spans in jobs for _, rows in spans
    ]

    def body(table_ref, tiles_hbm, x_ref, *refs):
        outs = refs
        token, tiles_ref, lhs, sems = outs[-4:]
        token[...] = jnp.zeros_like(token)
        load = pltpu.make_async_copy(tiles_hbm, tiles_ref, sems.at[0])
        load.start()
        load.wait()
        for first, count, spans in jobs:
            height = blocks * sum(rows for _, rows in spans)

            def one_owner(i, carry):
                lay_tiles(table_ref, (first + i) * blocks * blocks, tiles_ref, lhs, spans, 0, blocks, block)
                total = jnp.dot(lhs[pl.ds(0, height)], x_ref[...], preferred_element_type=jnp.float32)
                total = total.astype(jnp.bfloat16)
                at = 0
                for out, (_, rows) in zip(outs, spans):
                    out[i] = total[at : at + blocks * rows].reshape(blocks, rows, width)
                    at += blocks * rows
                return carry

            lax.fori_loop(0, count, one_owner, 0)
            outs = outs[len(spans) :]

    results = call(
        body,
        shapes + [TOKEN],
        [SMEM, HBM, VMEM],
        [VMEM] * (len(shapes) + 1),
        (table, tiles, inputs),
        [
            pltpu.VMEM(tiles.shape, jnp.bfloat16),
            pltpu.VMEM((most, blocks * block), jnp.bfloat16),
            pltpu.SemaphoreType.DMA((1,)),
        ],
    )
    grouped, at = [], 0
    for _, _, spans in jobs:
        grouped.append(results[at : at + len(spans)])
        at += len(spans)
    return (*grouped, results[-1])


def combine(token, total, got, at_hand):
    count, *shape = total.shape
    left = count // 2

    def body(token_ref, total_ref, got_ref, at_hand_ref, *outs):
        def add(i, carry):
            if got.ndim == total.ndim:
                value = got_ref[i]
            else:
                height = shape[0] * shape[1]
                value = got_ref[pl.ds(pl.multiple_of(i * height, height), height)].reshape(shape)
            value = total_ref[i].astype(jnp.float32) + value.astype(jnp.float32)
            if not left:
                outs[0][...] = value.astype(jnp.bfloat16)
            else:

                @pl.when(i < left)
                def _():
                    outs[0][jnp.minimum(i, left - 1)] = value

                @pl.when(i >= left)
                def _():
                    outs[1][jnp.maximum(i - left, 0)] = value.astype(jnp.bfloat16)

            return carry

        lax.fori_loop(0, count, add, 0)
        outs[-1][...] = token_ref[...]

    if left:
        out_shape = [
            jax.ShapeDtypeStruct((left, *shape), jnp.float32),
            jax.ShapeDtypeStruct((count - left, *shape), jnp.bfloat16),
        ]
    else:
        out_shape = [jax.ShapeDtypeStruct(tuple(shape), jnp.bfloat16)]
    out_shape.append(TOKEN)
    return call(body, out_shape, [VMEM] * 4, [VMEM] * len(out_shape), (token, total, got, at_hand))


def join(token, held, got):
    def body(token_ref, held_ref, got_ref, out, token_out):
        out[pl.ds(0, held.shape[0])] = held_ref[...]
        out[pl.ds(held.shape[0], got.shape[0])] = got_ref[...]
        token_out[...] = token_ref[...]

    both = jax.ShapeDtypeStruct((held.shape[0] + got.shape[0], *held.shape[1:]), held.dtype)
    return call(body, [both, TOKEN], [VMEM] * 3, [VMEM] * 2, (token, held, got))


def mix(token, offsets, held, got, weight):
    _, blocks, rows, depth = held.shape
    width = weight.shape[1]

    def body(token_ref, held_ref, got_ref, w_ref, out_ref, token_out):
        mine = lax.axis_index("feat")
        total = jnp.zeros((blocks * rows, width), jnp.float32)
        for n, offset in enumerate(offsets):
            piece = (held_ref if n < held.shape[0] else got_ref)[n % held.shape[0]]
            at = pl.multiple_of((mine ^ offset) * depth, depth)
            total += jnp.dot(
                piece.reshape(blocks * rows, depth), w_ref[pl.ds(at, depth)], preferred_element_type=jnp.float32
            )
        out_ref[0] = jnp.maximum(total, 0.0).astype(jnp.bfloat16).reshape(blocks, rows, width)
        token_out[...] = token_ref[...]

    return call(
        body,
        [jax.ShapeDtypeStruct((1, blocks, rows, width), jnp.bfloat16), TOKEN],
        [VMEM] * 4,
        [VMEM] * 2,
        (token, held, got, weight),
    )


def pick(token, wanted, held, got):
    count = 2 * held.shape[0] * READ_CAP
    extra = -(-count // 16) * 16
    _, blocks, rows, width = held.shape

    def body(token_ref, wanted_ref, held_ref, got_ref, out, token_out):
        lines = wanted_ref[pl.ds(wanted.shape[0] - extra, extra)].astype(jnp.float32)
        for i in range(count):
            n = i // READ_CAP
            source = held_ref if n < held.shape[0] else got_ref
            total = jnp.zeros((rows, width), jnp.bfloat16)
            for b in range(blocks):
                chosen = jnp.where(lines[i : i + 1] == b, 1.0, 0.0)
                chosen = jnp.broadcast_to(chosen, (rows, width)).astype(jnp.bfloat16)
                total += chosen * source[n % held.shape[0], b]
            out[i] = total
        token_out[...] = token_ref[...]

    return call(
        body,
        [jax.ShapeDtypeStruct((count, *held.shape[2:]), held.dtype), TOKEN],
        [VMEM] * 4,
        [VMEM] * 2,
        (token, wanted, held, got),
    )


def touch(token, value):
    def body(token_ref, value_ref, token_out):
        token_out[...] = token_ref[...]

    return call(body, [TOKEN], [VMEM] * 2, [VMEM], (token, value))


def lay_out(token, me, readers, entry, offsets, nears, fars, outputs, block):
    count = readers.shape[0]
    width = fars[0][0].shape[2]
    blocks = outputs[0].shape[0] if outputs else nears[0][0].shape[1]
    slots = len(offsets) * READ_CAP
    arrays = [array for held, got, _ in nears for array in (held, got)] + [far for far, _ in fars]

    def body(token_ref, me_ref, readers_ref, entry_ref, *refs):
        hidden_ref, ghost_ref, token_out, near_sems, far_sems = refs[-5:]
        near_refs, far_refs = refs[: 2 * len(nears)], refs[2 * len(nears) : len(arrays)]

        def each(act):
            for number, (held, _, span) in enumerate(nears):
                held_ref, got_ref = near_refs[2 * number : 2 * number + 2]
                part = pl.ds(*span)
                act(pltpu.make_async_copy(held_ref.at[0], hidden_ref.at[:, part], near_sems.at[number, slots]))
                for i in range(slots):
                    n, j = i // READ_CAP, i % READ_CAP
                    listed = entry_ref[(me_ref[0] ^ offsets[n]) * READ_CAP + j]
                    source = held_ref if n < held.shape[0] else got_ref
                    row = n % held.shape[0]

                    @pl.when(listed >= 0)
                    def _():
                        _, b = split(readers_ref[listed], blocks)
                        target = ghost_ref.at[listed, part]
                        act(pltpu.make_async_copy(source.at[row, b], target, near_sems.at[number, i]))

            for number, (_, span) in enumerate(fars):
                part = pl.ds(*span)
                for i in range(slots):
                    n, j = i // READ_CAP, i % READ_CAP
                    listed = entry_ref[(me_ref[0] ^ 1 ^ offsets[n]) * READ_CAP + j]

                    @pl.when(listed >= 0)
                    def _():
                        target = ghost_ref.at[listed, part]
                        act(pltpu.make_async_copy(far_refs[number].at[i], target, far_sems.at[number, i]))

        each(lambda copy: copy.start())
        token_out[...] = token_ref[...]
        each(lambda copy: copy.wait())

    operands = (token, me, readers, entry, *arrays, *outputs)
    return call(
        body,
        [
            jax.ShapeDtypeStruct((blocks, block, width), jnp.bfloat16),
            jax.ShapeDtypeStruct((count, block, width), jnp.bfloat16),
            TOKEN,
        ],
        [VMEM] + [SMEM] * 3 + [VMEM] * len(arrays) + [HBM] * len(outputs),
        [HBM, HBM, VMEM],
        operands,
        [
            pltpu.SemaphoreType.DMA((max(len(nears), 1), slots + 1)),
            pltpu.SemaphoreType.DMA((len(fars), slots)),
        ],
        aliases={len(operands) - 2: 0, len(operands) - 1: 1} if outputs else None,
    )


def local(features, tiles, tile_slot, tile_col, tile_id, touched, weight, readers):
    edges, feats = lax.axis_size("edge"), lax.axis_size("feat")
    half = edges // 2
    me = lax.axis_index("edge")
    block = tiles.shape[1]
    blocks = features.shape[0] // block
    width = features.shape[1]
    unit = block // sum(SHARES)
    spans = [(sum(SHARES[:i]) * unit, share * unit) for i, share in enumerate(SHARES)]

    def flip(value, bit, axis="edge"):
        return lax.ppermute(value, axis, [(d, d ^ bit) for d in range(lax.axis_size(axis))])

    columns = offsets_of(edges, 2)
    me = me.reshape(1)
    column_bits = [1 << i for i in range(1, edges.bit_length() - 1)]
    orders = [[*column_bits, 1], [1, *column_bits]]
    table, entry, *early, inputs = first_part(
        me, tile_slot, tile_col, tile_id, touched, tiles, features, readers, orders, half, half, spans[:2]
    )
    later, first_kept, _ = other_parts(
        table, tiles, inputs, [(edges + half, half, spans[2:]), (0, half, spans[:1])]
    )
    away = [*early, *later]
    kept, token = other_parts(table, tiles, inputs, [(edges, half, spans[1:])])
    kept = [*first_kept, *kept]

    def chained(function, *operands):
        nonlocal token
        *results, token = function(token, *operands)
        return results

    def spread(held, size, lowest, axis):
        bit = size // 2
        while True:
            got = flip(held, bit, axis)
            yield
            if bit == lowest:
                return held, got
            (held,) = chained(join, held, got)
            bit //= 2

    wanted, nears, fars = None, [], []
    ended = object()

    def one_part(part):
        nonlocal wanted
        first, *rest = orders[min(part, 1)]
        got = flip(away[part], first)
        yield
        total, sent = chained(combine, kept[part], got, weight)
        if part == 1:
            wanted = got
        for bit in rest:
            got = flip(sent, bit)
            yield
            total, *sent = chained(combine, total, got, weight)
            sent = sent[0] if sent else None
        held, got = yield from spread(total[None], feats, 1, "feat")
        (mixed,) = chained(mix, offsets_of(feats, 1), held, got, weight)
        held, got = yield from spread(mixed, edges, 2, "edge")
        (picked,) = chained(pick, wanted, held, got)
        nears.append((held, got, spans[part]))
        far = flip(picked, 1)
        yield
        fars.append((far, spans[part]))

    def links_of(bit):
        return {"x": 1.0} if bit == 1 else {"end": 1.0} if bit == 2 else {"end": 1.0, "middle": 2.0}

    feat_bits = [1 << i for i in reversed(range(feats.bit_length() - 1))]
    ways = []
    for part, (_, rows) in enumerate(spans):
        share = rows / block
        way = [(links_of(bit), share * half / (1 << n)) for n, bit in enumerate(orders[min(part, 1)])]
        way += [({"chip" if bit == 1 else "feat": 1.0}, share * (1.0 if bit > 1 else 0.3)) for bit in feat_bits]
        way += [(links_of(bit), share * half / bit) for bit in reversed(column_bits)]
        ways.append(way + [({"x": 1.0}, share * READ_CAP / blocks * half)])
    steps = [one_part(part) for part in range(len(spans))]
    for step in steps:
        next(step)
    known = sorted(ORDER) == [part for part, way in enumerate(ways) for _ in way]
    *order, last = ORDER if known else planned_order(ways)
    for part in order:
        if next(steps[part], ended) is ended:
            chained(touch, fars[-1][0])
    outputs = chained(lay_out, me, readers, entry, columns, nears, fars, (), block)
    next(steps[last], None)
    outputs = chained(lay_out, me, readers, entry, columns, [], fars[-1:], outputs, block)
    hidden, ghosts = outputs
    return hidden.reshape(blocks * block, width), ghosts.reshape(-1, width)


def solution(mesh):
    in_specs = (
        P("edge", "feat"),
        P("edge", None, None),
        P("edge"),
        P("edge"),
        P("edge"),
        P(),
        P(None, "feat"),
        P("edge"),
    )
    out_specs = (P("edge", "feat"), P("edge", "feat"))
    return jax.shard_map(local, mesh=mesh, in_specs=in_specs, out_specs=out_specs, check_vma=False)
```

```python
import jax
import jax.numpy as jnp
from jax import lax
from jax.experimental import pallas as pl
from jax.experimental.pallas import tpu as pltpu
from jax.sharding import PartitionSpec as P

SHARES = (2, 2, 2, 1, 1)
ORDER = (
    0, 1, 2, 0, 1, 4, 0, 2, 1, 0, 4, 2, 1, 3, 0, 4, 2, 1, 3, 4, 0, 1, 4, 2, 3, 0, 3, 2, 1, 4, 3, 0,
    2, 3, 4, 1, 3, 2, 4, 3,
)
READ_CAP = 2
VMEM_BYTES = 12 * 1024 * 1024
UNIT_TIME, START_TIME, STEP_TIME, LATENCY = 11.3, 0.9, 0.4, 0.6

SMEM = pl.BlockSpec(memory_space=pltpu.SMEM)
VMEM = pl.BlockSpec(memory_space=pltpu.VMEM)
HBM = pl.BlockSpec(memory_space=pltpu.HBM)
TOKEN = jax.ShapeDtypeStruct((8, 128), jnp.float32)


def call(body, out_shape, in_specs, out_specs, operands, scratch=(), aliases=None, limit=VMEM_BYTES):
    return pl.pallas_call(
        body,
        out_shape=out_shape,
        in_specs=in_specs,
        out_specs=out_specs,
        scratch_shapes=list(scratch),
        input_output_aliases=aliases or {},
        compiler_params=pltpu.CompilerParams(vmem_limit_bytes=limit),
        cost_estimate=pl.CostEstimate(flops=0, bytes_accessed=1, transcendentals=0),
    )(*operands)


def split(value, size):
    if size & (size - 1) == 0:
        return value >> (size.bit_length() - 1), value & (size - 1)
    return lax.div(value, size), lax.rem(value, size)


def place_of(peer, bits):
    place = 0
    for bit in bits:
        place = (place << 1) | ((peer >> (bit.bit_length() - 1)) & 1)
    return place


def planned_order(ways):
    now, order, flows, current, place = 0.0, [], [], {}, [0] * len(ways)

    def active():
        waiting = [f for f in flows if "x" in f["links"]][1:]
        running = [f for f in flows if not any(f is w for w in waiting)]
        load = {}
        for f in running:
            for link, weight in f["links"].items():
                load[link] = load.get(link, 0.0) + weight
        return [(f, min(1.0 / load[link] for link in f["links"])) for f in running]

    def advance(until):
        nonlocal now
        while now < until:
            running = active()
            step = min([until - now] + [f["left"] / rate for f, rate in running])
            now += max(step, 1e-3)
            for f, rate in running:
                f["left"] -= step * rate
                if f["left"] <= 1e-6:
                    f["end"] = now + LATENCY
            flows[:] = [f for f in flows if f["left"] > 1e-6]

    def begin(n):
        links, units = ways[n][place[n]]
        advance(now + START_TIME)
        current[n] = {"links": links, "left": units * UNIT_TIME, "end": None}
        flows.append(current[n])

    for n in range(len(ways)):
        begin(n)
    while current:
        ended = [(f["end"], n) for n, f in current.items() if f["end"] is not None and f["end"] <= now]
        if not ended:
            advance(now + 0.05)
            continue
        _, n = min(ended)
        order.append(n)
        del current[n]
        place[n] += 1
        advance(now + STEP_TIME)
        if place[n] < len(ways[n]):
            begin(n)
    return order


def offsets_of(size, lowest):
    offsets, bit = [0], size // 2
    while bit >= lowest:
        offsets += [offset | bit for offset in offsets]
        bit //= 2
    return offsets


def lay_tiles(table, base, tiles, lhs, spans, row_base, blocks, block, at=0):
    for b in range(blocks):
        for c in range(blocks):
            entry = table[base + b * blocks + c]
            tile = tiles[jnp.maximum(entry - 1, 0)]
            tile = jnp.where(entry > 0, tile, jnp.zeros_like(tile))
            top = at
            for first, rows in spans:
                lhs[pl.ds(top + b * rows, rows), pl.ds(c * block, block)] = tile[first - row_base : first - row_base + rows]
                top = top + blocks * rows


def first_part(me, slot, col, tile_id, touched, tiles, features, readers, orders, first, count, spans):
    block = tiles.shape[1]
    blocks = features.shape[0] // block
    width = features.shape[1]
    edges, cap = touched.shape[1], touched.shape[2]
    column_bits = [1 << i for i in range(1, edges.bit_length() - 1)]
    products = slot.shape[0]
    half = edges // 2
    loaded = sum(rows for _, rows in spans)
    tallest = max(rows for _, rows in spans)
    square = blocks * blocks

    listed = readers.shape[0]
    extra = -(-half * READ_CAP // 16) * 16
    shapes = [(count, blocks, rows, width) for _, rows in spans]
    shapes[1] = (count * blocks * spans[1][1] + extra, width)

    def body(me_ref, slot_hbm, col_hbm, id_hbm, touched_hbm, readers_hbm, tiles_hbm, x_hbm, *refs):
        table, entry, *outs = refs[: 2 + len(spans)]
        x_out, *scratch = refs[2 + len(spans) :]
        slot_ref, col_ref, id_ref, touched_ref, readers_ref, choice, tiles_ref, lhs, bases, seen, sems = scratch
        loads = [
            pltpu.make_async_copy(slot_hbm, slot_ref, sems.at[0]),
            pltpu.make_async_copy(col_hbm, col_ref, sems.at[1]),
            pltpu.make_async_copy(id_hbm, id_ref, sems.at[2]),
            pltpu.make_async_copy(touched_hbm.at[me_ref[0]], touched_ref, sems.at[5]),
            pltpu.make_async_copy(readers_hbm, readers_ref, sems.at[6]),
            pltpu.make_async_copy(x_hbm, x_out, sems.at[3]),
            pltpu.make_async_copy(tiles_hbm.at[:, pl.ds(0, loaded)], tiles_ref, sems.at[4]),
        ]
        for load in loads:
            load.start()

        def clear(i, carry):
            table[i] = 0
            return carry

        lax.fori_loop(0, len(orders) * edges * square, clear, 0, unroll=16)

        def place_slot(k, carry):
            owner, slot_at = split(k, cap)
            for n, order in enumerate(orders):
                place = place_of(owner ^ me_ref[0], order)
                bases[n * edges * cap + k] = ((n * edges + place) * blocks + touched_ref[slot_at, owner]) * blocks
            return carry

        for load in loads[:5]:
            load.wait()
        lax.fori_loop(0, edges * cap, place_slot, 0, unroll=8)

        for i in range(extra + 1):
            choice[i] = 0
        for i in range(edges * READ_CAP):
            entry[i] = -1
        for i in range(edges):
            seen[i] = 0

        def enter_lists(r, carry):
            owner, b = split(readers_ref[r], blocks)
            turn = seen[owner]
            seen[owner] = turn + 1
            turn = jnp.minimum(turn, READ_CAP - 1)
            entry[owner * READ_CAP + turn] = r
            peer = owner ^ me_ref[0] ^ 1
            row = place_of(peer, column_bits) * READ_CAP + turn
            choice[jnp.where(peer & 1 == 0, row, extra)] = b
            return carry

        lax.fori_loop(0, listed, enter_lists, 0)

        def enter(k, carry):
            for n in range(len(orders)):
                table[bases[n * edges * cap + slot_ref[k]] + col_ref[k]] = id_ref[k] + 1
            return carry

        lax.fori_loop(0, products, enter, 0, unroll=8)
        for load in loads[5:]:
            load.wait()

        for n, (span, out) in enumerate(zip(spans, outs)):
            height = blocks * span[1]

            def one_owner(i, carry):
                at = pl.multiple_of(i * height, height)
                base = (n * edges + first + i) * square
                lay_tiles(table, base, tiles_ref, lhs, [span], 0, blocks, block, at)
                return carry

            lax.fori_loop(0, count, one_owner, 0)
            total = jnp.dot(lhs[pl.ds(0, count * height)], x_out[...], preferred_element_type=jnp.float32)
            if n == 1:
                out[pl.ds(0, count * height)] = total.astype(jnp.bfloat16)
                for i in range(extra):
                    line = jnp.full((1, width), choice[i].astype(jnp.float32), jnp.float32)
                    out[pl.ds(count * height + i, 1)] = line.astype(jnp.bfloat16)
            else:
                out[...] = total.astype(jnp.bfloat16).reshape(out.shape)

    return call(
        body,
        [
            jax.ShapeDtypeStruct((len(orders) * edges * square,), jnp.int32),
            jax.ShapeDtypeStruct((edges * READ_CAP,), jnp.int32),
            *[jax.ShapeDtypeStruct(shape, jnp.bfloat16) for shape in shapes],
            jax.ShapeDtypeStruct(features.shape, jnp.bfloat16),
        ],
        [SMEM] + [HBM] * 7,
        [SMEM] * 2 + [VMEM] * (len(spans) + 1),
        (me, slot, col, tile_id, touched.transpose(0, 2, 1), readers, tiles, features),
        [
            pltpu.SMEM((products,), jnp.int32),
            pltpu.SMEM((products,), jnp.int32),
            pltpu.SMEM((products,), jnp.int32),
            pltpu.SMEM((cap, edges), jnp.int32),
            pltpu.SMEM((listed,), jnp.int32),
            pltpu.SMEM((extra + 1,), jnp.int32),
            pltpu.VMEM((tiles.shape[0], loaded, block), jnp.bfloat16),
            pltpu.VMEM((count * blocks * tallest, blocks * block), jnp.bfloat16),
            pltpu.SMEM((len(orders) * edges * cap,), jnp.int32),
            pltpu.SMEM((edges,), jnp.int32),
            pltpu.SemaphoreType.DMA((7,)),
        ],
        limit=62 * 1024 * 1024,
    )


def other_parts(table, tiles, inputs, jobs):
    block = tiles.shape[1]
    blocks = inputs.shape[0] // block
    width = inputs.shape[1]
    most = max(sum(rows for _, rows in spans) for _, _, spans in jobs) * blocks
    shapes = [
        jax.ShapeDtypeStruct((count, blocks, rows, width), jnp.bfloat16) for _, count, spans in jobs for _, rows in spans
    ]

    def body(table_ref, tiles_hbm, x_ref, *refs):
        outs = refs
        token, tiles_ref, lhs, sems = outs[-4:]
        token[...] = jnp.zeros_like(token)
        load = pltpu.make_async_copy(tiles_hbm, tiles_ref, sems.at[0])
        load.start()
        load.wait()
        for first, count, spans in jobs:
            height = blocks * sum(rows for _, rows in spans)

            def one_owner(i, carry):
                lay_tiles(table_ref, (first + i) * blocks * blocks, tiles_ref, lhs, spans, 0, blocks, block)
                total = jnp.dot(lhs[pl.ds(0, height)], x_ref[...], preferred_element_type=jnp.float32)
                total = total.astype(jnp.bfloat16)
                at = 0
                for out, (_, rows) in zip(outs, spans):
                    out[i] = total[at : at + blocks * rows].reshape(blocks, rows, width)
                    at += blocks * rows
                return carry

            lax.fori_loop(0, count, one_owner, 0)
            outs = outs[len(spans) :]

    results = call(
        body,
        shapes + [TOKEN],
        [SMEM, HBM, VMEM],
        [VMEM] * (len(shapes) + 1),
        (table, tiles, inputs),
        [
            pltpu.VMEM(tiles.shape, jnp.bfloat16),
            pltpu.VMEM((most, blocks * block), jnp.bfloat16),
            pltpu.SemaphoreType.DMA((1,)),
        ],
    )
    grouped, at = [], 0
    for _, _, spans in jobs:
        grouped.append(results[at : at + len(spans)])
        at += len(spans)
    return (*grouped, results[-1])


def combine(token, total, got, at_hand):
    count, *shape = total.shape
    left = count // 2

    def body(token_ref, total_ref, got_ref, at_hand_ref, *outs):
        def add(i, carry):
            if got.ndim == total.ndim:
                value = got_ref[i]
            else:
                height = shape[0] * shape[1]
                value = got_ref[pl.ds(pl.multiple_of(i * height, height), height)].reshape(shape)
            value = total_ref[i].astype(jnp.float32) + value.astype(jnp.float32)
            if not left:
                outs[0][...] = value.astype(jnp.bfloat16)
            else:

                @pl.when(i < left)
                def _():
                    outs[0][jnp.minimum(i, left - 1)] = value

                @pl.when(i >= left)
                def _():
                    outs[1][jnp.maximum(i - left, 0)] = value.astype(jnp.bfloat16)

            return carry

        lax.fori_loop(0, count, add, 0)
        outs[-1][...] = token_ref[...]

    if left:
        out_shape = [
            jax.ShapeDtypeStruct((left, *shape), jnp.float32),
            jax.ShapeDtypeStruct((count - left, *shape), jnp.bfloat16),
        ]
    else:
        out_shape = [jax.ShapeDtypeStruct(tuple(shape), jnp.bfloat16)]
    out_shape.append(TOKEN)
    return call(body, out_shape, [VMEM] * 4, [VMEM] * len(out_shape), (token, total, got, at_hand))


def join(token, held, got):
    def body(token_ref, held_ref, got_ref, out, token_out):
        out[pl.ds(0, held.shape[0])] = held_ref[...]
        out[pl.ds(held.shape[0], got.shape[0])] = got_ref[...]
        token_out[...] = token_ref[...]

    both = jax.ShapeDtypeStruct((held.shape[0] + got.shape[0], *held.shape[1:]), held.dtype)
    return call(body, [both, TOKEN], [VMEM] * 3, [VMEM] * 2, (token, held, got))


def mix(token, offsets, held, got, weight):
    _, blocks, rows, depth = held.shape
    width = weight.shape[1]

    def body(token_ref, held_ref, got_ref, w_ref, out_ref, token_out):
        mine = lax.axis_index("feat")
        total = jnp.zeros((blocks * rows, width), jnp.float32)
        for n, offset in enumerate(offsets):
            piece = (held_ref if n < held.shape[0] else got_ref)[n % held.shape[0]]
            at = pl.multiple_of((mine ^ offset) * depth, depth)
            total += jnp.dot(
                piece.reshape(blocks * rows, depth), w_ref[pl.ds(at, depth)], preferred_element_type=jnp.float32
            )
        out_ref[0] = jnp.maximum(total, 0.0).astype(jnp.bfloat16).reshape(blocks, rows, width)
        token_out[...] = token_ref[...]

    return call(
        body,
        [jax.ShapeDtypeStruct((1, blocks, rows, width), jnp.bfloat16), TOKEN],
        [VMEM] * 4,
        [VMEM] * 2,
        (token, held, got, weight),
    )


def pick(token, wanted, held, got):
    count = 2 * held.shape[0] * READ_CAP
    extra = -(-count // 16) * 16
    _, blocks, rows, width = held.shape

    def body(token_ref, wanted_ref, held_ref, got_ref, out, token_out):
        lines = wanted_ref[pl.ds(wanted.shape[0] - extra, extra)].astype(jnp.float32)
        for i in range(count):
            n = i // READ_CAP
            source = held_ref if n < held.shape[0] else got_ref
            total = jnp.zeros((rows, width), jnp.bfloat16)
            for b in range(blocks):
                chosen = jnp.where(lines[i : i + 1] == b, 1.0, 0.0)
                chosen = jnp.broadcast_to(chosen, (rows, width)).astype(jnp.bfloat16)
                total += chosen * source[n % held.shape[0], b]
            out[i] = total
        token_out[...] = token_ref[...]

    return call(
        body,
        [jax.ShapeDtypeStruct((count, *held.shape[2:]), held.dtype), TOKEN],
        [VMEM] * 4,
        [VMEM] * 2,
        (token, wanted, held, got),
    )


def touch(token, value):
    def body(token_ref, value_ref, token_out):
        token_out[...] = token_ref[...]

    return call(body, [TOKEN], [VMEM] * 2, [VMEM], (token, value))


def lay_out(token, me, readers, entry, offsets, nears, fars, outputs, block):
    count = readers.shape[0]
    width = fars[0][0].shape[2]
    blocks = outputs[0].shape[0] if outputs else nears[0][0].shape[1]
    slots = len(offsets) * READ_CAP
    arrays = [array for held, got, _ in nears for array in (held, got)] + [far for far, _ in fars]

    def body(token_ref, me_ref, readers_ref, entry_ref, *refs):
        hidden_ref, ghost_ref, token_out, near_sems, far_sems = refs[-5:]
        near_refs, far_refs = refs[: 2 * len(nears)], refs[2 * len(nears) : len(arrays)]

        def each(act):
            for number, (held, _, span) in enumerate(nears):
                held_ref, got_ref = near_refs[2 * number : 2 * number + 2]
                part = pl.ds(*span)
                act(pltpu.make_async_copy(held_ref.at[0], hidden_ref.at[:, part], near_sems.at[number, slots]))
                for i in range(slots):
                    n, j = i // READ_CAP, i % READ_CAP
                    listed = entry_ref[(me_ref[0] ^ offsets[n]) * READ_CAP + j]
                    source = held_ref if n < held.shape[0] else got_ref
                    row = n % held.shape[0]

                    @pl.when(listed >= 0)
                    def _():
                        _, b = split(readers_ref[listed], blocks)
                        target = ghost_ref.at[listed, part]
                        act(pltpu.make_async_copy(source.at[row, b], target, near_sems.at[number, i]))

            for number, (_, span) in enumerate(fars):
                part = pl.ds(*span)
                for i in range(slots):
                    n, j = i // READ_CAP, i % READ_CAP
                    listed = entry_ref[(me_ref[0] ^ 1 ^ offsets[n]) * READ_CAP + j]

                    @pl.when(listed >= 0)
                    def _():
                        target = ghost_ref.at[listed, part]
                        act(pltpu.make_async_copy(far_refs[number].at[i], target, far_sems.at[number, i]))

        each(lambda copy: copy.start())
        token_out[...] = token_ref[...]
        each(lambda copy: copy.wait())

    operands = (token, me, readers, entry, *arrays, *outputs)
    return call(
        body,
        [
            jax.ShapeDtypeStruct((blocks, block, width), jnp.bfloat16),
            jax.ShapeDtypeStruct((count, block, width), jnp.bfloat16),
            TOKEN,
        ],
        [VMEM] + [SMEM] * 3 + [VMEM] * len(arrays) + [HBM] * len(outputs),
        [HBM, HBM, VMEM],
        operands,
        [
            pltpu.SemaphoreType.DMA((max(len(nears), 1), slots + 1)),
            pltpu.SemaphoreType.DMA((len(fars), slots)),
        ],
        aliases={len(operands) - 2: 0, len(operands) - 1: 1} if outputs else None,
    )


def local(features, tiles, tile_slot, tile_col, tile_id, touched, weight, readers):
    edges, feats = lax.axis_size("edge"), lax.axis_size("feat")
    half = edges // 2
    me = lax.axis_index("edge")
    block = tiles.shape[1]
    blocks = features.shape[0] // block
    width = features.shape[1]
    unit = block // sum(SHARES)
    spans = [(sum(SHARES[:i]) * unit, share * unit) for i, share in enumerate(SHARES)]

    def flip(value, bit, axis="edge"):
        return lax.ppermute(value, axis, [(d, d ^ bit) for d in range(lax.axis_size(axis))])

    columns = offsets_of(edges, 2)
    me = me.reshape(1)
    column_bits = [1 << i for i in range(1, edges.bit_length() - 1)]
    orders = [[*column_bits, 1], [1, *column_bits]]
    table, entry, *early, inputs = first_part(
        me, tile_slot, tile_col, tile_id, touched, tiles, features, readers, orders, half, half, spans[:2]
    )
    later, first_kept, _ = other_parts(
        table, tiles, inputs, [(edges + half, half, spans[2:]), (0, half, spans[:1])]
    )
    away = [*early, *later]
    kept, token = other_parts(table, tiles, inputs, [(edges, half, spans[1:])])
    kept = [*first_kept, *kept]

    def chained(function, *operands):
        nonlocal token
        *results, token = function(token, *operands)
        return results

    def spread(held, size, lowest, axis):
        bit = size // 2
        while True:
            got = flip(held, bit, axis)
            yield
            if bit == lowest:
                return held, got
            (held,) = chained(join, held, got)
            bit //= 2

    wanted, nears, fars = None, [], []
    ended = object()

    def one_part(part):
        nonlocal wanted
        first, *rest = orders[min(part, 1)]
        got = flip(away[part], first)
        yield
        total, sent = chained(combine, kept[part], got, weight)
        if part == 1:
            wanted = got
        for bit in rest:
            got = flip(sent, bit)
            yield
            total, *sent = chained(combine, total, got, weight)
            sent = sent[0] if sent else None
        held, got = yield from spread(total[None], feats, 1, "feat")
        (mixed,) = chained(mix, offsets_of(feats, 1), held, got, weight)
        held, got = yield from spread(mixed, edges, 2, "edge")
        (picked,) = chained(pick, wanted, held, got)
        nears.append((held, got, spans[part]))
        far = flip(picked, 1)
        yield
        fars.append((far, spans[part]))

    def links_of(bit):
        return {"x": 1.0} if bit == 1 else {"end": 1.0} if bit == 2 else {"end": 1.0, "middle": 2.0}

    feat_bits = [1 << i for i in reversed(range(feats.bit_length() - 1))]
    ways = []
    for part, (_, rows) in enumerate(spans):
        share = rows / block
        way = [(links_of(bit), share * half / (1 << n)) for n, bit in enumerate(orders[min(part, 1)])]
        way += [({"chip" if bit == 1 else "feat": 1.0}, share * (1.0 if bit > 1 else 0.3)) for bit in feat_bits]
        way += [(links_of(bit), share * half / bit) for bit in reversed(column_bits)]
        ways.append(way + [({"x": 1.0}, share * READ_CAP / blocks * half)])
    steps = [one_part(part) for part in range(len(spans))]
    for step in steps:
        next(step)
    known = sorted(ORDER) == [part for part, way in enumerate(ways) for _ in way]
    *order, last = ORDER if known else planned_order(ways)
    for part in order:
        if next(steps[part], ended) is ended:
            chained(touch, fars[-1][0])
    outputs = chained(lay_out, me, readers, entry, columns, nears, fars, (), block)
    next(steps[last], None)
    outputs = chained(lay_out, me, readers, entry, columns, [], fars[-1:], outputs, block)
    hidden, ghosts = outputs
    return hidden.reshape(blocks * block, width), ghosts.reshape(-1, width)


def solution(mesh):
    in_specs = (
        P("edge", "feat"),
        P("edge", None, None),
        P("edge"),
        P("edge"),
        P("edge"),
        P(),
        P(None, "feat"),
        P("edge"),
    )
    out_specs = (P("edge", "feat"), P("edge", "feat"))
    return jax.shard_map(local, mesh=mesh, in_specs=in_specs, out_specs=out_specs, check_vma=False)
```

```python
import jax
import jax.numpy as jnp
from jax import lax
from jax.experimental import pallas as pl
from jax.experimental.pallas import tpu as pltpu
from jax.sharding import PartitionSpec as P

SHARES = (2, 2, 2, 1, 1)
ORDER = (
    1, 0, 2, 4, 1, 0, 2, 3, 1, 0, 4, 2, 1, 0, 0, 2, 4, 1, 0, 3, 1, 4, 4, 2, 3, 0, 3, 2, 1, 4, 0, 3,
    2, 3, 4, 1, 3, 2, 4, 3,
)
READ_CAP = 2
VMEM_BYTES = 12 * 1024 * 1024
UNIT_TIME, START_TIME, STEP_TIME, LATENCY = 11.3, 0.9, 0.4, 0.6

SMEM = pl.BlockSpec(memory_space=pltpu.SMEM)
VMEM = pl.BlockSpec(memory_space=pltpu.VMEM)
HBM = pl.BlockSpec(memory_space=pltpu.HBM)
TOKEN = jax.ShapeDtypeStruct((8, 128), jnp.float32)


def call(body, out_shape, in_specs, out_specs, operands, scratch=(), aliases=None, limit=VMEM_BYTES):
    return pl.pallas_call(
        body,
        out_shape=out_shape,
        in_specs=in_specs,
        out_specs=out_specs,
        scratch_shapes=list(scratch),
        input_output_aliases=aliases or {},
        compiler_params=pltpu.CompilerParams(vmem_limit_bytes=limit),
        cost_estimate=pl.CostEstimate(flops=0, bytes_accessed=1, transcendentals=0),
    )(*operands)


def split(value, size):
    if size & (size - 1) == 0:
        return value >> (size.bit_length() - 1), value & (size - 1)
    return lax.div(value, size), lax.rem(value, size)


def place_of(peer, bits):
    place = 0
    for bit in bits:
        place = (place << 1) | ((peer >> (bit.bit_length() - 1)) & 1)
    return place


def planned_order(ways):
    now, order, flows, current, place = 0.0, [], [], {}, [0] * len(ways)

    def active():
        waiting = [f for f in flows if "x" in f["links"]][1:]
        running = [f for f in flows if not any(f is w for w in waiting)]
        load = {}
        for f in running:
            for link, weight in f["links"].items():
                load[link] = load.get(link, 0.0) + weight
        return [(f, min(1.0 / load[link] for link in f["links"])) for f in running]

    def advance(until):
        nonlocal now
        while now < until:
            running = active()
            step = min([until - now] + [f["left"] / rate for f, rate in running])
            now += max(step, 1e-3)
            for f, rate in running:
                f["left"] -= step * rate
                if f["left"] <= 1e-6:
                    f["end"] = now + LATENCY
            flows[:] = [f for f in flows if f["left"] > 1e-6]

    def begin(n):
        links, units = ways[n][place[n]]
        advance(now + START_TIME)
        current[n] = {"links": links, "left": units * UNIT_TIME, "end": None}
        flows.append(current[n])

    for n in range(len(ways)):
        begin(n)
    while current:
        ended = [(f["end"], n) for n, f in current.items() if f["end"] is not None and f["end"] <= now]
        if not ended:
            advance(now + 0.05)
            continue
        _, n = min(ended)
        order.append(n)
        del current[n]
        place[n] += 1
        advance(now + STEP_TIME)
        if place[n] < len(ways[n]):
            begin(n)
    return order


def offsets_of(size, lowest):
    offsets, bit = [0], size // 2
    while bit >= lowest:
        offsets += [offset | bit for offset in offsets]
        bit //= 2
    return offsets


def lay_tiles(table, base, tiles, lhs, spans, row_base, blocks, block, at=0):
    for b in range(blocks):
        for c in range(blocks):
            entry = table[base + b * blocks + c]
            tile = tiles[jnp.maximum(entry - 1, 0)]
            tile = jnp.where(entry > 0, tile, jnp.zeros_like(tile))
            top = at
            for first, rows in spans:
                lhs[pl.ds(top + b * rows, rows), pl.ds(c * block, block)] = tile[first - row_base : first - row_base + rows]
                top = top + blocks * rows


def first_part(me, slot, col, tile_id, touched, tiles, features, readers, orders, first, count, spans):
    block = tiles.shape[1]
    blocks = features.shape[0] // block
    width = features.shape[1]
    edges, cap = touched.shape[1], touched.shape[2]
    column_bits = [1 << i for i in range(1, edges.bit_length() - 1)]
    products = slot.shape[0]
    half = edges // 2
    loaded = sum(rows for _, rows in spans)
    tallest = max(rows for _, rows in spans)
    square = blocks * blocks

    listed = readers.shape[0]
    extra = -(-half * READ_CAP // 16) * 16
    shapes = [(count, blocks, rows, width) for _, rows in spans]
    shapes[1] = (count * blocks * spans[1][1] + extra, width)

    def body(me_ref, slot_hbm, col_hbm, id_hbm, touched_hbm, readers_hbm, tiles_hbm, x_hbm, *refs):
        table, entry, *outs = refs[: 2 + len(spans)]
        x_out, *scratch = refs[2 + len(spans) :]
        slot_ref, col_ref, id_ref, touched_ref, readers_ref, choice, tiles_ref, lhs, bases, seen, sems = scratch
        loads = [
            pltpu.make_async_copy(slot_hbm, slot_ref, sems.at[0]),
            pltpu.make_async_copy(col_hbm, col_ref, sems.at[1]),
            pltpu.make_async_copy(id_hbm, id_ref, sems.at[2]),
            pltpu.make_async_copy(touched_hbm.at[me_ref[0]], touched_ref, sems.at[5]),
            pltpu.make_async_copy(readers_hbm, readers_ref, sems.at[6]),
            pltpu.make_async_copy(x_hbm, x_out, sems.at[3]),
            pltpu.make_async_copy(tiles_hbm.at[:, pl.ds(0, loaded)], tiles_ref, sems.at[4]),
        ]
        for load in loads:
            load.start()

        def clear(i, carry):
            table[i] = 0
            return carry

        lax.fori_loop(0, len(orders) * edges * square, clear, 0, unroll=16)

        def place_slot(k, carry):
            owner, slot_at = split(k, cap)
            for n, order in enumerate(orders):
                place = place_of(owner ^ me_ref[0], order)
                bases[n * edges * cap + k] = ((n * edges + place) * blocks + touched_ref[slot_at, owner]) * blocks
            return carry

        for load in loads[:5]:
            load.wait()
        lax.fori_loop(0, edges * cap, place_slot, 0, unroll=8)

        for i in range(extra + 1):
            choice[i] = 0
        for i in range(edges * READ_CAP):
            entry[i] = -1
        for i in range(edges):
            seen[i] = 0

        def enter_lists(r, carry):
            owner, b = split(readers_ref[r], blocks)
            turn = seen[owner]
            seen[owner] = turn + 1
            turn = jnp.minimum(turn, READ_CAP - 1)
            entry[owner * READ_CAP + turn] = r
            peer = owner ^ me_ref[0] ^ 1
            row = place_of(peer, column_bits) * READ_CAP + turn
            choice[jnp.where(peer & 1 == 0, row, extra)] = b
            return carry

        lax.fori_loop(0, listed, enter_lists, 0)

        def enter(k, carry):
            for n in range(len(orders)):
                table[bases[n * edges * cap + slot_ref[k]] + col_ref[k]] = id_ref[k] + 1
            return carry

        lax.fori_loop(0, products, enter, 0, unroll=8)
        for load in loads[5:]:
            load.wait()

        for n, (span, out) in enumerate(zip(spans, outs)):
            height = blocks * span[1]

            def one_owner(i, carry):
                at = pl.multiple_of(i * height, height)
                base = (n * edges + first + i) * square
                lay_tiles(table, base, tiles_ref, lhs, [span], 0, blocks, block, at)
                return carry

            lax.fori_loop(0, count, one_owner, 0)
            total = jnp.dot(lhs[pl.ds(0, count * height)], x_out[...], preferred_element_type=jnp.float32)
            if n == 1:
                out[pl.ds(0, count * height)] = total.astype(jnp.bfloat16)
                for i in range(extra):
                    line = jnp.full((1, width), choice[i].astype(jnp.float32), jnp.float32)
                    out[pl.ds(count * height + i, 1)] = line.astype(jnp.bfloat16)
            else:
                out[...] = total.astype(jnp.bfloat16).reshape(out.shape)

    return call(
        body,
        [
            jax.ShapeDtypeStruct((len(orders) * edges * square,), jnp.int32),
            jax.ShapeDtypeStruct((edges * READ_CAP,), jnp.int32),
            *[jax.ShapeDtypeStruct(shape, jnp.bfloat16) for shape in shapes],
            jax.ShapeDtypeStruct(features.shape, jnp.bfloat16),
        ],
        [SMEM] + [HBM] * 7,
        [SMEM] * 2 + [VMEM] * (len(spans) + 1),
        (me, slot, col, tile_id, touched.transpose(0, 2, 1), readers, tiles, features),
        [
            pltpu.SMEM((products,), jnp.int32),
            pltpu.SMEM((products,), jnp.int32),
            pltpu.SMEM((products,), jnp.int32),
            pltpu.SMEM((cap, edges), jnp.int32),
            pltpu.SMEM((listed,), jnp.int32),
            pltpu.SMEM((extra + 1,), jnp.int32),
            pltpu.VMEM((tiles.shape[0], loaded, block), jnp.bfloat16),
            pltpu.VMEM((count * blocks * tallest, blocks * block), jnp.bfloat16),
            pltpu.SMEM((len(orders) * edges * cap,), jnp.int32),
            pltpu.SMEM((edges,), jnp.int32),
            pltpu.SemaphoreType.DMA((7,)),
        ],
        limit=62 * 1024 * 1024,
    )


def other_parts(table, tiles, inputs, jobs):
    block = tiles.shape[1]
    blocks = inputs.shape[0] // block
    width = inputs.shape[1]
    most = max(sum(rows for _, rows in spans) for _, _, spans in jobs) * blocks
    shapes = [
        jax.ShapeDtypeStruct((count, blocks, rows, width), jnp.bfloat16) for _, count, spans in jobs for _, rows in spans
    ]

    def body(table_ref, tiles_hbm, x_ref, *refs):
        outs = refs
        token, tiles_ref, lhs, sems = outs[-4:]
        token[...] = jnp.zeros_like(token)
        load = pltpu.make_async_copy(tiles_hbm, tiles_ref, sems.at[0])
        load.start()
        load.wait()
        for first, count, spans in jobs:
            height = blocks * sum(rows for _, rows in spans)

            def one_owner(i, carry):
                lay_tiles(table_ref, (first + i) * blocks * blocks, tiles_ref, lhs, spans, 0, blocks, block)
                total = jnp.dot(lhs[pl.ds(0, height)], x_ref[...], preferred_element_type=jnp.float32)
                total = total.astype(jnp.bfloat16)
                at = 0
                for out, (_, rows) in zip(outs, spans):
                    out[i] = total[at : at + blocks * rows].reshape(blocks, rows, width)
                    at += blocks * rows
                return carry

            lax.fori_loop(0, count, one_owner, 0)
            outs = outs[len(spans) :]

    results = call(
        body,
        shapes + [TOKEN],
        [SMEM, HBM, VMEM],
        [VMEM] * (len(shapes) + 1),
        (table, tiles, inputs),
        [
            pltpu.VMEM(tiles.shape, jnp.bfloat16),
            pltpu.VMEM((most, blocks * block), jnp.bfloat16),
            pltpu.SemaphoreType.DMA((1,)),
        ],
    )
    grouped, at = [], 0
    for _, _, spans in jobs:
        grouped.append(results[at : at + len(spans)])
        at += len(spans)
    return (*grouped, results[-1])


def combine(token, total, got, at_hand):
    count, *shape = total.shape
    left = count // 2

    def body(token_ref, total_ref, got_ref, at_hand_ref, *outs):
        def add(i, carry):
            if got.ndim == total.ndim:
                value = got_ref[i]
            else:
                height = shape[0] * shape[1]
                value = got_ref[pl.ds(pl.multiple_of(i * height, height), height)].reshape(shape)
            value = total_ref[i].astype(jnp.float32) + value.astype(jnp.float32)
            if not left:
                outs[0][...] = value.astype(jnp.bfloat16)
            else:

                @pl.when(i < left)
                def _():
                    outs[0][jnp.minimum(i, left - 1)] = value

                @pl.when(i >= left)
                def _():
                    outs[1][jnp.maximum(i - left, 0)] = value.astype(jnp.bfloat16)

            return carry

        lax.fori_loop(0, count, add, 0)
        outs[-1][...] = token_ref[...]

    if left:
        out_shape = [
            jax.ShapeDtypeStruct((left, *shape), jnp.float32),
            jax.ShapeDtypeStruct((count - left, *shape), jnp.bfloat16),
        ]
    else:
        out_shape = [jax.ShapeDtypeStruct(tuple(shape), jnp.bfloat16)]
    out_shape.append(TOKEN)
    return call(body, out_shape, [VMEM] * 4, [VMEM] * len(out_shape), (token, total, got, at_hand))


def join(token, held, got):
    def body(token_ref, held_ref, got_ref, out, token_out):
        out[pl.ds(0, held.shape[0])] = held_ref[...]
        out[pl.ds(held.shape[0], got.shape[0])] = got_ref[...]
        token_out[...] = token_ref[...]

    both = jax.ShapeDtypeStruct((held.shape[0] + got.shape[0], *held.shape[1:]), held.dtype)
    return call(body, [both, TOKEN], [VMEM] * 3, [VMEM] * 2, (token, held, got))


def mix(token, offsets, held, got, weight):
    _, blocks, rows, depth = held.shape
    width = weight.shape[1]

    def body(token_ref, held_ref, got_ref, w_ref, out_ref, token_out):
        mine = lax.axis_index("feat")
        total = jnp.zeros((blocks * rows, width), jnp.float32)
        for n, offset in enumerate(offsets):
            piece = (held_ref if n < held.shape[0] else got_ref)[n % held.shape[0]]
            at = pl.multiple_of((mine ^ offset) * depth, depth)
            total += jnp.dot(
                piece.reshape(blocks * rows, depth), w_ref[pl.ds(at, depth)], preferred_element_type=jnp.float32
            )
        out_ref[0] = jnp.maximum(total, 0.0).astype(jnp.bfloat16).reshape(blocks, rows, width)
        token_out[...] = token_ref[...]

    return call(
        body,
        [jax.ShapeDtypeStruct((1, blocks, rows, width), jnp.bfloat16), TOKEN],
        [VMEM] * 4,
        [VMEM] * 2,
        (token, held, got, weight),
    )


def pick(token, wanted, held, got):
    count = 2 * held.shape[0] * READ_CAP
    extra = -(-count // 16) * 16
    _, blocks, rows, width = held.shape

    def body(token_ref, wanted_ref, held_ref, got_ref, out, token_out):
        lines = wanted_ref[pl.ds(wanted.shape[0] - extra, extra)].astype(jnp.float32)
        for i in range(count):
            n = i // READ_CAP
            source = held_ref if n < held.shape[0] else got_ref
            total = jnp.zeros((rows, width), jnp.bfloat16)
            for b in range(blocks):
                chosen = jnp.where(lines[i : i + 1] == b, 1.0, 0.0)
                chosen = jnp.broadcast_to(chosen, (rows, width)).astype(jnp.bfloat16)
                total += chosen * source[n % held.shape[0], b]
            out[i] = total
        token_out[...] = token_ref[...]

    return call(
        body,
        [jax.ShapeDtypeStruct((count, *held.shape[2:]), held.dtype), TOKEN],
        [VMEM] * 4,
        [VMEM] * 2,
        (token, wanted, held, got),
    )


def touch(token, value):
    def body(token_ref, value_ref, token_out):
        token_out[...] = token_ref[...]

    return call(body, [TOKEN], [VMEM] * 2, [VMEM], (token, value))


def lay_out(token, me, readers, entry, offsets, nears, fars, outputs, block):
    count = readers.shape[0]
    width = fars[0][0].shape[2]
    blocks = outputs[0].shape[0] if outputs else nears[0][0].shape[1]
    slots = len(offsets) * READ_CAP
    arrays = [array for held, got, _ in nears for array in (held, got)] + [far for far, _ in fars]

    def body(token_ref, me_ref, readers_ref, entry_ref, *refs):
        hidden_ref, ghost_ref, token_out, near_sems, far_sems = refs[-5:]
        near_refs, far_refs = refs[: 2 * len(nears)], refs[2 * len(nears) : len(arrays)]

        def each(act):
            for number, (held, _, span) in enumerate(nears):
                held_ref, got_ref = near_refs[2 * number : 2 * number + 2]
                part = pl.ds(*span)
                act(pltpu.make_async_copy(held_ref.at[0], hidden_ref.at[:, part], near_sems.at[number, slots]))
                for i in range(slots):
                    n, j = i // READ_CAP, i % READ_CAP
                    listed = entry_ref[(me_ref[0] ^ offsets[n]) * READ_CAP + j]
                    source = held_ref if n < held.shape[0] else got_ref
                    row = n % held.shape[0]

                    @pl.when(listed >= 0)
                    def _():
                        _, b = split(readers_ref[listed], blocks)
                        target = ghost_ref.at[listed, part]
                        act(pltpu.make_async_copy(source.at[row, b], target, near_sems.at[number, i]))

            for number, (_, span) in enumerate(fars):
                part = pl.ds(*span)
                for i in range(slots):
                    n, j = i // READ_CAP, i % READ_CAP
                    listed = entry_ref[(me_ref[0] ^ 1 ^ offsets[n]) * READ_CAP + j]

                    @pl.when(listed >= 0)
                    def _():
                        target = ghost_ref.at[listed, part]
                        act(pltpu.make_async_copy(far_refs[number].at[i], target, far_sems.at[number, i]))

        each(lambda copy: copy.start())
        token_out[...] = token_ref[...]
        each(lambda copy: copy.wait())

    operands = (token, me, readers, entry, *arrays, *outputs)
    return call(
        body,
        [
            jax.ShapeDtypeStruct((blocks, block, width), jnp.bfloat16),
            jax.ShapeDtypeStruct((count, block, width), jnp.bfloat16),
            TOKEN,
        ],
        [VMEM] + [SMEM] * 3 + [VMEM] * len(arrays) + [HBM] * len(outputs),
        [HBM, HBM, VMEM],
        operands,
        [
            pltpu.SemaphoreType.DMA((max(len(nears), 1), slots + 1)),
            pltpu.SemaphoreType.DMA((len(fars), slots)),
        ],
        aliases={len(operands) - 2: 0, len(operands) - 1: 1} if outputs else None,
    )


def local(features, tiles, tile_slot, tile_col, tile_id, touched, weight, readers):
    edges, feats = lax.axis_size("edge"), lax.axis_size("feat")
    half = edges // 2
    me = lax.axis_index("edge")
    block = tiles.shape[1]
    blocks = features.shape[0] // block
    width = features.shape[1]
    unit = block // sum(SHARES)
    spans = [(sum(SHARES[:i]) * unit, share * unit) for i, share in enumerate(SHARES)]

    def flip(value, bit, axis="edge"):
        return lax.ppermute(value, axis, [(d, d ^ bit) for d in range(lax.axis_size(axis))])

    columns = offsets_of(edges, 2)
    me = me.reshape(1)
    column_bits = [1 << i for i in range(1, edges.bit_length() - 1)]
    orders = [[*column_bits, 1], [1, *column_bits]]
    table, entry, *early, inputs = first_part(
        me, tile_slot, tile_col, tile_id, touched, tiles, features, readers, orders, half, half, spans[:2]
    )
    later, first_kept, _ = other_parts(
        table, tiles, inputs, [(edges + half, half, spans[2:]), (0, half, spans[:1])]
    )
    away = [*early, *later]
    kept, token = other_parts(table, tiles, inputs, [(edges, half, spans[1:])])
    kept = [*first_kept, *kept]

    def chained(function, *operands):
        nonlocal token
        *results, token = function(token, *operands)
        return results

    def spread(held, size, lowest, axis):
        bit = size // 2
        while True:
            got = flip(held, bit, axis)
            yield
            if bit == lowest:
                return held, got
            (held,) = chained(join, held, got)
            bit //= 2

    wanted, nears, fars = None, [], []
    ended = object()

    def one_part(part):
        nonlocal wanted
        first, *rest = orders[min(part, 1)]
        got = flip(away[part], first)
        yield
        total, sent = chained(combine, kept[part], got, weight)
        if part == 1:
            wanted = got
        for bit in rest:
            got = flip(sent, bit)
            yield
            total, *sent = chained(combine, total, got, weight)
            sent = sent[0] if sent else None
        held, got = yield from spread(total[None], feats, 1, "feat")
        (mixed,) = chained(mix, offsets_of(feats, 1), held, got, weight)
        held, got = yield from spread(mixed, edges, 2, "edge")
        (picked,) = chained(pick, wanted, held, got)
        nears.append((held, got, spans[part]))
        far = flip(picked, 1)
        yield
        fars.append((far, spans[part]))

    def links_of(bit):
        return {"x": 1.0} if bit == 1 else {"end": 1.0} if bit == 2 else {"end": 1.0, "middle": 2.0}

    feat_bits = [1 << i for i in reversed(range(feats.bit_length() - 1))]
    ways = []
    for part, (_, rows) in enumerate(spans):
        share = rows / block
        way = [(links_of(bit), share * half / (1 << n)) for n, bit in enumerate(orders[min(part, 1)])]
        way += [({"chip" if bit == 1 else "feat": 1.0}, share * (1.0 if bit > 1 else 0.3)) for bit in feat_bits]
        way += [(links_of(bit), share * half / bit) for bit in reversed(column_bits)]
        ways.append(way + [({"x": 1.0}, share * READ_CAP / blocks * half)])
    steps = [one_part(part) for part in range(len(spans))]
    for step in steps:
        next(step)
    known = sorted(ORDER) == [part for part, way in enumerate(ways) for _ in way]
    *order, last = ORDER if known else planned_order(ways)
    for part in order:
        if next(steps[part], ended) is ended:
            chained(touch, fars[-1][0])
    outputs = chained(lay_out, me, readers, entry, columns, nears, fars, (), block)
    next(steps[last], None)
    outputs = chained(lay_out, me, readers, entry, columns, [], fars[-1:], outputs, block)
    hidden, ghosts = outputs
    return hidden.reshape(blocks * block, width), ghosts.reshape(-1, width)


def solution(mesh):
    in_specs = (
        P("edge", "feat"),
        P("edge", None, None),
        P("edge"),
        P("edge"),
        P("edge"),
        P(),
        P(None, "feat"),
        P("edge"),
    )
    out_specs = (P("edge", "feat"), P("edge", "feat"))
    return jax.shard_map(local, mesh=mesh, in_specs=in_specs, out_specs=out_specs, check_vma=False)
```

```python
import jax
import jax.numpy as jnp
from jax import lax
from jax.experimental import pallas as pl
from jax.experimental.pallas import tpu as pltpu
from jax.sharding import PartitionSpec as P

SHARES = (2, 2, 2, 1, 1)
ORDER = (
    1, 0, 2, 3, 1, 0, 2, 4, 1, 0, 4, 2, 1, 0, 0, 4, 4, 3, 1, 0, 2, 1, 4, 0, 2, 3, 1, 3, 2, 4, 3, 1,
    2, 3, 4, 0, 3, 2, 4, 3,
)
READ_CAP = 2
VMEM_BYTES = 12 * 1024 * 1024
UNIT_TIME, START_TIME, STEP_TIME, LATENCY = 11.3, 0.9, 0.4, 0.6

SMEM = pl.BlockSpec(memory_space=pltpu.SMEM)
VMEM = pl.BlockSpec(memory_space=pltpu.VMEM)
HBM = pl.BlockSpec(memory_space=pltpu.HBM)
TOKEN = jax.ShapeDtypeStruct((8, 128), jnp.float32)


def call(body, out_shape, in_specs, out_specs, operands, scratch=(), aliases=None, limit=VMEM_BYTES):
    return pl.pallas_call(
        body,
        out_shape=out_shape,
        in_specs=in_specs,
        out_specs=out_specs,
        scratch_shapes=list(scratch),
        input_output_aliases=aliases or {},
        compiler_params=pltpu.CompilerParams(vmem_limit_bytes=limit),
        cost_estimate=pl.CostEstimate(flops=0, bytes_accessed=1, transcendentals=0),
    )(*operands)


def split(value, size):
    if size & (size - 1) == 0:
        return value >> (size.bit_length() - 1), value & (size - 1)
    return lax.div(value, size), lax.rem(value, size)


def place_of(peer, bits):
    place = 0
    for bit in bits:
        place = (place << 1) | ((peer >> (bit.bit_length() - 1)) & 1)
    return place


def planned_order(ways):
    now, order, flows, current, place = 0.0, [], [], {}, [0] * len(ways)

    def active():
        waiting = [f for f in flows if "x" in f["links"]][1:]
        running = [f for f in flows if not any(f is w for w in waiting)]
        load = {}
        for f in running:
            for link, weight in f["links"].items():
                load[link] = load.get(link, 0.0) + weight
        return [(f, min(1.0 / load[link] for link in f["links"])) for f in running]

    def advance(until):
        nonlocal now
        while now < until:
            running = active()
            step = min([until - now] + [f["left"] / rate for f, rate in running])
            now += max(step, 1e-3)
            for f, rate in running:
                f["left"] -= step * rate
                if f["left"] <= 1e-6:
                    f["end"] = now + LATENCY
            flows[:] = [f for f in flows if f["left"] > 1e-6]

    def begin(n):
        links, units = ways[n][place[n]]
        advance(now + START_TIME)
        current[n] = {"links": links, "left": units * UNIT_TIME, "end": None}
        flows.append(current[n])

    for n in range(len(ways)):
        begin(n)
    while current:
        ended = [(f["end"], n) for n, f in current.items() if f["end"] is not None and f["end"] <= now]
        if not ended:
            advance(now + 0.05)
            continue
        _, n = min(ended)
        order.append(n)
        del current[n]
        place[n] += 1
        advance(now + STEP_TIME)
        if place[n] < len(ways[n]):
            begin(n)
    return order


def offsets_of(size, lowest):
    offsets, bit = [0], size // 2
    while bit >= lowest:
        offsets += [offset | bit for offset in offsets]
        bit //= 2
    return offsets


def lay_tiles(table, base, tiles, lhs, spans, row_base, blocks, block, at=0):
    for b in range(blocks):
        for c in range(blocks):
            entry = table[base + b * blocks + c]
            tile = tiles[jnp.maximum(entry - 1, 0)]
            tile = jnp.where(entry > 0, tile, jnp.zeros_like(tile))
            top = at
            for first, rows in spans:
                lhs[pl.ds(top + b * rows, rows), pl.ds(c * block, block)] = tile[first - row_base : first - row_base + rows]
                top = top + blocks * rows


def first_part(me, slot, col, tile_id, touched, tiles, features, readers, orders, first, count, spans):
    block = tiles.shape[1]
    blocks = features.shape[0] // block
    width = features.shape[1]
    edges, cap = touched.shape[1], touched.shape[2]
    column_bits = [1 << i for i in range(1, edges.bit_length() - 1)]
    products = slot.shape[0]
    half = edges // 2
    loaded = sum(rows for _, rows in spans)
    tallest = max(rows for _, rows in spans)
    square = blocks * blocks

    listed = readers.shape[0]
    extra = -(-half * READ_CAP // 16) * 16
    shapes = [(count, blocks, rows, width) for _, rows in spans]
    shapes[1] = (count * blocks * spans[1][1] + extra, width)

    def body(me_ref, slot_hbm, col_hbm, id_hbm, touched_hbm, readers_hbm, tiles_hbm, x_hbm, *refs):
        table, entry, *outs = refs[: 2 + len(spans)]
        x_out, *scratch = refs[2 + len(spans) :]
        slot_ref, col_ref, id_ref, touched_ref, readers_ref, choice, tiles_ref, lhs, bases, seen, sems = scratch
        loads = [
            pltpu.make_async_copy(slot_hbm, slot_ref, sems.at[0]),
            pltpu.make_async_copy(col_hbm, col_ref, sems.at[1]),
            pltpu.make_async_copy(id_hbm, id_ref, sems.at[2]),
            pltpu.make_async_copy(touched_hbm.at[me_ref[0]], touched_ref, sems.at[5]),
            pltpu.make_async_copy(readers_hbm, readers_ref, sems.at[6]),
            pltpu.make_async_copy(x_hbm, x_out, sems.at[3]),
            pltpu.make_async_copy(tiles_hbm.at[:, pl.ds(0, loaded)], tiles_ref, sems.at[4]),
        ]
        for load in loads:
            load.start()

        def clear(i, carry):
            table[i] = 0
            return carry

        lax.fori_loop(0, len(orders) * edges * square, clear, 0, unroll=16)

        def place_slot(k, carry):
            owner, slot_at = split(k, cap)
            for n, order in enumerate(orders):
                place = place_of(owner ^ me_ref[0], order)
                bases[n * edges * cap + k] = ((n * edges + place) * blocks + touched_ref[slot_at, owner]) * blocks
            return carry

        for load in loads[:5]:
            load.wait()
        lax.fori_loop(0, edges * cap, place_slot, 0, unroll=8)

        for i in range(extra + 1):
            choice[i] = 0
        for i in range(edges * READ_CAP):
            entry[i] = -1
        for i in range(edges):
            seen[i] = 0

        def enter_lists(r, carry):
            owner, b = split(readers_ref[r], blocks)
            turn = seen[owner]
            seen[owner] = turn + 1
            turn = jnp.minimum(turn, READ_CAP - 1)
            entry[owner * READ_CAP + turn] = r
            peer = owner ^ me_ref[0] ^ 1
            row = place_of(peer, column_bits) * READ_CAP + turn
            choice[jnp.where(peer & 1 == 0, row, extra)] = b
            return carry

        lax.fori_loop(0, listed, enter_lists, 0)

        def enter(k, carry):
            for n in range(len(orders)):
                table[bases[n * edges * cap + slot_ref[k]] + col_ref[k]] = id_ref[k] + 1
            return carry

        lax.fori_loop(0, products, enter, 0, unroll=8)
        for load in loads[5:]:
            load.wait()

        for n, (span, out) in enumerate(zip(spans, outs)):
            height = blocks * span[1]

            def one_owner(i, carry):
                at = pl.multiple_of(i * height, height)
                base = (n * edges + first + i) * square
                lay_tiles(table, base, tiles_ref, lhs, [span], 0, blocks, block, at)
                return carry

            lax.fori_loop(0, count, one_owner, 0)
            total = jnp.dot(lhs[pl.ds(0, count * height)], x_out[...], preferred_element_type=jnp.float32)
            if n == 1:
                out[pl.ds(0, count * height)] = total.astype(jnp.bfloat16)
                for i in range(extra):
                    line = jnp.full((1, width), choice[i].astype(jnp.float32), jnp.float32)
                    out[pl.ds(count * height + i, 1)] = line.astype(jnp.bfloat16)
            else:
                out[...] = total.astype(jnp.bfloat16).reshape(out.shape)

    return call(
        body,
        [
            jax.ShapeDtypeStruct((len(orders) * edges * square,), jnp.int32),
            jax.ShapeDtypeStruct((edges * READ_CAP,), jnp.int32),
            *[jax.ShapeDtypeStruct(shape, jnp.bfloat16) for shape in shapes],
            jax.ShapeDtypeStruct(features.shape, jnp.bfloat16),
        ],
        [SMEM] + [HBM] * 7,
        [SMEM] * 2 + [VMEM] * (len(spans) + 1),
        (me, slot, col, tile_id, touched.transpose(0, 2, 1), readers, tiles, features),
        [
            pltpu.SMEM((products,), jnp.int32),
            pltpu.SMEM((products,), jnp.int32),
            pltpu.SMEM((products,), jnp.int32),
            pltpu.SMEM((cap, edges), jnp.int32),
            pltpu.SMEM((listed,), jnp.int32),
            pltpu.SMEM((extra + 1,), jnp.int32),
            pltpu.VMEM((tiles.shape[0], loaded, block), jnp.bfloat16),
            pltpu.VMEM((count * blocks * tallest, blocks * block), jnp.bfloat16),
            pltpu.SMEM((len(orders) * edges * cap,), jnp.int32),
            pltpu.SMEM((edges,), jnp.int32),
            pltpu.SemaphoreType.DMA((7,)),
        ],
        limit=62 * 1024 * 1024,
    )


def other_parts(table, tiles, inputs, jobs):
    block = tiles.shape[1]
    blocks = inputs.shape[0] // block
    width = inputs.shape[1]
    most = max(sum(rows for _, rows in spans) for _, _, spans in jobs) * blocks
    shapes = [
        jax.ShapeDtypeStruct((count, blocks, rows, width), jnp.bfloat16) for _, count, spans in jobs for _, rows in spans
    ]

    def body(table_ref, tiles_hbm, x_ref, *refs):
        outs = refs
        token, tiles_ref, lhs, sems = outs[-4:]
        token[...] = jnp.zeros_like(token)
        load = pltpu.make_async_copy(tiles_hbm, tiles_ref, sems.at[0])
        load.start()
        load.wait()
        for first, count, spans in jobs:
            height = blocks * sum(rows for _, rows in spans)

            def one_owner(i, carry):
                lay_tiles(table_ref, (first + i) * blocks * blocks, tiles_ref, lhs, spans, 0, blocks, block)
                total = jnp.dot(lhs[pl.ds(0, height)], x_ref[...], preferred_element_type=jnp.float32)
                total = total.astype(jnp.bfloat16)
                at = 0
                for out, (_, rows) in zip(outs, spans):
                    out[i] = total[at : at + blocks * rows].reshape(blocks, rows, width)
                    at += blocks * rows
                return carry

            lax.fori_loop(0, count, one_owner, 0)
            outs = outs[len(spans) :]

    results = call(
        body,
        shapes + [TOKEN],
        [SMEM, HBM, VMEM],
        [VMEM] * (len(shapes) + 1),
        (table, tiles, inputs),
        [
            pltpu.VMEM(tiles.shape, jnp.bfloat16),
            pltpu.VMEM((most, blocks * block), jnp.bfloat16),
            pltpu.SemaphoreType.DMA((1,)),
        ],
    )
    grouped, at = [], 0
    for _, _, spans in jobs:
        grouped.append(results[at : at + len(spans)])
        at += len(spans)
    return (*grouped, results[-1])


def combine(token, total, got, at_hand):
    count, *shape = total.shape
    left = count // 2

    def body(token_ref, total_ref, got_ref, at_hand_ref, *outs):
        def add(i, carry):
            if got.ndim == total.ndim:
                value = got_ref[i]
            else:
                height = shape[0] * shape[1]
                value = got_ref[pl.ds(pl.multiple_of(i * height, height), height)].reshape(shape)
            value = total_ref[i].astype(jnp.float32) + value.astype(jnp.float32)
            if not left:
                outs[0][...] = value.astype(jnp.bfloat16)
            else:

                @pl.when(i < left)
                def _():
                    outs[0][jnp.minimum(i, left - 1)] = value

                @pl.when(i >= left)
                def _():
                    outs[1][jnp.maximum(i - left, 0)] = value.astype(jnp.bfloat16)

            return carry

        lax.fori_loop(0, count, add, 0)
        outs[-1][...] = token_ref[...]

    if left:
        out_shape = [
            jax.ShapeDtypeStruct((left, *shape), jnp.float32),
            jax.ShapeDtypeStruct((count - left, *shape), jnp.bfloat16),
        ]
    else:
        out_shape = [jax.ShapeDtypeStruct(tuple(shape), jnp.bfloat16)]
    out_shape.append(TOKEN)
    return call(body, out_shape, [VMEM] * 4, [VMEM] * len(out_shape), (token, total, got, at_hand))


def join(token, held, got):
    def body(token_ref, held_ref, got_ref, out, token_out):
        out[pl.ds(0, held.shape[0])] = held_ref[...]
        out[pl.ds(held.shape[0], got.shape[0])] = got_ref[...]
        token_out[...] = token_ref[...]

    both = jax.ShapeDtypeStruct((held.shape[0] + got.shape[0], *held.shape[1:]), held.dtype)
    return call(body, [both, TOKEN], [VMEM] * 3, [VMEM] * 2, (token, held, got))


def mix(token, offsets, held, got, weight):
    _, blocks, rows, depth = held.shape
    width = weight.shape[1]

    def body(token_ref, held_ref, got_ref, w_ref, out_ref, token_out):
        mine = lax.axis_index("feat")
        total = jnp.zeros((blocks * rows, width), jnp.float32)
        for n, offset in enumerate(offsets):
            piece = (held_ref if n < held.shape[0] else got_ref)[n % held.shape[0]]
            at = pl.multiple_of((mine ^ offset) * depth, depth)
            total += jnp.dot(
                piece.reshape(blocks * rows, depth), w_ref[pl.ds(at, depth)], preferred_element_type=jnp.float32
            )
        out_ref[0] = jnp.maximum(total, 0.0).astype(jnp.bfloat16).reshape(blocks, rows, width)
        token_out[...] = token_ref[...]

    return call(
        body,
        [jax.ShapeDtypeStruct((1, blocks, rows, width), jnp.bfloat16), TOKEN],
        [VMEM] * 4,
        [VMEM] * 2,
        (token, held, got, weight),
    )


def pick(token, wanted, held, got):
    count = 2 * held.shape[0] * READ_CAP
    extra = -(-count // 16) * 16
    _, blocks, rows, width = held.shape

    def body(token_ref, wanted_ref, held_ref, got_ref, out, token_out):
        lines = wanted_ref[pl.ds(wanted.shape[0] - extra, extra)].astype(jnp.float32)
        for i in range(count):
            n = i // READ_CAP
            source = held_ref if n < held.shape[0] else got_ref
            total = jnp.zeros((rows, width), jnp.bfloat16)
            for b in range(blocks):
                chosen = jnp.where(lines[i : i + 1] == b, 1.0, 0.0)
                chosen = jnp.broadcast_to(chosen, (rows, width)).astype(jnp.bfloat16)
                total += chosen * source[n % held.shape[0], b]
            out[i] = total
        token_out[...] = token_ref[...]

    return call(
        body,
        [jax.ShapeDtypeStruct((count, *held.shape[2:]), held.dtype), TOKEN],
        [VMEM] * 4,
        [VMEM] * 2,
        (token, wanted, held, got),
    )


def touch(token, value):
    def body(token_ref, value_ref, token_out):
        token_out[...] = token_ref[...]

    return call(body, [TOKEN], [VMEM] * 2, [VMEM], (token, value))


def lay_out(token, me, readers, entry, offsets, nears, fars, outputs, block):
    count = readers.shape[0]
    width = fars[0][0].shape[2]
    blocks = outputs[0].shape[0] if outputs else nears[0][0].shape[1]
    slots = len(offsets) * READ_CAP
    arrays = [array for held, got, _ in nears for array in (held, got)] + [far for far, _ in fars]

    def body(token_ref, me_ref, readers_ref, entry_ref, *refs):
        hidden_ref, ghost_ref, token_out, near_sems, far_sems = refs[-5:]
        near_refs, far_refs = refs[: 2 * len(nears)], refs[2 * len(nears) : len(arrays)]

        def each(act):
            for number, (held, _, span) in enumerate(nears):
                held_ref, got_ref = near_refs[2 * number : 2 * number + 2]
                part = pl.ds(*span)
                act(pltpu.make_async_copy(held_ref.at[0], hidden_ref.at[:, part], near_sems.at[number, slots]))
                for i in range(slots):
                    n, j = i // READ_CAP, i % READ_CAP
                    listed = entry_ref[(me_ref[0] ^ offsets[n]) * READ_CAP + j]
                    source = held_ref if n < held.shape[0] else got_ref
                    row = n % held.shape[0]

                    @pl.when(listed >= 0)
                    def _():
                        _, b = split(readers_ref[listed], blocks)
                        target = ghost_ref.at[listed, part]
                        act(pltpu.make_async_copy(source.at[row, b], target, near_sems.at[number, i]))

            for number, (_, span) in enumerate(fars):
                part = pl.ds(*span)
                for i in range(slots):
                    n, j = i // READ_CAP, i % READ_CAP
                    listed = entry_ref[(me_ref[0] ^ 1 ^ offsets[n]) * READ_CAP + j]

                    @pl.when(listed >= 0)
                    def _():
                        target = ghost_ref.at[listed, part]
                        act(pltpu.make_async_copy(far_refs[number].at[i], target, far_sems.at[number, i]))

        each(lambda copy: copy.start())
        token_out[...] = token_ref[...]
        each(lambda copy: copy.wait())

    operands = (token, me, readers, entry, *arrays, *outputs)
    return call(
        body,
        [
            jax.ShapeDtypeStruct((blocks, block, width), jnp.bfloat16),
            jax.ShapeDtypeStruct((count, block, width), jnp.bfloat16),
            TOKEN,
        ],
        [VMEM] + [SMEM] * 3 + [VMEM] * len(arrays) + [HBM] * len(outputs),
        [HBM, HBM, VMEM],
        operands,
        [
            pltpu.SemaphoreType.DMA((max(len(nears), 1), slots + 1)),
            pltpu.SemaphoreType.DMA((len(fars), slots)),
        ],
        aliases={len(operands) - 2: 0, len(operands) - 1: 1} if outputs else None,
    )


def local(features, tiles, tile_slot, tile_col, tile_id, touched, weight, readers):
    edges, feats = lax.axis_size("edge"), lax.axis_size("feat")
    half = edges // 2
    me = lax.axis_index("edge")
    block = tiles.shape[1]
    blocks = features.shape[0] // block
    width = features.shape[1]
    unit = block // sum(SHARES)
    spans = [(sum(SHARES[:i]) * unit, share * unit) for i, share in enumerate(SHARES)]

    def flip(value, bit, axis="edge"):
        return lax.ppermute(value, axis, [(d, d ^ bit) for d in range(lax.axis_size(axis))])

    columns = offsets_of(edges, 2)
    me = me.reshape(1)
    column_bits = [1 << i for i in range(1, edges.bit_length() - 1)]
    orders = [[*column_bits, 1], [1, *column_bits]]
    table, entry, *early, inputs = first_part(
        me, tile_slot, tile_col, tile_id, touched, tiles, features, readers, orders, half, half, spans[:2]
    )
    later, first_kept, _ = other_parts(
        table, tiles, inputs, [(edges + half, half, spans[2:]), (0, half, spans[:1])]
    )
    away = [*early, *later]
    kept, token = other_parts(table, tiles, inputs, [(edges, half, spans[1:])])
    kept = [*first_kept, *kept]

    def chained(function, *operands):
        nonlocal token
        *results, token = function(token, *operands)
        return results

    def spread(held, size, lowest, axis):
        bit = size // 2
        while True:
            got = flip(held, bit, axis)
            yield
            if bit == lowest:
                return held, got
            (held,) = chained(join, held, got)
            bit //= 2

    wanted, nears, fars = None, [], []
    ended = object()

    def one_part(part):
        nonlocal wanted
        first, *rest = orders[min(part, 1)]
        got = flip(away[part], first)
        yield
        total, sent = chained(combine, kept[part], got, weight)
        if part == 1:
            wanted = got
        for bit in rest:
            got = flip(sent, bit)
            yield
            total, *sent = chained(combine, total, got, weight)
            sent = sent[0] if sent else None
        held, got = yield from spread(total[None], feats, 1, "feat")
        (mixed,) = chained(mix, offsets_of(feats, 1), held, got, weight)
        held, got = yield from spread(mixed, edges, 2, "edge")
        (picked,) = chained(pick, wanted, held, got)
        nears.append((held, got, spans[part]))
        far = flip(picked, 1)
        yield
        fars.append((far, spans[part]))

    def links_of(bit):
        return {"x": 1.0} if bit == 1 else {"end": 1.0} if bit == 2 else {"end": 1.0, "middle": 2.0}

    feat_bits = [1 << i for i in reversed(range(feats.bit_length() - 1))]
    ways = []
    for part, (_, rows) in enumerate(spans):
        share = rows / block
        way = [(links_of(bit), share * half / (1 << n)) for n, bit in enumerate(orders[min(part, 1)])]
        way += [({"chip" if bit == 1 else "feat": 1.0}, share * (1.0 if bit > 1 else 0.3)) for bit in feat_bits]
        way += [(links_of(bit), share * half / bit) for bit in reversed(column_bits)]
        ways.append(way + [({"x": 1.0}, share * READ_CAP / blocks * half)])
    steps = [one_part(part) for part in range(len(spans))]
    for step in steps:
        next(step)
    known = sorted(ORDER) == [part for part, way in enumerate(ways) for _ in way]
    *order, last = ORDER if known else planned_order(ways)
    for part in order:
        if next(steps[part], ended) is ended:
            chained(touch, fars[-1][0])
    outputs = chained(lay_out, me, readers, entry, columns, nears, fars, (), block)
    next(steps[last], None)
    outputs = chained(lay_out, me, readers, entry, columns, [], fars[-1:], outputs, block)
    hidden, ghosts = outputs
    return hidden.reshape(blocks * block, width), ghosts.reshape(-1, width)


def solution(mesh):
    in_specs = (
        P("edge", "feat"),
        P("edge", None, None),
        P("edge"),
        P("edge"),
        P("edge"),
        P(),
        P(None, "feat"),
        P("edge"),
    )
    out_specs = (P("edge", "feat"), P("edge", "feat"))
    return jax.shard_map(local, mesh=mesh, in_specs=in_specs, out_specs=out_specs, check_vma=False)
```

```python
import jax
import jax.numpy as jnp
from jax import lax
from jax.experimental import pallas as pl
from jax.experimental.pallas import tpu as pltpu
from jax.sharding import PartitionSpec as P

SHARES = (2, 2, 2, 1, 1)
ORDER = (
    1, 0, 2, 4, 1, 0, 2, 3, 1, 0, 4, 2, 3, 1, 1, 4, 0, 4, 1, 2, 2, 3, 3, 0, 2, 1, 0, 4, 2, 4, 3, 1,
    0, 3, 4, 2, 3, 0, 4, 3,
)
READ_CAP = 2
VMEM_BYTES = 12 * 1024 * 1024
UNIT_TIME, START_TIME, STEP_TIME, LATENCY = 11.3, 0.9, 0.4, 0.6

SMEM = pl.BlockSpec(memory_space=pltpu.SMEM)
VMEM = pl.BlockSpec(memory_space=pltpu.VMEM)
HBM = pl.BlockSpec(memory_space=pltpu.HBM)
TOKEN = jax.ShapeDtypeStruct((8, 128), jnp.float32)


def call(body, out_shape, in_specs, out_specs, operands, scratch=(), aliases=None, limit=VMEM_BYTES):
    return pl.pallas_call(
        body,
        out_shape=out_shape,
        in_specs=in_specs,
        out_specs=out_specs,
        scratch_shapes=list(scratch),
        input_output_aliases=aliases or {},
        compiler_params=pltpu.CompilerParams(vmem_limit_bytes=limit),
        cost_estimate=pl.CostEstimate(flops=0, bytes_accessed=1, transcendentals=0),
    )(*operands)


def split(value, size):
    if size & (size - 1) == 0:
        return value >> (size.bit_length() - 1), value & (size - 1)
    return lax.div(value, size), lax.rem(value, size)


def place_of(peer, bits):
    place = 0
    for bit in bits:
        place = (place << 1) | ((peer >> (bit.bit_length() - 1)) & 1)
    return place


def planned_order(ways):
    now, order, flows, current, place = 0.0, [], [], {}, [0] * len(ways)

    def active():
        waiting = [f for f in flows if "x" in f["links"]][1:]
        running = [f for f in flows if not any(f is w for w in waiting)]
        load = {}
        for f in running:
            for link, weight in f["links"].items():
                load[link] = load.get(link, 0.0) + weight
        return [(f, min(1.0 / load[link] for link in f["links"])) for f in running]

    def advance(until):
        nonlocal now
        while now < until:
            running = active()
            step = min([until - now] + [f["left"] / rate for f, rate in running])
            now += max(step, 1e-3)
            for f, rate in running:
                f["left"] -= step * rate
                if f["left"] <= 1e-6:
                    f["end"] = now + LATENCY
            flows[:] = [f for f in flows if f["left"] > 1e-6]

    def begin(n):
        links, units = ways[n][place[n]]
        advance(now + START_TIME)
        current[n] = {"links": links, "left": units * UNIT_TIME, "end": None}
        flows.append(current[n])

    for n in range(len(ways)):
        begin(n)
    while current:
        ended = [(f["end"], n) for n, f in current.items() if f["end"] is not None and f["end"] <= now]
        if not ended:
            advance(now + 0.05)
            continue
        _, n = min(ended)
        order.append(n)
        del current[n]
        place[n] += 1
        advance(now + STEP_TIME)
        if place[n] < len(ways[n]):
            begin(n)
    return order


def offsets_of(size, lowest):
    offsets, bit = [0], size // 2
    while bit >= lowest:
        offsets += [offset | bit for offset in offsets]
        bit //= 2
    return offsets


def lay_tiles(table, base, tiles, lhs, spans, row_base, blocks, block, at=0):
    for b in range(blocks):
        for c in range(blocks):
            entry = table[base + b * blocks + c]
            tile = tiles[jnp.maximum(entry - 1, 0)]
            tile = jnp.where(entry > 0, tile, jnp.zeros_like(tile))
            top = at
            for first, rows in spans:
                lhs[pl.ds(top + b * rows, rows), pl.ds(c * block, block)] = tile[first - row_base : first - row_base + rows]
                top = top + blocks * rows


def first_part(me, slot, col, tile_id, touched, tiles, features, readers, orders, first, count, spans):
    block = tiles.shape[1]
    blocks = features.shape[0] // block
    width = features.shape[1]
    edges, cap = touched.shape[1], touched.shape[2]
    column_bits = [1 << i for i in range(1, edges.bit_length() - 1)]
    products = slot.shape[0]
    half = edges // 2
    loaded = sum(rows for _, rows in spans)
    tallest = max(rows for _, rows in spans)
    square = blocks * blocks

    listed = readers.shape[0]
    extra = -(-half * READ_CAP // 16) * 16
    shapes = [(count, blocks, rows, width) for _, rows in spans]
    shapes[1] = (count * blocks * spans[1][1] + extra, width)

    def body(me_ref, slot_hbm, col_hbm, id_hbm, touched_hbm, readers_hbm, tiles_hbm, x_hbm, *refs):
        table, entry, *outs = refs[: 2 + len(spans)]
        x_out, *scratch = refs[2 + len(spans) :]
        slot_ref, col_ref, id_ref, touched_ref, readers_ref, choice, tiles_ref, lhs, bases, seen, sems = scratch
        loads = [
            pltpu.make_async_copy(slot_hbm, slot_ref, sems.at[0]),
            pltpu.make_async_copy(col_hbm, col_ref, sems.at[1]),
            pltpu.make_async_copy(id_hbm, id_ref, sems.at[2]),
            pltpu.make_async_copy(touched_hbm.at[me_ref[0]], touched_ref, sems.at[5]),
            pltpu.make_async_copy(readers_hbm, readers_ref, sems.at[6]),
            pltpu.make_async_copy(x_hbm, x_out, sems.at[3]),
            pltpu.make_async_copy(tiles_hbm.at[:, pl.ds(0, loaded)], tiles_ref, sems.at[4]),
        ]
        for load in loads:
            load.start()

        def clear(i, carry):
            table[i] = 0
            return carry

        lax.fori_loop(0, len(orders) * edges * square, clear, 0, unroll=16)

        def place_slot(k, carry):
            owner, slot_at = split(k, cap)
            for n, order in enumerate(orders):
                place = place_of(owner ^ me_ref[0], order)
                bases[n * edges * cap + k] = ((n * edges + place) * blocks + touched_ref[slot_at, owner]) * blocks
            return carry

        for load in loads[:5]:
            load.wait()
        lax.fori_loop(0, edges * cap, place_slot, 0, unroll=8)

        for i in range(extra + 1):
            choice[i] = 0
        for i in range(edges * READ_CAP):
            entry[i] = -1
        for i in range(edges):
            seen[i] = 0

        def enter_lists(r, carry):
            owner, b = split(readers_ref[r], blocks)
            turn = seen[owner]
            seen[owner] = turn + 1
            turn = jnp.minimum(turn, READ_CAP - 1)
            entry[owner * READ_CAP + turn] = r
            peer = owner ^ me_ref[0] ^ 1
            row = place_of(peer, column_bits) * READ_CAP + turn
            choice[jnp.where(peer & 1 == 0, row, extra)] = b
            return carry

        lax.fori_loop(0, listed, enter_lists, 0)

        def enter(k, carry):
            for n in range(len(orders)):
                table[bases[n * edges * cap + slot_ref[k]] + col_ref[k]] = id_ref[k] + 1
            return carry

        lax.fori_loop(0, products, enter, 0, unroll=8)
        for load in loads[5:]:
            load.wait()

        for n, (span, out) in enumerate(zip(spans, outs)):
            height = blocks * span[1]

            def one_owner(i, carry):
                at = pl.multiple_of(i * height, height)
                base = (n * edges + first + i) * square
                lay_tiles(table, base, tiles_ref, lhs, [span], 0, blocks, block, at)
                return carry

            lax.fori_loop(0, count, one_owner, 0)
            total = jnp.dot(lhs[pl.ds(0, count * height)], x_out[...], preferred_element_type=jnp.float32)
            if n == 1:
                out[pl.ds(0, count * height)] = total.astype(jnp.bfloat16)
                for i in range(extra):
                    line = jnp.full((1, width), choice[i].astype(jnp.float32), jnp.float32)
                    out[pl.ds(count * height + i, 1)] = line.astype(jnp.bfloat16)
            else:
                out[...] = total.astype(jnp.bfloat16).reshape(out.shape)

    return call(
        body,
        [
            jax.ShapeDtypeStruct((len(orders) * edges * square,), jnp.int32),
            jax.ShapeDtypeStruct((edges * READ_CAP,), jnp.int32),
            *[jax.ShapeDtypeStruct(shape, jnp.bfloat16) for shape in shapes],
            jax.ShapeDtypeStruct(features.shape, jnp.bfloat16),
        ],
        [SMEM] + [HBM] * 7,
        [SMEM] * 2 + [VMEM] * (len(spans) + 1),
        (me, slot, col, tile_id, touched.transpose(0, 2, 1), readers, tiles, features),
        [
            pltpu.SMEM((products,), jnp.int32),
            pltpu.SMEM((products,), jnp.int32),
            pltpu.SMEM((products,), jnp.int32),
            pltpu.SMEM((cap, edges), jnp.int32),
            pltpu.SMEM((listed,), jnp.int32),
            pltpu.SMEM((extra + 1,), jnp.int32),
            pltpu.VMEM((tiles.shape[0], loaded, block), jnp.bfloat16),
            pltpu.VMEM((count * blocks * tallest, blocks * block), jnp.bfloat16),
            pltpu.SMEM((len(orders) * edges * cap,), jnp.int32),
            pltpu.SMEM((edges,), jnp.int32),
            pltpu.SemaphoreType.DMA((7,)),
        ],
        limit=62 * 1024 * 1024,
    )


def other_parts(table, tiles, inputs, jobs):
    block = tiles.shape[1]
    blocks = inputs.shape[0] // block
    width = inputs.shape[1]
    most = max(sum(rows for _, rows in spans) for _, _, spans in jobs) * blocks
    shapes = [
        jax.ShapeDtypeStruct((count, blocks, rows, width), jnp.bfloat16) for _, count, spans in jobs for _, rows in spans
    ]

    def body(table_ref, tiles_hbm, x_ref, *refs):
        outs = refs
        token, tiles_ref, lhs, sems = outs[-4:]
        token[...] = jnp.zeros_like(token)
        load = pltpu.make_async_copy(tiles_hbm, tiles_ref, sems.at[0])
        load.start()
        load.wait()
        for first, count, spans in jobs:
            height = blocks * sum(rows for _, rows in spans)

            def one_owner(i, carry):
                lay_tiles(table_ref, (first + i) * blocks * blocks, tiles_ref, lhs, spans, 0, blocks, block)
                total = jnp.dot(lhs[pl.ds(0, height)], x_ref[...], preferred_element_type=jnp.float32)
                total = total.astype(jnp.bfloat16)
                at = 0
                for out, (_, rows) in zip(outs, spans):
                    out[i] = total[at : at + blocks * rows].reshape(blocks, rows, width)
                    at += blocks * rows
                return carry

            lax.fori_loop(0, count, one_owner, 0)
            outs = outs[len(spans) :]

    results = call(
        body,
        shapes + [TOKEN],
        [SMEM, HBM, VMEM],
        [VMEM] * (len(shapes) + 1),
        (table, tiles, inputs),
        [
            pltpu.VMEM(tiles.shape, jnp.bfloat16),
            pltpu.VMEM((most, blocks * block), jnp.bfloat16),
            pltpu.SemaphoreType.DMA((1,)),
        ],
    )
    grouped, at = [], 0
    for _, _, spans in jobs:
        grouped.append(results[at : at + len(spans)])
        at += len(spans)
    return (*grouped, results[-1])


def combine(token, total, got, at_hand):
    count, *shape = total.shape
    left = count // 2

    def body(token_ref, total_ref, got_ref, at_hand_ref, *outs):
        def add(i, carry):
            if got.ndim == total.ndim:
                value = got_ref[i]
            else:
                height = shape[0] * shape[1]
                value = got_ref[pl.ds(pl.multiple_of(i * height, height), height)].reshape(shape)
            value = total_ref[i].astype(jnp.float32) + value.astype(jnp.float32)
            if not left:
                outs[0][...] = value.astype(jnp.bfloat16)
            else:

                @pl.when(i < left)
                def _():
                    outs[0][jnp.minimum(i, left - 1)] = value

                @pl.when(i >= left)
                def _():
                    outs[1][jnp.maximum(i - left, 0)] = value.astype(jnp.bfloat16)

            return carry

        lax.fori_loop(0, count, add, 0)
        outs[-1][...] = token_ref[...]

    if left:
        out_shape = [
            jax.ShapeDtypeStruct((left, *shape), jnp.float32),
            jax.ShapeDtypeStruct((count - left, *shape), jnp.bfloat16),
        ]
    else:
        out_shape = [jax.ShapeDtypeStruct(tuple(shape), jnp.bfloat16)]
    out_shape.append(TOKEN)
    return call(body, out_shape, [VMEM] * 4, [VMEM] * len(out_shape), (token, total, got, at_hand))


def join(token, held, got):
    def body(token_ref, held_ref, got_ref, out, token_out):
        out[pl.ds(0, held.shape[0])] = held_ref[...]
        out[pl.ds(held.shape[0], got.shape[0])] = got_ref[...]
        token_out[...] = token_ref[...]

    both = jax.ShapeDtypeStruct((held.shape[0] + got.shape[0], *held.shape[1:]), held.dtype)
    return call(body, [both, TOKEN], [VMEM] * 3, [VMEM] * 2, (token, held, got))


def mix(token, offsets, held, got, weight):
    _, blocks, rows, depth = held.shape
    width = weight.shape[1]

    def body(token_ref, held_ref, got_ref, w_ref, out_ref, token_out):
        mine = lax.axis_index("feat")
        total = jnp.zeros((blocks * rows, width), jnp.float32)
        for n, offset in enumerate(offsets):
            piece = (held_ref if n < held.shape[0] else got_ref)[n % held.shape[0]]
            at = pl.multiple_of((mine ^ offset) * depth, depth)
            total += jnp.dot(
                piece.reshape(blocks * rows, depth), w_ref[pl.ds(at, depth)], preferred_element_type=jnp.float32
            )
        out_ref[0] = jnp.maximum(total, 0.0).astype(jnp.bfloat16).reshape(blocks, rows, width)
        token_out[...] = token_ref[...]

    return call(
        body,
        [jax.ShapeDtypeStruct((1, blocks, rows, width), jnp.bfloat16), TOKEN],
        [VMEM] * 4,
        [VMEM] * 2,
        (token, held, got, weight),
    )


def pick(token, wanted, held, got):
    count = 2 * held.shape[0] * READ_CAP
    extra = -(-count // 16) * 16
    _, blocks, rows, width = held.shape

    def body(token_ref, wanted_ref, held_ref, got_ref, out, token_out):
        lines = wanted_ref[pl.ds(wanted.shape[0] - extra, extra)].astype(jnp.float32)
        for i in range(count):
            n = i // READ_CAP
            source = held_ref if n < held.shape[0] else got_ref
            total = jnp.zeros((rows, width), jnp.bfloat16)
            for b in range(blocks):
                chosen = jnp.where(lines[i : i + 1] == b, 1.0, 0.0)
                chosen = jnp.broadcast_to(chosen, (rows, width)).astype(jnp.bfloat16)
                total += chosen * source[n % held.shape[0], b]
            out[i] = total
        token_out[...] = token_ref[...]

    return call(
        body,
        [jax.ShapeDtypeStruct((count, *held.shape[2:]), held.dtype), TOKEN],
        [VMEM] * 4,
        [VMEM] * 2,
        (token, wanted, held, got),
    )


def touch(token, value):
    def body(token_ref, value_ref, token_out):
        token_out[...] = token_ref[...]

    return call(body, [TOKEN], [VMEM] * 2, [VMEM], (token, value))


def lay_out(token, me, readers, entry, offsets, nears, fars, outputs, block):
    count = readers.shape[0]
    width = fars[0][0].shape[2]
    blocks = outputs[0].shape[0] if outputs else nears[0][0].shape[1]
    slots = len(offsets) * READ_CAP
    arrays = [array for held, got, _ in nears for array in (held, got)] + [far for far, _ in fars]

    def body(token_ref, me_ref, readers_ref, entry_ref, *refs):
        hidden_ref, ghost_ref, token_out, near_sems, far_sems = refs[-5:]
        near_refs, far_refs = refs[: 2 * len(nears)], refs[2 * len(nears) : len(arrays)]

        def each(act):
            for number, (held, _, span) in enumerate(nears):
                held_ref, got_ref = near_refs[2 * number : 2 * number + 2]
                part = pl.ds(*span)
                act(pltpu.make_async_copy(held_ref.at[0], hidden_ref.at[:, part], near_sems.at[number, slots]))
                for i in range(slots):
                    n, j = i // READ_CAP, i % READ_CAP
                    listed = entry_ref[(me_ref[0] ^ offsets[n]) * READ_CAP + j]
                    source = held_ref if n < held.shape[0] else got_ref
                    row = n % held.shape[0]

                    @pl.when(listed >= 0)
                    def _():
                        _, b = split(readers_ref[listed], blocks)
                        target = ghost_ref.at[listed, part]
                        act(pltpu.make_async_copy(source.at[row, b], target, near_sems.at[number, i]))

            for number, (_, span) in enumerate(fars):
                part = pl.ds(*span)
                for i in range(slots):
                    n, j = i // READ_CAP, i % READ_CAP
                    listed = entry_ref[(me_ref[0] ^ 1 ^ offsets[n]) * READ_CAP + j]

                    @pl.when(listed >= 0)
                    def _():
                        target = ghost_ref.at[listed, part]
                        act(pltpu.make_async_copy(far_refs[number].at[i], target, far_sems.at[number, i]))

        each(lambda copy: copy.start())
        token_out[...] = token_ref[...]
        each(lambda copy: copy.wait())

    operands = (token, me, readers, entry, *arrays, *outputs)
    return call(
        body,
        [
            jax.ShapeDtypeStruct((blocks, block, width), jnp.bfloat16),
            jax.ShapeDtypeStruct((count, block, width), jnp.bfloat16),
            TOKEN,
        ],
        [VMEM] + [SMEM] * 3 + [VMEM] * len(arrays) + [HBM] * len(outputs),
        [HBM, HBM, VMEM],
        operands,
        [
            pltpu.SemaphoreType.DMA((max(len(nears), 1), slots + 1)),
            pltpu.SemaphoreType.DMA((len(fars), slots)),
        ],
        aliases={len(operands) - 2: 0, len(operands) - 1: 1} if outputs else None,
    )


def local(features, tiles, tile_slot, tile_col, tile_id, touched, weight, readers):
    edges, feats = lax.axis_size("edge"), lax.axis_size("feat")
    half = edges // 2
    me = lax.axis_index("edge")
    block = tiles.shape[1]
    blocks = features.shape[0] // block
    width = features.shape[1]
    unit = block // sum(SHARES)
    spans = [(sum(SHARES[:i]) * unit, share * unit) for i, share in enumerate(SHARES)]

    def flip(value, bit, axis="edge"):
        return lax.ppermute(value, axis, [(d, d ^ bit) for d in range(lax.axis_size(axis))])

    columns = offsets_of(edges, 2)
    me = me.reshape(1)
    column_bits = [1 << i for i in range(1, edges.bit_length() - 1)]
    orders = [[*column_bits, 1], [1, *column_bits]]
    table, entry, *early, inputs = first_part(
        me, tile_slot, tile_col, tile_id, touched, tiles, features, readers, orders, half, half, spans[:2]
    )
    later, first_kept, _ = other_parts(
        table, tiles, inputs, [(edges + half, half, spans[2:]), (0, half, spans[:1])]
    )
    away = [*early, *later]
    kept, token = other_parts(table, tiles, inputs, [(edges, half, spans[1:])])
    kept = [*first_kept, *kept]

    def chained(function, *operands):
        nonlocal token
        *results, token = function(token, *operands)
        return results

    def spread(held, size, lowest, axis):
        bit = size // 2
        while True:
            got = flip(held, bit, axis)
            yield
            if bit == lowest:
                return held, got
            (held,) = chained(join, held, got)
            bit //= 2

    wanted, nears, fars = None, [], []
    ended = object()

    def one_part(part):
        nonlocal wanted
        first, *rest = orders[min(part, 1)]
        got = flip(away[part], first)
        yield
        total, sent = chained(combine, kept[part], got, weight)
        if part == 1:
            wanted = got
        for bit in rest:
            got = flip(sent, bit)
            yield
            total, *sent = chained(combine, total, got, weight)
            sent = sent[0] if sent else None
        held, got = yield from spread(total[None], feats, 1, "feat")
        (mixed,) = chained(mix, offsets_of(feats, 1), held, got, weight)
        held, got = yield from spread(mixed, edges, 2, "edge")
        (picked,) = chained(pick, wanted, held, got)
        nears.append((held, got, spans[part]))
        far = flip(picked, 1)
        yield
        fars.append((far, spans[part]))

    def links_of(bit):
        return {"x": 1.0} if bit == 1 else {"end": 1.0} if bit == 2 else {"end": 1.0, "middle": 2.0}

    feat_bits = [1 << i for i in reversed(range(feats.bit_length() - 1))]
    ways = []
    for part, (_, rows) in enumerate(spans):
        share = rows / block
        way = [(links_of(bit), share * half / (1 << n)) for n, bit in enumerate(orders[min(part, 1)])]
        way += [({"chip" if bit == 1 else "feat": 1.0}, share * (1.0 if bit > 1 else 0.3)) for bit in feat_bits]
        way += [(links_of(bit), share * half / bit) for bit in reversed(column_bits)]
        ways.append(way + [({"x": 1.0}, share * READ_CAP / blocks * half)])
    steps = [one_part(part) for part in range(len(spans))]
    for step in steps:
        next(step)
    known = sorted(ORDER) == [part for part, way in enumerate(ways) for _ in way]
    *order, last = ORDER if known else planned_order(ways)
    for part in order:
        if next(steps[part], ended) is ended:
            chained(touch, fars[-1][0])
    outputs = chained(lay_out, me, readers, entry, columns, nears, fars, (), block)
    next(steps[last], None)
    outputs = chained(lay_out, me, readers, entry, columns, [], fars[-1:], outputs, block)
    hidden, ghosts = outputs
    return hidden.reshape(blocks * block, width), ghosts.reshape(-1, width)


def solution(mesh):
    in_specs = (
        P("edge", "feat"),
        P("edge", None, None),
        P("edge"),
        P("edge"),
        P("edge"),
        P(),
        P(None, "feat"),
        P("edge"),
    )
    out_specs = (P("edge", "feat"), P("edge", "feat"))
    return jax.shard_map(local, mesh=mesh, in_specs=in_specs, out_specs=out_specs, check_vma=False)
```
